32 devices in a mesh: dp: 8 (over z, x), mp: 4 (over y, core).
Axes of the slice: x: 2, y: 2, z: 4, core: 2. Of those that a mesh axis runs over, the one named last changes fastest.
Arguments:
- text_in: bfloat16 [8704, 768], P(('dp', 'mp')), may hold values from -6 to 6
- segment_ids: int32 [136, 64], P('dp'), may hold values from 0 to 3, never falling along the last dimension, each value on 1 to 40 neighbouring positions
- valid_lengths: int32 [136], P('dp'), may hold values from 40 to 64
- text_grad: bfloat16 [8704, 768], P(('dp', 'mp')), may hold values from -6 to 6
- attn_gain: bfloat16 [768], replicated, may hold values from 0.5 to 1.5
- attn_shift: bfloat16 [768], replicated, may hold values from -3 to 3
- qkv_weight: bfloat16 [768, 3, 768], P(None, None, 'mp'), may hold values from -0.21875 to 0.21875
- qv_bias: bfloat16 [2, 768], P(None, 'mp'), may hold values from -3 to 3
- out_weight: bfloat16 [768, 768], P('mp'), may hold values from -0.875 to 0.875
- out_bias: bfloat16 [768], replicated, may hold values from -3 to 3
- mlp_gain: bfloat16 [768], replicated, may hold values from 0.5 to 1.5
- mlp_shift: bfloat16 [768], replicated, may hold values from -3 to 3
- fc1_weight: bfloat16 [768, 3072], P(None, 'mp'), may hold values from -0.21875 to 0.21875
- fc1_bias: bfloat16 [3072], P('mp'), may hold values from -3 to 3
- fc2_weight: bfloat16 [3072, 768], P('mp'), may hold values from -0.21875 to 0.21875
- fc2_bias: bfloat16 [768], replicated, may hold values from -3 to 3
- images: bfloat16 [12800, 768], P(('dp', 'mp')), may hold values from -6 to 6
- img_attn_gain: bfloat16 [768], replicated, may hold values from 0.5 to 1.5
- img_attn_shift: bfloat16 [768], replicated, may hold values from -3 to 3
- img_qkv_weight: bfloat16 [768, 3, 768], P(None, None, 'mp'), may hold values from -0.21875 to 0.21875
- img_qv_bias: bfloat16 [2, 768], P(None, 'mp'), may hold values from -3 to 3
- img_out_weight: bfloat16 [768, 768], P('mp'), may hold values from -1.25 to 1.25
- img_out_bias: bfloat16 [768], replicated, may hold values from -3 to 3
- img_mlp_gain: bfloat16 [768], replicated, may hold values from 0.5 to 1.5
- img_mlp_shift: bfloat16 [768], replicated, may hold values from -3 to 3
- img_fc1_weight: bfloat16 [768, 3072], P(None, 'mp'), may hold values from -0.21875 to 0.21875
- img_fc1_bias: bfloat16 [3072], P('mp'), may hold values from -3 to 3
- img_fc2_weight: bfloat16 [3072, 768], P('mp'), may hold values from -0.21875 to 0.21875
- img_fc2_bias: bfloat16 [768], replicated, may hold values from -3 to 3
Outputs:
- text_out: bfloat16 [8704, 768], P(('dp', 'mp'))
- image_out: bfloat16 [12800, 768], P(('dp', 'mp'))
- text_in_grad: bfloat16 [8704, 768], P(('dp', 'mp'))
- grad_attn_gain: float32 [768], replicated
- grad_attn_shift: float32 [768], replicated
- grad_qkv_weight: float32 [768, 3, 768], P(None, None, 'mp')
- grad_qv_bias: float32 [2, 768], P(None, 'mp')
- grad_out_weight: float32 [768, 768], P('mp')
- grad_out_bias: float32 [768], replicated
- grad_mlp_gain: float32 [768], replicated
- grad_mlp_shift: float32 [768], replicated
- grad_fc1_weight: float32 [768, 3072], P(None, 'mp')
- grad_fc1_bias: float32 [3072], P('mp')
- grad_fc2_weight: float32 [3072, 768], P('mp')
- grad_fc2_bias: float32 [768], replicated
The draws below stay inside these ranges and needn't reach their ends.
Inputs may be any that keep to these rules, and one draw needn't show every extreme that they name: `segment_ids`: along each row the number never falls. `valid_lengths`: positions at or past it in a row are padding.
All inputs are finite; a program needn't handle non-finite values.
Results may differ from the reference program's by a relative error of at most 0.015.
Values may be sent and summed in bfloat16 or wider, within the bound.
No kernel may reach another device: no remote copies, remote signals or barrier semaphores. Data moves between devices by JAX's collectives and lax.ppermute only.
A program may use at most 128 MiB of HBM per device.

```python
import math
import jax
import jax.numpy as jnp
import numpy as np
from jax import lax

D = 768
HEADS = 12
HEAD = 64
FF = 3072
SEQ = 64
IMG_SEQ = 50
ROWS_DEV = 17
IMG_DEV = 32
ROWS = 136
TXT_TOK = 8704
IMG_TOK = 12800
N_DP = 8


def plant(array, stream_key, smallest, high):
    longest = array.shape.index(max(array.shape))
    spots = []
    for shift in (0, 1):
        where = [jax.random.randint(jax.random.fold_in(stream_key, axis), (), 0, length) for axis, length in enumerate(array.shape)]
        where[longest] = (where[longest] + shift) % array.shape[longest]
        spots.append(tuple(where))
    return array.at[spots[0]].set(smallest).at[spots[1]].set(high)


def block_levels(key, dims, cuts, low, largest):
    level = 1.0
    for dim, blocks in cuts:
        steps = jax.random.uniform(jax.random.fold_in(jax.random.fold_in(key, 6), dim), (blocks,), jnp.float32, low / len(cuts), largest / len(cuts))
        level = level * jnp.repeat(jnp.exp(steps), dims[dim] // blocks).reshape((-1,) + (1,) * (len(dims) - 1 - dim))
    return level


def length_profile(count, total, bound, slope):
    weights = [(1 << 20) // math.isqrt(standing ** slope) + 1 for standing in range(2, count + 1)]
    spare, counts = total - bound - (count - 1), [1] * (count - 1)
    while spare > 0:
        movable = [i for i in range(count - 1) if counts[i] < bound]
        whole, remaining = sum([weights[i] for i in movable]), spare
        for i in movable:
            more = min(bound - counts[i], max(1, remaining * weights[i] // whole), spare)
            counts[i] = counts[i] + more
            spare = spare - more
    return np.array([bound] + counts)


def uneven(stream_key, number_of, total, bound, slope):
    if number_of == 2:
        one = jax.random.randint(stream_key, (), max(1, total - bound), min(bound, total - 1) + 1)
        return jnp.stack([one, total - one])
    tallies = jnp.asarray(length_profile(number_of, total, bound, slope), jnp.int32)
    pairs = (number_of - 1) // 2
    donor, taker = tallies[1:1 + 2 * pairs:2], tallies[2:2 + 2 * pairs:2]
    margin = jnp.minimum(donor - 1, bound - taker)
    passed = jax.random.randint(jax.random.fold_in(stream_key, 1), (pairs,), 0, 1 << 20) % (margin + 1)
    tallies = tallies.at[1:1 + 2 * pairs:2].set(donor - passed).at[2:2 + 2 * pairs:2].set(taker + passed)
    return tallies[jax.random.permutation(jax.random.fold_in(stream_key, 2), number_of)]


def gaussian(stream_key, dims, scale, most, cuts=(), held_as=jnp.bfloat16):
    loudness = block_levels(stream_key, dims, cuts, -0.22, 0.18) if cuts else 1.0
    entries = jax.random.normal(stream_key, dims, jnp.float32) * scale * loudness
    return jnp.minimum(jnp.maximum(entries, -most), most).astype(held_as)


def setup_inputs(seed: int = 0) -> dict:
    splits = jax.random.split(jax.random.key(seed), 30)
    text_in = gaussian(splits[0], (TXT_TOK, D), 1.0, 6.0, ((0, 32),))
    segment_ids = jax.vmap(lambda own: jnp.searchsorted(jnp.cumsum(uneven(own, 4, SEQ, 40, 2)), jnp.arange(SEQ), side="right"))(jax.random.split(splits[1], ROWS)).reshape((ROWS, SEQ)).astype(jnp.int32)
    valid_lengths = plant(jax.random.randint(splits[2], (ROWS,), 40, SEQ + 1), jax.random.fold_in(splits[2], 1), 40, SEQ).astype(jnp.int32)
    text_grad = gaussian(splits[3], (TXT_TOK, D), 1.0, 6.0, ((0, 32),))
    attn_gain = jnp.clip(1.0 + 0.1 * jax.random.normal(splits[4], (D,), jnp.float32), 0.5, 1.5).astype(jnp.bfloat16)
    attn_shift = gaussian(splits[5], (D,), 0.5, 3.0)
    qkv_weight = gaussian(splits[6], (D, 3, D), D ** -0.5, 0.21875, ((2, 4),))
    qv_bias = gaussian(splits[7], (2, D), 0.5, 3.0, ((1, 4),))
    out_weight = gaussian(splits[8], (D, D), (D // 16) ** -0.5, 0.875, ((0, 4),))
    out_bias = gaussian(splits[9], (D,), 0.5, 3.0)
    mlp_gain = jnp.clip(1.0 + 0.1 * jax.random.normal(splits[10], (D,), jnp.float32), 0.5, 1.5).astype(jnp.bfloat16)
    mlp_shift = gaussian(splits[11], (D,), 0.5, 3.0)
    fc1_weight = gaussian(splits[12], (D, FF), D ** -0.5, 0.21875, ((1, 4),))
    fc1_bias = gaussian(splits[13], (FF,), 0.5, 3.0, ((0, 4),))
    fc2_weight = gaussian(splits[14], (FF, D), (FF // 4) ** -0.5, 0.21875, ((0, 4),))
    fc2_bias = gaussian(splits[15], (D,), 0.5, 3.0)
    images = gaussian(splits[16], (IMG_TOK, D), 1.0, 6.0, ((0, 32),))
    img_attn_gain = jnp.clip(1.0 + 0.1 * jax.random.normal(splits[17], (D,), jnp.float32), 0.5, 1.5).astype(jnp.bfloat16)
    img_attn_shift = gaussian(splits[18], (D,), 0.5, 3.0)
    img_qkv_weight = gaussian(splits[19], (D, 3, D), D ** -0.5, 0.21875, ((2, 4),))
    img_qv_bias = gaussian(splits[20], (2, D), 0.5, 3.0, ((1, 4),))
    img_out_weight = gaussian(splits[21], (D, D), (D // 32) ** -0.5, 1.25, ((0, 4),))
    img_out_bias = gaussian(splits[22], (D,), 0.5, 3.0)
    img_mlp_gain = jnp.clip(1.0 + 0.1 * jax.random.normal(splits[23], (D,), jnp.float32), 0.5, 1.5).astype(jnp.bfloat16)
    img_mlp_shift = gaussian(splits[24], (D,), 0.5, 3.0)
    img_fc1_weight = gaussian(splits[25], (D, FF), D ** -0.5, 0.21875, ((1, 4),))
    img_fc1_bias = gaussian(splits[26], (FF,), 0.5, 3.0, ((0, 4),))
    img_fc2_weight = gaussian(splits[27], (FF, D), (FF // 4) ** -0.5, 0.21875, ((0, 4),))
    img_fc2_bias = gaussian(splits[28], (D,), 0.5, 3.0)
    return dict(text_in=text_in, segment_ids=segment_ids, valid_lengths=valid_lengths, text_grad=text_grad, attn_gain=attn_gain, attn_shift=attn_shift, qkv_weight=qkv_weight, qv_bias=qv_bias, out_weight=out_weight, out_bias=out_bias, mlp_gain=mlp_gain, mlp_shift=mlp_shift, fc1_weight=fc1_weight, fc1_bias=fc1_bias, fc2_weight=fc2_weight, fc2_bias=fc2_bias, images=images, img_attn_gain=img_attn_gain, img_attn_shift=img_attn_shift, img_qkv_weight=img_qkv_weight, img_qv_bias=img_qv_bias, img_out_weight=img_out_weight, img_out_bias=img_out_bias, img_mlp_gain=img_mlp_gain, img_mlp_shift=img_mlp_shift, img_fc1_weight=img_fc1_weight, img_fc1_bias=img_fc1_bias, img_fc2_weight=img_fc2_weight, img_fc2_bias=img_fc2_bias)


@jax.custom_vjp
def low(v):
    return lax.optimization_barrier(v.astype(jnp.bfloat16)).astype(jnp.float32)

@jax.custom_vjp
def low_back(v):
    return v

def low_keep(v):
    return (low(v), None)

def low_pass(kept, grad):
    return (grad,)

def back_keep(v):
    return (v, None)

def back_low(kept, grad):
    return (low(grad),)
low.defvjp(low_keep, low_pass)
low_back.defvjp(back_keep, back_low)
epsilon = 1e-05
highest = lax.Precision.HIGHEST

def layer_norm(stream, gain, shift):
    centred = stream - lax.optimization_barrier(jnp.mean(stream, axis=-1, keepdims=True))
    inverse = lax.rsqrt(lax.optimization_barrier(jnp.mean(centred * centred, axis=-1, keepdims=True)) + epsilon)
    return centred * inverse * gain + shift

def product(left, right):
    return jnp.dot(left, right, precision=highest, preferred_element_type=jnp.float32)

def block(params, stream, allowed, rows, length):
    attn_gain, attn_shift, qkv_weight, qv_bias, out_weight, out_bias, mlp_gain, mlp_shift, fc1_weight, fc1_bias, fc2_weight, fc2_bias = params
    attn_rows = low(layer_norm(stream, attn_gain, attn_shift))
    projected = product(attn_rows, qkv_weight.reshape(D, 3 * D))
    query_rows = low(low_back(projected[:, :D] + qv_bias[0]))
    key_rows = low(low_back(projected[:, D:2 * D]))
    value_rows = low(low_back(projected[:, 2 * D:] + qv_bias[1]))
    split = (rows, length, HEADS, HEAD)
    raw = jnp.einsum('rthe,rshe->rhts', query_rows.reshape(split), key_rows.reshape(split), precision=highest)
    scores = jnp.where(allowed[:, None] > 0, low_back(raw * HEAD ** (-0.5)), -1000000000.0)
    peak = lax.optimization_barrier(jnp.max(scores, axis=-1, keepdims=True))
    weights = jnp.exp(scores - peak)
    probs = low(weights / lax.optimization_barrier(jnp.sum(weights, axis=-1, keepdims=True)))
    context = jnp.einsum('rhts,rshe->rthe', probs, value_rows.reshape(split), precision=highest)
    context = low(low_back(context.reshape(rows * length, D)))
    after_attn = stream + low_back(product(context, out_weight) + out_bias)
    mlp_rows = low(layer_norm(after_attn, mlp_gain, mlp_shift))
    hidden = low_back(product(mlp_rows, fc1_weight) + fc1_bias)
    active = low(jax.nn.gelu(hidden))
    return after_attn + low_back(product(active, fc2_weight) + fc2_bias)

def allowed_rows(segment_ids, valid_lengths):
    positions = jnp.arange(SEQ, dtype=jnp.int32)
    same = segment_ids[:, :, None] == segment_ids[:, None, :]
    live = positions[None, None, :] < valid_lengths[:, None, None]
    diagonal = (positions[:, None] == positions[None, :])[None]
    return (same & (live | diagonal)).astype(jnp.int32)

def reference(text_in, segment_ids, valid_lengths, text_grad, attn_gain, attn_shift, qkv_weight, qv_bias, out_weight, out_bias, mlp_gain, mlp_shift, fc1_weight, fc1_bias, fc2_weight, fc2_bias, images, img_attn_gain, img_attn_shift, img_qkv_weight, img_qv_bias, img_out_weight, img_out_bias, img_mlp_gain, img_mlp_shift, img_fc1_weight, img_fc1_bias, img_fc2_weight, img_fc2_bias):
    text_params = tuple((item.astype(jnp.float32) for item in (attn_gain, attn_shift, qkv_weight, qv_bias, out_weight, out_bias, mlp_gain, mlp_shift, fc1_weight, fc1_bias, fc2_weight, fc2_bias)))
    image_params = tuple((item.astype(jnp.float32) for item in (img_attn_gain, img_attn_shift, img_qkv_weight, img_qv_bias, img_out_weight, img_out_bias, img_mlp_gain, img_mlp_shift, img_fc1_weight, img_fc1_bias, img_fc2_weight, img_fc2_bias)))
    allowed = allowed_rows(segment_ids, valid_lengths).reshape(N_DP, ROWS_DEV, SEQ, SEQ)

    def one_group(params, pair):
        return block(params, pair[0], pair[1], ROWS_DEV, SEQ)
    checked = jax.checkpoint(one_group)

    def text_forward(params, stream):
        groups = stream.reshape(N_DP, ROWS_DEV * SEQ, D)
        outcome = lax.map(lambda pair: checked(params, pair), (groups, allowed))
        return outcome.reshape(TXT_TOK, D)
    text_out, pullback = jax.vjp(text_forward, text_params, text_in.astype(jnp.float32))
    param_grads, input_grad = pullback(text_grad.astype(jnp.float32))
    unmasked = jnp.ones((IMG_DEV, IMG_SEQ, IMG_SEQ), dtype=jnp.int32)
    image_groups = images.astype(jnp.float32).reshape(N_DP, IMG_DEV * IMG_SEQ, D)
    image_out = lax.map(lambda group: block(image_params, group, unmasked, IMG_DEV, IMG_SEQ), image_groups)
    image_out = image_out.reshape(IMG_TOK, D)
    return (text_out.astype(jnp.bfloat16), image_out.astype(jnp.bfloat16), input_grad.astype(jnp.bfloat16), param_grads[0], param_grads[1], param_grads[2], param_grads[3], param_grads[4], param_grads[5], param_grads[6], param_grads[7], param_grads[8], param_grads[9], param_grads[10], param_grads[11])
```

```python
import functools

import jax
import jax.numpy as jnp
from jax import lax
from jax.experimental import pallas as pl
from jax.experimental.pallas import tpu as pltpu
from jax.sharding import PartitionSpec as P

HEAD = 64
IMG_SEQ = 50
EPS = 1e-05
BF = jnp.bfloat16
F32 = jnp.float32
SCALE = HEAD ** (-0.5)
NEG = -1000000000.0
ROOT = 0.7978845608028654
CUBE = 0.044715

NN = (((1,), (0,)), ((), ()))
NT = (((1,), (1,)), ((), ()))
TN = (((0,), (0,)), ((), ()))


def dot(a, b, dims=NN):
    return lax.dot_general(a, b, dims, preferred_element_type=F32)


def shape(*dims, dtype=BF):
    return jax.ShapeDtypeStruct(dims, dtype)


def kernel_call(body, outs, args, scratch=(), flops=0, vmem=32, any_args=()):
    in_specs = [
        pl.BlockSpec(memory_space=pl.ANY if i in any_args else pltpu.VMEM)
        for i in range(len(args))
    ]
    moved = sum(a.size * a.dtype.itemsize for a in args) + sum(
        o.size * o.dtype.itemsize for o in outs
    )
    return pl.pallas_call(
        body,
        out_shape=tuple(outs),
        in_specs=in_specs,
        out_specs=tuple(pl.BlockSpec(memory_space=pltpu.VMEM) for _ in outs),
        scratch_shapes=list(scratch),
        compiler_params=pltpu.CompilerParams(vmem_limit_bytes=vmem * 1024 * 1024),
        cost_estimate=pl.CostEstimate(flops=int(flops), bytes_accessed=int(moved), transcendentals=0),
    )(*args)


def norm(x):
    centred = x - jnp.mean(x, axis=-1, keepdims=True)
    inverse = lax.rsqrt(jnp.mean(centred * centred, axis=-1, keepdims=True) + EPS)
    return centred * inverse, inverse


def norm_back(upstream, gain, normed, inverse):
    scaled = upstream * gain
    first = jnp.mean(scaled, axis=-1, keepdims=True)
    second = jnp.mean(scaled * normed, axis=-1, keepdims=True)
    return inverse * (scaled - first - normed * second)


def head_marks(width, dtype):
    lane = lax.broadcasted_iota(jnp.int32, (1, width), 1) // HEAD
    return [jnp.where(lane == h, 1.0, 0.0).astype(dtype) for h in range(width // HEAD)]


def stack_heads(rows, marks):
    return jnp.concatenate([rows * mark for mark in marks], axis=0)


def fold_heads(stacked, count, marks):
    total = stacked[:count] * marks[0]
    for h in range(1, len(marks)):
        total += stacked[h * count : (h + 1) * count] * marks[h]
    return total


def masked_scores(q_stack, k, mask):
    raw = dot(q_stack, k, NT)
    heads = raw.shape[0] // mask.shape[0]
    raw = raw.reshape(heads, mask.shape[0], mask.shape[1])
    return jnp.where(mask[None] > 0, raw * SCALE, NEG)


def softmax_parts(scores):
    peak = jnp.max(scores, axis=-1, keepdims=True)
    weights = jnp.exp(scores - peak)
    return weights, jnp.sum(weights, axis=-1, keepdims=True)


def attend(q, k, v, mask):
    count = q.shape[0]
    scores = masked_scores(stack_heads(q, head_marks(q.shape[1], BF)), k, mask)
    weights, total = softmax_parts(scores)
    probs = (weights / total).astype(BF).reshape(-1, mask.shape[1])
    return fold_heads(dot(probs, v), count, head_marks(q.shape[1], F32)).astype(BF)


def attend_back(q, k, v, grad, mask):
    count = q.shape[0]
    low = head_marks(q.shape[1], BF)
    q_stack = stack_heads(q, low)
    g_stack = stack_heads(grad, low)
    weights, total = softmax_parts(masked_scores(q_stack, k, mask))
    probs = weights / total
    prob_grad = dot(g_stack, v, NT).reshape(probs.shape)
    centre = jnp.sum(prob_grad * probs, axis=-1, keepdims=True)
    score_grad = (probs * (prob_grad - centre)).astype(BF).reshape(-1, mask.shape[1])
    probs_low = probs.astype(BF).reshape(-1, mask.shape[1])
    v_grad = dot(probs_low, g_stack, TN)
    q_grad = fold_heads(dot(score_grad, k), count, head_marks(q.shape[1], F32)) * SCALE
    k_grad = dot(score_grad, q_stack, TN) * SCALE
    return q_grad.astype(BF), k_grad.astype(BF), v_grad.astype(BF)


def gelu_parts(v):
    square = v * v
    t = jnp.tanh(ROOT * (v + CUBE * (square * v)))
    half = 0.5 * (1.0 + t)
    slope = half + 0.5 * v * (1.0 - t * t) * (ROOT * (1.0 + 3.0 * CUBE * square))
    return v * half, slope


def chunk_start(index, size):
    return pl.ds(pl.multiple_of(index * size, 16), size)


def row_blocks(count, length, first):
    blocks = []
    for low, high in ((0, first), (first, count)):
        row = low
        if (high - low) % 2:
            blocks.append((row * length, length))
            row += 1
        while row < high:
            blocks.append((row * length, 2 * length))
            row += 2
    return blocks


def attn_forward_kernel(blocks, x0, x1, x2, x3, gain, shift, w_t, bias, out_w, mask,
                        x_mine, rows_ref, qkv, ctx, keep0, keep1, send0, send1):
    me = lax.axis_index("mp")
    core = me % 2
    size = x0.shape[0]
    width = out_w.shape[0]
    gain_f, shift_f = gain[...].astype(F32), shift[...].astype(F32)
    bias_f = bias[...].astype(F32)
    for j, x in enumerate((x0, x1, x2, x3)):
        owner = me ^ j
        at = chunk_start(owner, size)
        if j % 2 == 0:
            x_mine[owner // 2] = x[...]
        normed, _ = norm(x[...].astype(F32))
        rows = (normed * gain_f + shift_f).astype(BF)
        rows_ref[at, :] = rows
        for part in range(3):
            out = dot(rows, w_t[part * width : (part + 1) * width, :], NT)
            if part != 1:
                out = out + bias_f[part // 2 : part // 2 + 1]
            qkv[part, at, :] = out.astype(BF)
    for start, count in blocks:
        at = slice(start, start + count)
        ctx[at, :] = attend(qkv[0, at, :], qkv[1, at, :], qkv[2, at, :], mask[at, :count])
    weight = out_w[...]
    for half, (keep, send) in enumerate(((keep0, send0), (keep1, send1))):
        send[...] = dot(ctx[chunk_start(2 * half + 1 - core, size), :], weight).astype(BF)
        keep[...] = dot(ctx[chunk_start(2 * half + core, size), :], weight).astype(BF)


def after_attn_kernel(half, x_mine, mine, theirs, out_bias, gain, shift, after, rows):
    total = mine[...].astype(F32) + theirs[...].astype(F32)
    stream = x_mine[half].astype(F32) + (total + out_bias[...].astype(F32))
    after[...] = stream
    normed, _ = norm(stream)
    rows[...] = (normed * gain[...].astype(F32) + shift[...].astype(F32)).astype(BF)


def mlp_kernel(rows0, rows1, grad0, grad1, w1, b1, w2,
               act, hid_grad, br_keep, br_send, mg_keep, mg_send):
    size = rows0.shape[0]
    bias = b1[...].astype(F32)
    parts = ((rows1, grad1, br_send, mg_send, 1), (rows0, grad0, br_keep, mg_keep, 0))
    for rows, grad, br, mg, place in parts:
        at = slice(place * size, (place + 1) * size)
        hidden = dot(rows[...], w1[...]) + bias
        active_grad = dot(grad[...], w2[...], NT)
        active, slope = gelu_parts(hidden)
        active = active.astype(BF)
        act[at, :] = active
        grads = (active_grad * slope).astype(BF)
        hid_grad[at, :] = grads
        mg[...] = dot(grads, w1[...], NT).astype(BF)
        br[...] = dot(active, w2[...]).astype(BF)


def mlp_back_kernel(after, mine, theirs, grad, gain, after_grad, out_grad, sums):
    normed, inverse = norm(after[...])
    rows_grad = mine[...].astype(F32) + theirs[...].astype(F32)
    sums[...] = jnp.concatenate(
        [
            jnp.sum(rows_grad * normed, axis=0, keepdims=True),
            jnp.sum(rows_grad, axis=0, keepdims=True),
        ],
        axis=0,
    )
    value = grad[...].astype(F32) + norm_back(rows_grad, gain[...].astype(F32), normed, inverse)
    after_grad[...] = value
    out_grad[...] = value.astype(BF)


def attn_back_first_kernel(blocks, og_mine, og_other, qkv, mask, out_w, og, cg, pg):
    core = lax.axis_index("mp") % 2
    size = og_mine.shape[0]
    for rows, place in ((og_mine, core), (og_other, 1 - core)):
        at = chunk_start(place, size)
        og[at, :] = rows[...]
        cg[at, :] = dot(rows[...], out_w[...], NT).astype(BF)
    for start, count in blocks:
        at = slice(start, start + count)
        grads = attend_back(
            qkv[0, at, :], qkv[1, at, :], qkv[2, at, :], cg[at, :], mask[at, :count]
        )
        for part in range(3):
            pg[part, at, :] = grads[part]


def attn_back_second_kernel(blocks, og_mine, og_other, cg_first, pg_first, qkv, mask, out_w, w_t,
                            og, pg, p0, p1, p2, p3, cg, flat):
    me = lax.axis_index("mp")
    core = me % 2
    size = og_mine.shape[0]
    width = out_w.shape[0]
    half = 2 * size
    done = pg_first.shape[1]
    cg[:half, :] = cg_first[...]
    for rows, place in ((og_mine, core), (og_other, 1 - core)):
        at = chunk_start(place, size)
        og[at, :] = rows[...]
        cg[chunk_start(2 + place, size), :] = dot(rows[...], out_w[...], NT).astype(BF)
    for start, count in blocks:
        at = slice(start, start + count)
        grads = attend_back(
            qkv[0, at, :], qkv[1, at, :], qkv[2, at, :], cg[at, :], mask[at, :count]
        )
        for part in range(3):
            pg[part, start - done : start - done + count, :] = grads[part]
            flat[part, at, :] = grads[part]
    for part in range(3):
        flat[part, :done, :] = pg_first[part]
    for j, out in ((3, p3), (1, p1), (2, p2), (0, p0)):
        at = chunk_start(me ^ j, size)
        total = dot(flat[0, at, :], w_t[:width, :])
        for part in range(1, 3):
            total += dot(flat[part, at, :], w_t[part * width : (part + 1) * width, :])
        out[...] = total.astype(BF)


def place_of(relative, order):
    place = 0
    for k, bit in enumerate(order):
        place = place + ((relative // bit) % 2) * 2 ** (len(order) - 1 - k)
    return place


def spread(full, keep, send, order):
    blocks = 2 ** len(order)
    size = full.shape[0] // blocks
    here = lax.axis_index("dp")
    for b in range(blocks):
        place = place_of(here ^ b, order)
        value = full[b * size : (b + 1) * size, :].astype(BF)

        @pl.when(place < blocks // 2)
        def _():
            keep[chunk_start(place, size), :] = value

        @pl.when(place >= blocks // 2)
        def _():
            send[chunk_start(place - blocks // 2, size), :] = value


def emit(full, outs, order):
    if order is None:
        outs[0][...] = full[...]
    else:
        spread(full, outs[0], outs[1], order)


def mlp_weights_kernel(orders, act0, act1, hg0, hg1, rows00, rows01, rows10, rows11,
                       tg00, tg01, tg10, tg11, *rest):
    per = 1 if orders[0] is None else 2
    outs2, outs1, sums, full = rest[:per], rest[per : 2 * per], rest[2 * per], rest[2 * per + 1]
    size = rows00.shape[0]
    rows = ((rows00, rows01), (rows10, rows11))
    grads = ((tg00, tg01), (tg10, tg11))
    total = None
    for half, act in enumerate((act0, act1)):
        for place in range(2):
            term = dot(act[place * size : (place + 1) * size, :], grads[half][place][...], TN)
            total = term if total is None else total + term
    full[...] = total
    emit(full, outs2, orders[0])
    total = None
    for half, hg in enumerate((hg0, hg1)):
        for place in range(2):
            term = dot(rows[half][place][...], hg[place * size : (place + 1) * size, :], TN)
            total = term if total is None else total + term
    full[...] = total
    emit(full, outs1, orders[1])
    fc2_bias = sum(
        jnp.sum(g[...].astype(F32), axis=0, keepdims=True) for pair in grads for g in pair
    )
    fc1_bias = sum(jnp.sum(h[...].astype(F32), axis=0, keepdims=True) for h in (hg0, hg1))
    sums[...] = jnp.concatenate([fc2_bias, fc1_bias], axis=0)


def attn_weights_kernel(orders, ctx, og0, og1, rows, pg_first, pg_rest, *rest):
    per = 1 if orders[0] is None else 2
    outs_a, outs_b = rest[:per], rest[per : 2 * per]
    out_sum, qv_sum, full = rest[2 * per : 2 * per + 3]
    half = og0.shape[0]
    done = pg_first.shape[1]
    width = ctx.shape[1]

    def part_grad(part):
        return dot(pg_first[part], rows[:done, :], TN) + dot(pg_rest[part], rows[done:, :], TN)

    full[:width, :] = part_grad(0)
    full[width:, :] = part_grad(1)
    emit(full, outs_a, orders[0])
    full[:width, :] = part_grad(2)
    full[width:, :] = dot(ctx[:half, :], og0[...], TN) + dot(ctx[half:, :], og1[...], TN)
    emit(full, outs_b, orders[1])
    out_sum[...] = jnp.sum(og0[...].astype(F32), axis=0, keepdims=True) + jnp.sum(
        og1[...].astype(F32), axis=0, keepdims=True
    )
    qv_sum[...] = jnp.concatenate(
        [
            jnp.sum(pg_first[part].astype(F32), axis=0, keepdims=True)
            + jnp.sum(pg_rest[part].astype(F32), axis=0, keepdims=True)
            for part in (0, 2)
        ],
        axis=0,
    )


def input_grad_kernel(x, mine, other, theirs, after_grad0, after_grad1, gain, grad, sums):
    side = lax.axis_index("mp") // 2
    normed, inverse = norm(x[...].astype(F32))
    rows_grad = mine[...].astype(F32) + other[...].astype(F32) + theirs[...].astype(F32)
    sums[...] = jnp.concatenate(
        [
            jnp.sum(rows_grad * normed, axis=0, keepdims=True),
            jnp.sum(rows_grad, axis=0, keepdims=True),
        ],
        axis=0,
    )
    after_grad = jnp.where(side == 0, after_grad0[...], after_grad1[...])
    value = after_grad + norm_back(rows_grad, gain[...].astype(F32), normed, inverse)
    grad[...] = value.astype(BF)


def text_out_kernel(mine, theirs, after0, after1, bias, out):
    side = lax.axis_index("mp") // 2
    after = jnp.where(side == 0, after0[...], after1[...])
    branch = mine[...].astype(F32) + theirs[...].astype(F32)
    out[...] = (after + (branch + bias[...].astype(F32))).astype(BF)


def gather_blocks_kernel(order, sizes, packed, *outs):
    blocks = 2 ** len(order)
    size = packed.shape[0] // blocks
    here = lax.axis_index("dp")
    edges = [sum(sizes[:i]) for i in range(len(sizes) + 1)]
    for b in range(blocks):
        value = packed[chunk_start(place_of(here ^ b, order), size), :].astype(F32)
        for out, low, high in zip(outs, edges[:-1], edges[1:]):
            first, last = max(low, b * size), min(high, (b + 1) * size)
            if first < last:
                out[first - low : last - low, :] = value[first - b * size : last - b * size]


def image_windows(count, images):
    windows = []
    per = 4
    for low in range(0, images, per):
        start = (low * IMG_SEQ + 15) // 16 * 16 if low else 0
        end = min(count, ((low + per) * IMG_SEQ + 15) // 16 * 16)
        if low + per >= images:
            end = count
        key_start = start // IMG_SEQ * IMG_SEQ // 16 * 16
        key_end = min(count, ((end - 1) // IMG_SEQ * IMG_SEQ + IMG_SEQ + 15) // 16 * 16)
        windows.append((start, end, key_start, key_end))
    return windows


def image_kernel(x, gain1, shift1, out_bias, gain2, shift2, fc2_bias, own, w1, w2, w3,
                 out, bundle, sems):
    count, dim = x.shape
    images = count // IMG_SEQ
    sources = (own, w1, w2, w3)
    width = dim // 4
    attn_rows, fc_rows = 4 * width, dim
    cuts = ((0, attn_rows), (attn_rows, attn_rows + 2 * fc_rows + 16))
    copies = []
    for phase, (low, high) in enumerate(cuts):
        for s, source in enumerate(sources):
            copies.append(
                pltpu.make_async_copy(
                    source.at[low:high], bundle.at[s, low:high], sems.at[phase, s]
                )
            )
    bias_at = attn_rows + 2 * fc_rows
    bias_copies = [
        pltpu.make_async_copy(
            source.at[bias_at + 16 : bias_at + 32], bundle.at[s, bias_at + 16 : bias_at + 32], sems.at[2, s]
        )
        for s, source in enumerate(sources)
    ]
    for copy in bias_copies + copies:
        copy.start()
    stream = x[...].astype(F32)
    normed, _ = norm(stream)
    rows = (normed * gain1[...].astype(F32) + shift1[...].astype(F32)).astype(BF)
    total = jnp.zeros((count, dim), F32)
    windows = image_windows(count, images)
    for s in range(4):
        bias_copies[s].wait()
        copies[s].wait()
        weights = bundle.at[s]
        bias = bundle[s, bias_at + 16 : bias_at + 32, :].astype(F32)
        q = (dot(rows, weights[:width, :], NT) + bias[0:1, :width]).astype(BF)
        k = dot(rows, weights[width : 2 * width, :], NT).astype(BF)
        v = (dot(rows, weights[2 * width : 3 * width, :], NT) + bias[1:2, :width]).astype(BF)
        parts = []
        for q_low, q_high, k_low, k_high in windows:
            extent = (q_high - q_low, k_high - k_low)
            q_image = (lax.broadcasted_iota(jnp.int32, extent, 0) + q_low) // IMG_SEQ
            k_image = (lax.broadcasted_iota(jnp.int32, extent, 1) + k_low) // IMG_SEQ
            mask = jnp.where(q_image == k_image, 1.0, 0.0)
            parts.append(attend(q[q_low:q_high], k[k_low:k_high], v[k_low:k_high], mask))
        context = jnp.concatenate(parts, axis=0)
        total += dot(context, weights[3 * width : 4 * width, :])
    after = stream + (total + out_bias[...].astype(F32))
    normed, _ = norm(after)
    rows = (normed * gain2[...].astype(F32) + shift2[...].astype(F32)).astype(BF)
    total = jnp.zeros((count, dim), F32)
    for s in range(4):
        copies[4 + s].wait()
        weights = bundle.at[s]
        bias = bundle[s, bias_at : bias_at + 16, :].astype(F32)[0:1]
        hidden = dot(rows, weights[attn_rows : attn_rows + fc_rows, :]) + bias
        active = gelu_parts(hidden)[0].astype(BF)
        total += dot(active, weights[attn_rows + fc_rows : attn_rows + 2 * fc_rows, :])
    out[...] = (after + (total + fc2_bias[...].astype(F32))).astype(BF)


def core_swap(x):
    return lax.ppermute(x, "mp", [(i, i ^ 1) for i in range(lax.axis_size("mp"))])


def side_swap(x):
    return lax.ppermute(x, "mp", [(i, i ^ 2) for i in range(lax.axis_size("mp"))])


def dp_swap(x, bit):
    return lax.ppermute(x, "dp", [(i, i ^ bit) for i in range(lax.axis_size("dp"))])


def add_low(a, b):
    return (a.astype(F32) + b.astype(F32)).astype(BF)


def butterfly(keep, send, order):
    for k, bit in enumerate(order):
        arrived = dp_swap(send, bit)
        if k + 1 < len(order):
            half = keep.shape[0] // 2
            keep, send = (
                add_low(keep[:half], arrived[:half]),
                add_low(keep[half:], arrived[half:]),
            )
        else:
            keep = add_low(keep, arrived)
    for bit in reversed(order):
        keep = jnp.concatenate([keep, dp_swap(keep, bit)], axis=0)
    return keep


def per_device(
    text_in,
    segment_ids,
    valid_lengths,
    text_grad,
    attn_gain,
    attn_shift,
    qkv_weight,
    qv_bias,
    out_weight,
    out_bias,
    mlp_gain,
    mlp_shift,
    fc1_weight,
    fc1_bias,
    fc2_weight,
    fc2_bias,
    images,
    img_attn_gain,
    img_attn_shift,
    img_qkv_weight,
    img_qv_bias,
    img_out_weight,
    img_out_bias,
    img_mlp_gain,
    img_mlp_shift,
    img_fc1_weight,
    img_fc1_bias,
    img_fc2_weight,
    img_fc2_bias,
):
    size, dim = text_in.shape
    row_count, length = segment_ids.shape
    width = qkv_weight.shape[2]
    n_dp = lax.axis_size("dp")
    tokens = 4 * size
    side = lax.axis_index("mp") // 2
    flat = lambda v: v.reshape(1, -1)

    w_t = qkv_weight.transpose(1, 2, 0).reshape(3 * width, dim)
    img_w_t = img_qkv_weight.transpose(1, 2, 0).reshape(3 * width, dim)
    used = 4 * width + 2 * dim + 32
    total_rows = -(-used // (16 * n_dp)) * 16 * n_dp
    bundle = jnp.concatenate(
        [
            img_w_t,
            img_out_weight,
            img_fc1_weight,
            img_fc2_weight,
            jnp.pad(flat(img_fc1_bias), ((0, 15), (0, 0))),
            jnp.pad(img_qv_bias, ((0, total_rows - used + 14), (0, dim - width))),
        ],
        axis=0,
    )
    part_rows = total_rows // n_dp

    x0 = text_in
    x2 = side_swap(x0)
    x1 = core_swap(x0)
    part = lax.dynamic_slice_in_dim(bundle, lax.axis_index("dp") * part_rows, part_rows, 0)
    far_part = side_swap(part)
    x3 = core_swap(x2)
    far_bundle = lax.all_gather(far_part, "dp", axis=0, tiled=True)

    t0 = text_grad
    t1 = core_swap(t0)
    t2 = side_swap(t0)
    t3 = core_swap(t2)
    first = side == 0
    tg = (
        (jnp.where(first, t0, t2), jnp.where(first, t1, t3)),
        (jnp.where(first, t2, t0), jnp.where(first, t3, t1)),
    )

    rows_first = 2 * size // length
    blocks = row_blocks(row_count, length, rows_first)
    positions = jnp.arange(length, dtype=jnp.int32)
    same = segment_ids[:, :, None] == segment_ids[:, None, :]
    live = positions[None, None, :] < valid_lengths[:, None, None]
    diagonal = (positions[:, None] == positions[None, :])[None]
    allowed = (same & (live | diagonal)).astype(F32)
    pieces = []
    for start, count in blocks:
        row = start // length
        if count == length:
            pieces.append(jnp.pad(allowed[row], ((0, 0), (0, length))))
        else:
            pieces.append(jnp.pad(allowed[row], ((0, 0), (0, length))))
            pieces.append(jnp.pad(allowed[row + 1], ((0, 0), (length, 0))))
    mask = jnp.concatenate(pieces, axis=0)
    blocks_first = [b for b in blocks if b[0] < rows_first * length]
    blocks_rest = [b for b in blocks if b[0] >= rows_first * length]

    chunk = shape(size, dim)
    x_mine, attn_rows, qkv, ctx, keep0, keep1, send0, send1 = kernel_call(
        functools.partial(attn_forward_kernel, blocks),
        [shape(2, size, dim), shape(tokens, dim), shape(3, tokens, width), shape(tokens, width)]
        + [chunk] * 4,
        [x0, x1, x2, x3, flat(attn_gain), flat(attn_shift), w_t, qv_bias, out_weight, mask],
        flops=2 * tokens * dim * width * 4,
    )

    after, mlp_rows, mlp_other = [], [], []
    for half, (keep, send) in enumerate(((keep0, send0), (keep1, send1))):
        mine = add_low(keep, core_swap(send))
        theirs = side_swap(mine)
        stream, rows = kernel_call(
            functools.partial(after_attn_kernel, half),
            [shape(size, dim, dtype=F32), chunk],
            [x_mine, mine, theirs, flat(out_bias), flat(mlp_gain), flat(mlp_shift)],
        )
        after.append(stream)
        mlp_rows.append(rows)
        mlp_other.append(core_swap(rows))

    act, hid_grad, branch = [], [], []
    after_grad, out_grad, out_grad_other, mlp_sums = [], [], [], []
    for half in range(2):
        active, hidden_grad, br_keep, br_send, mg_keep, mg_send = kernel_call(
            mlp_kernel,
            [shape(2 * size, dim)] * 2 + [chunk] * 4,
            [mlp_rows[half], mlp_other[half], *tg[half], fc1_weight, flat(fc1_bias), fc2_weight],
            flops=2 * 2 * size * dim * dim * 4,
        )
        act.append(active)
        hid_grad.append(hidden_grad)
        mine = add_low(mg_keep, core_swap(mg_send))
        theirs = side_swap(mine)
        value, low, sums = kernel_call(
            mlp_back_kernel,
            [shape(size, dim, dtype=F32), chunk, shape(2, dim, dtype=F32)],
            [after[half], mine, theirs, tg[half][0], flat(mlp_gain)],
        )
        after_grad.append(value)
        out_grad.append(low)
        out_grad_other.append(core_swap(low))
        mlp_sums.append(sums)
        branch.append(add_low(br_keep, core_swap(br_send)))

    bits = [2**k for k in range(n_dp.bit_length() - 1)]
    order_a, order_b = tuple(bits), tuple(bits[1:] + bits[:1])
    plain = 2 ** len(bits) != n_dp or (2 * width) % (16 * n_dp) != 0 or dim % (16 * n_dp) != 0
    if plain:
        order_a = order_b = None

    def grad_shapes(rows):
        if plain:
            return [shape(rows, dim, dtype=F32)]
        return [shape(rows // 2, dim)] * 2

    def reduce(parts, order, sizes):
        if plain:
            total = lax.psum(parts[0], "dp")
            return jnp.split(total, [sum(sizes[: i + 1]) for i in range(len(sizes) - 1)], axis=0)
        packed = butterfly(*parts, order)
        return kernel_call(
            functools.partial(gather_blocks_kernel, order, sizes),
            [shape(rows, dim, dtype=F32) for rows in sizes],
            [packed],
        )

    *parts, fc_sums = kernel_call(
        functools.partial(mlp_weights_kernel, (order_a, order_b)),
        grad_shapes(dim) * 2 + [shape(2, dim, dtype=F32)],
        [*act, *hid_grad, mlp_rows[0], mlp_other[0], mlp_rows[1], mlp_other[1], *tg[0], *tg[1]],
        scratch=[pltpu.VMEM((dim, dim), F32)],
        flops=2 * tokens * dim * dim * 2,
    )
    per = len(parts) // 2
    (grad_fc2_weight,) = reduce(parts[:per], order_a, (dim,))
    (grad_fc1_weight,) = reduce(parts[per:], order_b, (dim,))

    og_first, cg_first, pg_first = kernel_call(
        functools.partial(attn_back_first_kernel, blocks_first),
        [shape(2 * size, dim), shape(2 * size, width), shape(3, rows_first * length, width)],
        [out_grad[0], out_grad_other[0], qkv, mask, out_weight],
        flops=2 * 2 * size * dim * width * 2,
    )
    rest = tokens - rows_first * length
    og_second, pg_rest, p0, p1, p2, p3 = kernel_call(
        functools.partial(attn_back_second_kernel, blocks_rest),
        [shape(2 * size, dim), shape(3, rest, width)] + [chunk] * 4,
        [out_grad[1], out_grad_other[1], cg_first, pg_first, qkv, mask, out_weight, w_t],
        scratch=[pltpu.VMEM((tokens, width), BF), pltpu.VMEM((3, tokens, width), BF)],
        flops=2 * tokens * dim * width * 4,
    )
    to_side = add_low(p2, core_swap(p3))
    other = core_swap(p1)
    theirs = side_swap(to_side)
    text_in_grad, attn_sums = kernel_call(
        input_grad_kernel,
        [chunk, shape(2, dim, dtype=F32)],
        [text_in, p0, other, theirs, *after_grad, flat(attn_gain)],
    )

    *parts, out_sum, qv_sum = kernel_call(
        functools.partial(attn_weights_kernel, (order_a, order_b)),
        grad_shapes(2 * width) * 2 + [shape(1, dim, dtype=F32), shape(2, width, dtype=F32)],
        [ctx, og_first, og_second, attn_rows, pg_first, pg_rest],
        scratch=[pltpu.VMEM((2 * width, dim), F32)],
        flops=2 * tokens * dim * width * 4,
    )
    per = len(parts) // 2
    (grad_qk,) = reduce(parts[:per], order_a, (2 * width,))
    grad_v, grad_out_weight = reduce(parts[per:], order_b, (width, width))
    grad_qkv = jnp.concatenate([grad_qk, grad_v], axis=0)
    grad_qkv_weight = grad_qkv.reshape(3, width, dim).transpose(2, 0, 1)

    norm_sums = jnp.concatenate([mlp_sums[0] + mlp_sums[1], attn_sums], axis=0)
    norm_sums = norm_sums + core_swap(norm_sums)
    norm_sums = jnp.concatenate([norm_sums[:2], norm_sums[2:] + side_swap(norm_sums[2:])], axis=0)
    small = jnp.concatenate(
        [norm_sums, fc_sums, out_sum, jnp.pad(flat(qv_sum), ((0, 0), (0, dim - 2 * width)))], axis=0
    )
    if plain:
        small = lax.psum(small, "dp")
    else:
        for bit in bits:
            small = small + dp_swap(small, bit)

    text_out = None
    theirs = side_swap(jnp.where(first, branch[1], branch[0]))
    (text_out,) = kernel_call(
        text_out_kernel,
        [chunk],
        [jnp.where(first, branch[0], branch[1]), theirs, *after, flat(fc2_bias)],
    )

    own_other = core_swap(bundle)
    far_other = core_swap(far_bundle)
    (image_out,) = kernel_call(
        image_kernel,
        [shape(*images.shape)],
        [images, flat(img_attn_gain), flat(img_attn_shift), flat(img_out_bias),
         flat(img_mlp_gain), flat(img_mlp_shift), flat(img_fc2_bias),
         bundle, own_other, far_bundle, far_other],
        scratch=[pltpu.VMEM((4, used, dim), BF), pltpu.SemaphoreType.DMA((3, 4))],
        flops=2 * images.shape[0] * dim * dim * 12,
        vmem=48,
        any_args=(7, 8, 9, 10),
    )
    return (
        text_out,
        image_out,
        text_in_grad,
        small[2],
        small[3],
        grad_qkv_weight,
        small[7, : 2 * width].reshape(2, width),
        grad_out_weight,
        small[6],
        small[0],
        small[1],
        grad_fc1_weight,
        small[5],
        grad_fc2_weight,
        small[4],
    )


def solution(mesh):
    in_specs = (
        P(("dp", "mp"), None),
        P("dp", None),
        P("dp"),
        P(("dp", "mp"), None),
        P(),
        P(),
        P(None, None, "mp"),
        P(None, "mp"),
        P("mp", None),
        P(),
        P(),
        P(),
        P(None, "mp"),
        P("mp"),
        P("mp", None),
        P(),
        P(("dp", "mp"), None),
        P(),
        P(),
        P(None, None, "mp"),
        P(None, "mp"),
        P("mp", None),
        P(),
        P(),
        P(),
        P(None, "mp"),
        P("mp"),
        P("mp", None),
        P(),
    )
    out_specs = (
        P(("dp", "mp"), None),
        P(("dp", "mp"), None),
        P(("dp", "mp"), None),
        P(),
        P(),
        P(None, None, "mp"),
        P(None, "mp"),
        P("mp", None),
        P(),
        P(),
        P(),
        P(None, "mp"),
        P("mp"),
        P("mp", None),
        P(),
    )
    return jax.shard_map(
        per_device, mesh=mesh, in_specs=in_specs, out_specs=out_specs, check_vma=False
    )
```

```python
import functools

import jax
import jax.numpy as jnp
from jax import lax
from jax.experimental import pallas as pl
from jax.experimental.pallas import tpu as pltpu
from jax.sharding import PartitionSpec as P

HEAD = 64
IMG_SEQ = 50
EPS = 1e-05
BF = jnp.bfloat16
F32 = jnp.float32
SCALE = HEAD ** (-0.5)
NEG = -1000000000.0
ROOT = 0.7978845608028654
CUBE = 0.044715

NN = (((1,), (0,)), ((), ()))
NT = (((1,), (1,)), ((), ()))
TN = (((0,), (0,)), ((), ()))


def dot(a, b, dims=NN):
    return lax.dot_general(a, b, dims, preferred_element_type=F32)


def shape(*dims, dtype=BF):
    return jax.ShapeDtypeStruct(dims, dtype)


class Line:
    def __init__(self):
        self.token = None

    def __call__(self, body, outs, args, scratch=(), vmem=16, untouched=(), scalars=(), after=(),
                 same=None, outside=False):
        args = list(args)
        real = len(args)
        args += list(after) + ([] if self.token is None else [self.token])
        given = len(args)

        def in_space(i):
            if i >= real or i in untouched:
                return pl.ANY
            return pltpu.SMEM if i in scalars else pltpu.VMEM

        def run(*refs):
            body(*refs[:real], *refs[given : given + len(outs)], *refs[given + len(outs) + 1 :])

        out_space = pl.ANY if outside or same is not None else pltpu.VMEM
        results = pl.pallas_call(
            run,
            out_shape=(*outs, shape(8, 128, dtype=F32)),
            in_specs=[pl.BlockSpec(memory_space=in_space(i)) for i in range(given)],
            out_specs=tuple(
                pl.BlockSpec(memory_space=space) for space in [out_space] * len(outs) + [pl.ANY]
            ),
            scratch_shapes=list(scratch),
            input_output_aliases={} if same is None else {same: 0},
            compiler_params=pltpu.CompilerParams(vmem_limit_bytes=vmem * 1024 * 1024),
            cost_estimate=pl.CostEstimate(flops=1, bytes_accessed=1, transcendentals=0),
        )(*args)
        self.token = results[-1]
        return results[:-1] if len(outs) > 1 else results[0]

    def hold(self, value):
        return self(lambda *refs: None, [shape(*value.shape, dtype=value.dtype)], [value],
                    untouched=(0,), same=0)


def norm(x):
    centred = x - jnp.mean(x, axis=-1, keepdims=True)
    inverse = lax.rsqrt(jnp.mean(centred * centred, axis=-1, keepdims=True) + EPS)
    return centred * inverse, inverse


def norm_back(upstream, gain, normed, inverse):
    scaled = upstream * gain
    first = jnp.mean(scaled, axis=-1, keepdims=True)
    second = jnp.mean(scaled * normed, axis=-1, keepdims=True)
    return inverse * (scaled - first - normed * second)


def head_marks(width, dtype):
    lane = lax.broadcasted_iota(jnp.int32, (1, width), 1) // HEAD
    return [jnp.where(lane == h, 1.0, 0.0).astype(dtype) for h in range(width // HEAD)]


def stack_heads(rows, marks):
    return jnp.concatenate([rows * mark for mark in marks], axis=0)


def fold_heads(stacked, count, marks):
    total = stacked[:count] * marks[0]
    for h in range(1, len(marks)):
        total += stacked[h * count : (h + 1) * count] * marks[h]
    return total


def masked_scores(q_stack, k, mask):
    raw = dot(q_stack, k, NT)
    heads = raw.shape[0] // mask.shape[0]
    raw = raw.reshape(heads, mask.shape[0], mask.shape[1])
    return jnp.where(mask[None] > 0, raw * SCALE, NEG)


def softmax_parts(scores):
    peak = jnp.max(scores, axis=-1, keepdims=True)
    weights = jnp.exp(scores - peak)
    return weights, jnp.sum(weights, axis=-1, keepdims=True)


def attend(q, k, v, mask):
    count = q.shape[0]
    scores = masked_scores(stack_heads(q, head_marks(q.shape[1], BF)), k, mask)
    weights, total = softmax_parts(scores)
    probs = (weights / total).astype(BF).reshape(-1, mask.shape[1])
    return fold_heads(dot(probs, v), count, head_marks(q.shape[1], F32)).astype(BF)


def attend_back(q, k, v, grad, mask):
    count = q.shape[0]
    low = head_marks(q.shape[1], BF)
    q_stack = stack_heads(q, low)
    g_stack = stack_heads(grad, low)
    weights, total = softmax_parts(masked_scores(q_stack, k, mask))
    probs = weights / total
    prob_grad = dot(g_stack, v, NT).reshape(probs.shape)
    centre = jnp.sum(prob_grad * probs, axis=-1, keepdims=True)
    score_grad = (probs * (prob_grad - centre)).astype(BF).reshape(-1, mask.shape[1])
    probs_low = probs.astype(BF).reshape(-1, mask.shape[1])
    v_grad = dot(probs_low, g_stack, TN)
    q_grad = fold_heads(dot(score_grad, k), count, head_marks(q.shape[1], F32)) * SCALE
    k_grad = dot(score_grad, q_stack, TN) * SCALE
    return q_grad.astype(BF), k_grad.astype(BF), v_grad.astype(BF)


def gelu_parts(v):
    square = v * v
    t = jnp.tanh(ROOT * (v + CUBE * (square * v)))
    half = 0.5 * (1.0 + t)
    slope = half + 0.5 * v * (1.0 - t * t) * (ROOT * (1.0 + 3.0 * CUBE * square))
    return v * half, slope


def repeat(count, body):
    def step(i, carry):
        body(i)
        return carry

    lax.fori_loop(0, count, step, 0)


def lanes(index, size):
    return pl.ds(pl.multiple_of(index * size, 128), size)


def chunk_start(index, size):
    return pl.ds(pl.multiple_of(index * size, 16), size)


def row_blocks(count, length, first):
    blocks = []
    for low, high in ((0, first), (first, count)):
        row = low
        if (high - low) % 2:
            blocks.append((row * length, length))
            row += 1
        while row < high:
            blocks.append((row * length, 2 * length))
            row += 2
    return blocks


def mask_kernel(blocks, segments, lengths, mask):
    length = segments.shape[1]
    square = (length, length)
    key = lax.broadcasted_iota(jnp.int32, square, 1)
    diagonal = key == lax.broadcasted_iota(jnp.int32, square, 0)
    mask[...] = jnp.zeros(mask.shape, F32)
    for start, count in blocks:
        for place in range(count // length):
            row = start // length + place
            along = jnp.broadcast_to(segments[row : row + 1, :].astype(F32), square)
            seen = (along == along.T) & ((key < lengths[row]) | diagonal)
            low = start + place * length
            mask[low : low + length, place * length : (place + 1) * length] = jnp.where(
                seen, 1.0, 0.0
            )


def bundle_kernel(w_t, out_w, qv, bundle, held, sems):
    width = qv.shape[1]
    held[...] = jnp.zeros(held.shape, held.dtype)
    held[0:2, :width] = qv[...]
    start, copies = 0, []
    for k, piece in enumerate((w_t, out_w, held)):
        rows = piece.shape[0]
        copies.append(pltpu.make_async_copy(piece, bundle.at[start : start + rows], sems.at[k]))
        copies[-1].start()
        start += rows
    for copy in copies:
        copy.wait()


ATTN_GAIN, ATTN_SHIFT, OUT_BIAS, MLP_GAIN, MLP_SHIFT, FC2_BIAS, FC1_BIAS = range(7)


def vectors_kernel(*refs):
    *items, text, image = refs
    for out, own in ((text, items[: len(items) // 2]), (image, items[len(items) // 2 :])):
        out[...] = jnp.zeros(out.shape, F32)
        for k, item in enumerate(own):
            out[k : k + 1, :] = item[...].astype(F32).reshape(1, -1)


def vector(vectors, index):
    return vectors[index : index + 1, :]


def project(x_pair, vectors, w_t, bias, rows, qkv, bias_rows, at):
    size = x_pair.shape[1]
    width = bias.shape[1]
    gain, shift = vector(vectors, ATTN_GAIN), vector(vectors, ATTN_SHIFT)
    bias_rows[...] = jnp.zeros(bias_rows.shape, F32)
    bias_rows[0:1, :] = bias[...].astype(F32)[0:1]
    bias_rows[2:3, :] = bias[...].astype(F32)[1:2]

    def normalize(i):
        normed, _ = norm(x_pair[i].astype(F32))
        rows[chunk_start(i, size), :] = (normed * gain + shift).astype(BF)

    def part(i):
        value = dot(rows[...], w_t[chunk_start(i, width), :], NT) + bias_rows[pl.ds(i, 1), :]
        qkv[i, at, :] = value.astype(BF)

    repeat(2, normalize)
    repeat(3, part)


def own_rows_kernel(x0, x1, vectors, w_t, bias, rows_out, qkv, x_pair, bias_rows):
    core = lax.axis_index("mp") % 2
    x_pair[core] = x0[...]
    x_pair[1 - core] = x1[...]
    project(x_pair, vectors, w_t, bias, rows_out, qkv, bias_rows, slice(None))


def far_operands_kernel(grad, bundle, packed, sem):
    size = grad.shape[0]
    part = packed.shape[0] - size
    copy = pltpu.make_async_copy(
        bundle.at[chunk_start(lax.axis_index("dp"), part)], packed.at[size:], sem
    )
    copy.start()
    packed[:size] = grad[...]
    copy.wait()


def unpack_kernel(packed, grad, part):
    size = grad.shape[0]
    grad[...] = packed[:size]
    part[...] = packed[size:]


def block_loop(blocks, body, unroll=False):
    if unroll:
        for start, tokens in blocks:
            body(pl.ds(start, tokens), tokens)
        return
    singles = [b for b in blocks if b[1] != blocks[-1][1]]
    pairs = [b[0] for b in blocks if b[1] == blocks[-1][1]]
    count = blocks[-1][1]
    for start, tokens in singles:
        body(pl.ds(start, tokens), tokens)

    def pair(i):
        start = pairs[0] + i * count
        for k in range(1, len(pairs)):
            gap = pairs[k] - pairs[k - 1] - count
            if gap:
                start = start + jnp.where(i >= k, gap, 0)
        body(pl.ds(pl.multiple_of(start, 16), count), count)

    repeat(len(pairs), pair)


def attn_forward_kernel(blocks, x2, x3, qkv_own, vectors, w_t, bias, out_w, mask,
                        rows_out, qkv, ctx, keep0, keep1, send0, send1, x_pair, bias_rows):
    me = lax.axis_index("mp")
    core, side = me % 2, me // 2
    size, dim = x2.shape
    x_pair[core] = x2[...]
    x_pair[1 - core] = x3[...]
    far = chunk_start(1 - side, 2 * size)
    project(x_pair, vectors, w_t, bias, rows_out, qkv, bias_rows, far)
    own = chunk_start(side, 2 * size)
    for part in range(3):
        qkv[part, own, :] = qkv_own[part]

    def block(at, count):
        ctx[at, :] = attend(qkv[0, at, :], qkv[1, at, :], qkv[2, at, :], mask[at, :count])

    block_loop(blocks, block, unroll=True)

    def columns(i):
        cols = lanes(i, 256)
        weight = out_w[:, cols]
        for half, (keep, send) in enumerate(((keep0, send0), (keep1, send1))):
            theirs = ctx[chunk_start(2 * half + 1 - core, size), :]
            send[:, cols] = dot(theirs, weight).astype(BF)
            mine = ctx[chunk_start(2 * half + core, size), :]
            keep[:, cols] = dot(mine, weight).astype(BF)

    repeat(dim // 256, columns)


def add_kernel(a, b, out):
    out[...] = (a[...].astype(F32) + b[...].astype(F32)).astype(BF)


def add_pair_kernel(a0, b0, a1, b1, out0, out1):
    for a, b, out in ((a0, b0, out0), (a1, b1, out1)):
        out[...] = (a[...].astype(F32) + b[...].astype(F32)).astype(BF)


def add_split_kernel(a, b, keep, send):
    half = keep.shape[0]
    keep[...] = (a[:half].astype(F32) + b[:half].astype(F32)).astype(BF)
    send[...] = (a[half:].astype(F32) + b[half:].astype(F32)).astype(BF)


def join_kernel(a, b, out):
    half = a.shape[0]
    out[:half] = a[...]
    out[half:] = b[...]


def chosen(half, own, far):
    return jnp.where(lax.axis_index("mp") // 2 == half, own[...], far[...])


def after_attn_kernel(half, x0, x2, mine, theirs, vectors, after_out, rows):
    total = mine[...].astype(F32) + theirs[...].astype(F32)
    stream = chosen(half, x0, x2).astype(F32) + (total + vector(vectors, OUT_BIAS))
    after_out[...] = stream
    normed, _ = norm(stream)
    rows[...] = (normed * vector(vectors, MLP_GAIN) + vector(vectors, MLP_SHIFT)).astype(BF)


def mlp_kernel(half, rows0, rows1, t0, t1, t2, t3, w1, vectors, w2,
               act, hid_grad, br_keep, br_send, mg_keep, mg_send, rows, grad):
    size, dim = rows0.shape
    rows[:size, :] = rows0[...]
    rows[size:, :] = rows1[...]
    grad[:size, :] = chosen(half, t0, t2)
    grad[size:, :] = chosen(half, t1, t3)

    def units(i):
        cols = lanes(i, 256)
        hidden = dot(rows[...], w1[:, cols]) + vectors[FC1_BIAS : FC1_BIAS + 1, cols]
        active, slope = gelu_parts(hidden)
        act[:, cols] = active.astype(BF)
        active_grad = dot(grad[...], w2[cols, :], NT)
        hid_grad[:, cols] = (active_grad * slope).astype(BF)

    def columns(i):
        cols = lanes(i, 256)
        value = dot(hid_grad[...], w1[cols, :], NT).astype(BF)
        mg_keep[:, cols] = value[:size]
        mg_send[:, cols] = value[size:]
        value = dot(act[...], w2[:, cols]).astype(BF)
        br_keep[:, cols] = value[:size]
        br_send[:, cols] = value[size:]

    repeat(w1.shape[1] // 256, units)
    repeat(dim // 256, columns)


def mlp_back_kernel(half, after, mine, theirs, t0, t2, vectors, after_grad, out_grad, sums):
    normed, inverse = norm(after[...])
    rows_grad = mine[...].astype(F32) + theirs[...].astype(F32)
    sums[...] = jnp.concatenate(
        [
            jnp.sum(rows_grad * normed, axis=0, keepdims=True),
            jnp.sum(rows_grad, axis=0, keepdims=True),
        ],
        axis=0,
    )
    value = chosen(half, t0, t2).astype(F32) + norm_back(
        rows_grad, vector(vectors, MLP_GAIN), normed, inverse
    )
    after_grad[...] = value
    out_grad[...] = value.astype(BF)


def attn_back_first_kernel(blocks, og_mine, og_other, qkv, mask, out_w, og, cg, pg):
    core = lax.axis_index("mp") % 2
    size = og_mine.shape[0]
    og[chunk_start(core, size), :] = og_mine[...]
    og[chunk_start(1 - core, size), :] = og_other[...]
    cg[...] = dot(og[...], out_w[...], NT).astype(BF)

    def block(at, count):
        grads = attend_back(
            qkv[0, at, :], qkv[1, at, :], qkv[2, at, :], cg[at, :], mask[at, :count]
        )
        for part in range(3):
            pg[part, at, :] = grads[part]

    block_loop(blocks, block)


def attn_back_second_kernel(blocks, og_mine, og_other, cg_first, pg_first, qkv, mask, out_w, w_t,
                            og, pg, p0, p1, p2, p3, cg):
    me = lax.axis_index("mp")
    core = me % 2
    size, dim = og_mine.shape
    width = out_w.shape[0]
    half = 2 * size
    done = pg_first.shape[1]
    og[chunk_start(core, size), :] = og_mine[...]
    og[chunk_start(1 - core, size), :] = og_other[...]
    cg[half:, :] = dot(og[...], out_w[...], NT).astype(BF)
    cg[:half, :] = cg_first[...]
    for part in range(3):
        pg[part, :done, :] = pg_first[part]

    def block(at, count):
        grads = attend_back(
            qkv[0, at, :], qkv[1, at, :], qkv[2, at, :], cg[at, :], mask[at, :count]
        )
        for part in range(3):
            pg[part, at, :] = grads[part]

    block_loop(blocks, block, unroll=True)

    def columns(i):
        cols = lanes(i, 256)
        for j, out in ((3, p3), (1, p1), (2, p2), (0, p0)):
            at = chunk_start(me ^ j, size)
            total = dot(pg[0, at, :], w_t[:width, cols])
            for part in range(1, 3):
                total += dot(pg[part, at, :], w_t[part * width : (part + 1) * width, cols])
            out[:, cols] = total.astype(BF)

    repeat(dim // 256, columns)


def place_in(relative, order):
    place = 0
    for k, bit in enumerate(order):
        place = place + ((relative // bit) % 2) * 2 ** (len(order) - 1 - k)
    return place


def place_of(relative, orders):
    core = lax.axis_index("mp") % 2
    return jnp.where(core == 0, place_in(relative, orders[0]), place_in(relative, orders[1]))


def emit(full, outs, orders):
    if orders is None:
        outs[0][...] = full[...]
        return
    keep, send = outs
    blocks = 2 ** len(orders[0])
    size = full.shape[0] // blocks
    here = lax.axis_index("dp")

    def block(b):
        place = place_of(here ^ b, orders)
        value = full[chunk_start(b, size), :].astype(BF)

        @pl.when(place < blocks // 2)
        def _():
            keep[chunk_start(place, size), :] = value

        @pl.when(place >= blocks // 2)
        def _():
            send[chunk_start(place - blocks // 2, size), :] = value

    repeat(blocks, block)


def weight_product(left, right, full):
    def block(i):
        at = pl.ds(pl.multiple_of(i * 256, 256), 256)
        full[at, :] = dot(left[:, lanes(i, 256)], right[...], TN)

    repeat(left.shape[1] // 256, block)


def row_sum(ref):
    return jnp.sum(ref[...].astype(F32), axis=0, keepdims=True)


def fc2_weight_kernel(orders, act0, act1, t0, t1, t2, t3, *rest):
    *outs, sums, full, left, right = rest
    size = t0.shape[0]
    side = lax.axis_index("mp") // 2
    left[chunk_start(side, 2 * size), :] = act0[...]
    left[chunk_start(1 - side, 2 * size), :] = act1[...]
    for k, t in enumerate((t0, t1, t2, t3)):
        right[k * size : (k + 1) * size, :] = t[...]
    weight_product(left, right, full)
    emit(full, outs, orders)
    sums[...] = row_sum(right)


def fc1_weight_kernel(orders, rows00, rows01, rows10, rows11, hg0, hg1, *rest):
    *outs, sums, full, left, right = rest
    size = rows00.shape[0]
    for k, rows in enumerate((rows00, rows01, rows10, rows11)):
        left[k * size : (k + 1) * size, :] = rows[...]
    right[: 2 * size, :] = hg0[...]
    right[2 * size :, :] = hg1[...]
    weight_product(left, right, full)
    emit(full, outs, orders)
    sums[...] = row_sum(right)


def attn_weights_kernel(orders, ctx, og0, og1, rows_own, rows_far, pg, *rest):
    *outs, out_sum, qv_sum, full, rows, og = rest
    half = og0.shape[0]
    side = lax.axis_index("mp") // 2
    width = ctx.shape[1]
    rows[chunk_start(side, half), :] = rows_own[...]
    rows[chunk_start(1 - side, half), :] = rows_far[...]
    og[:half, :] = og0[...]
    og[half:, :] = og1[...]

    def part(i):
        full[chunk_start(i, width), :] = dot(pg[i], rows[...], TN)

    repeat(3, part)
    full[3 * width :, :] = dot(ctx[...], og[...], TN)
    emit(full, outs, orders)
    out_sum[...] = row_sum(og)
    qv_sum[...] = jnp.concatenate(
        [jnp.sum(pg[part].astype(F32), axis=0, keepdims=True) for part in (0, 2)], axis=0
    )


def gather_blocks_kernel(orders, low_half, high_half, out):
    blocks = 2 ** len(orders[0])
    size = 2 * low_half.shape[0] // blocks
    here = lax.axis_index("dp")

    def block(b):
        place = place_of(here ^ b, orders)
        at = chunk_start(place % (blocks // 2), size)
        value = jnp.where(place < blocks // 2, low_half[at, :], high_half[at, :])
        out[chunk_start(b, size), :] = value.astype(F32)

    repeat(blocks, block)


def gather_attn_kernel(orders, low_half, high_half, qkv, out_w, full):
    gather_blocks_kernel(orders, low_half, high_half, full)
    rows = qkv.shape[0]
    qkv[...] = full[:rows, :]
    out_w[...] = full[rows:, :]


def input_grad_kernel(x, mine, theirs, after_grad0, after_grad1, vectors, grad, sums):
    side = lax.axis_index("mp") // 2
    normed, inverse = norm(x[...].astype(F32))
    rows_grad = mine[...].astype(F32) + theirs[...].astype(F32)
    sums[...] = jnp.concatenate(
        [
            jnp.sum(rows_grad * normed, axis=0, keepdims=True),
            jnp.sum(rows_grad, axis=0, keepdims=True),
        ],
        axis=0,
    )
    after_grad = jnp.where(side == 0, after_grad0[...], after_grad1[...])
    value = after_grad + norm_back(
        rows_grad, vector(vectors, ATTN_GAIN), normed, inverse
    )
    grad[...] = value.astype(BF)


def text_out_kernel(mine0, mine1, theirs, after0, after1, vectors, out):
    side = lax.axis_index("mp") // 2
    after = jnp.where(side == 0, after0[...], after1[...])
    mine = jnp.where(side == 0, mine0[...], mine1[...])
    branch = mine.astype(F32) + theirs[...].astype(F32)
    out[...] = (after + (branch + vector(vectors, FC2_BIAS))).astype(BF)


def far_branch_kernel(br0, br1, far):
    far[...] = jnp.where(lax.axis_index("mp") // 2 == 0, br1[...], br0[...])


def add_rows_kernel(a, b, out):
    out[...] = a[...] + b[...]


def norm_sums_kernel(mlp0, mlp1, attn, out):
    out[0:2, :] = mlp0[...] + mlp1[...]
    out[2:4, :] = attn[...]


def small_kernel(sums, far, fc2, fc1, out_b, qv, out):
    width = qv.shape[1]
    out[0:2, :] = sums[0:2, :]
    out[2:4, :] = sums[2:4, :] + far[2:4, :]
    out[4:5, :] = fc2[...]
    out[5:6, :] = fc1[...]
    out[6:7, :] = out_b[...]
    out[7:8, :] = jnp.zeros((1, out.shape[1]), F32)
    out[7:8, :width] = qv[0:1, :]
    out[7:8, 2 * width : 3 * width] = qv[1:2, :]


def image_windows(count, images):
    windows = []
    per = 4
    for low in range(0, images, per):
        start = (low * IMG_SEQ + 15) // 16 * 16 if low else 0
        end = min(count, ((low + per) * IMG_SEQ + 15) // 16 * 16)
        if low + per >= images:
            end = count
        key_start = start // IMG_SEQ * IMG_SEQ // 16 * 16
        key_end = min(count, ((end - 1) // IMG_SEQ * IMG_SEQ + IMG_SEQ + 15) // 16 * 16)
        windows.append((start, end, key_start, key_end))
    return windows


def image_attn_kernel(first, last, shards, x, vectors, *rest):
    rest = list(rest)
    before = None if first else rest.pop(0)
    sources, rest = rest[:shards], rest[shards:]
    *outs, total, rows, context, bundle, sems = rest
    count, dim = x.shape
    images = count // IMG_SEQ
    width = dim // 4
    copies = [
        pltpu.make_async_copy(source.at[0 : 4 * width + 16], bundle.at[s], sems.at[s])
        for s, source in enumerate(sources)
    ]
    for copy in copies:
        copy.start()
    normed, _ = norm(x[...].astype(F32))
    rows[...] = (normed * vector(vectors, ATTN_GAIN) + vector(vectors, ATTN_SHIFT)).astype(BF)
    total[...] = jnp.zeros((count, dim), F32) if first else before[...]
    windows = image_windows(count, images)

    def shard(s):
        for k in range(shards):

            @pl.when(s == k)
            def _():
                copies[k].wait()

        weights = bundle.at[s]
        bias = weights[4 * width : 4 * width + 16, :].astype(F32)
        q = (dot(rows[...], weights[:width, :], NT) + bias[0:1, :width]).astype(BF)
        k = dot(rows[...], weights[width : 2 * width, :], NT).astype(BF)
        v = (dot(rows[...], weights[2 * width : 3 * width, :], NT) + bias[1:2, :width]).astype(BF)
        for q_low, q_high, k_low, k_high in windows:
            extent = (q_high - q_low, k_high - k_low)
            q_image = (lax.broadcasted_iota(jnp.int32, extent, 0) + q_low) // IMG_SEQ
            k_image = (lax.broadcasted_iota(jnp.int32, extent, 1) + k_low) // IMG_SEQ
            mask = jnp.where(q_image == k_image, 1.0, 0.0)
            context[q_low:q_high, :] = attend(
                q[q_low:q_high], k[k_low:k_high], v[k_low:k_high], mask
            )

        def columns(i):
            cols = lanes(i, 256)
            total[:, cols] += dot(context[...], bundle[s, 3 * width : 4 * width, cols])

        repeat(dim // 256, columns)

    repeat(shards, shard)
    if not last:
        outs[0][...] = total[...]
        return
    after_ref, rows_ref = outs
    after = x[...].astype(F32) + (total[...] + vector(vectors, OUT_BIAS))
    after_ref[...] = after
    normed, _ = norm(after)
    rows_ref[...] = (normed * vector(vectors, MLP_GAIN) + vector(vectors, MLP_SHIFT)).astype(BF)


def image_mlp_kernel(r0, r1, r2, r3, w1, vectors, w2, p0, p1, p2, p3, rows, active):
    size, dim = r0.shape
    for k, r in enumerate((r3, r1, r2, r0)):
        rows[k * size : (k + 1) * size, :] = r[...]

    def units(i):
        cols = lanes(i, 256)
        hidden = dot(rows[...], w1[:, cols]) + vectors[FC1_BIAS : FC1_BIAS + 1, cols]
        active[:, cols] = gelu_parts(hidden)[0].astype(BF)

    def columns(i):
        cols = lanes(i, 256)
        value = dot(active[...], w2[:, cols]).astype(BF)
        for k, p in enumerate((p3, p1, p2, p0)):
            p[:, cols] = value[k * size : (k + 1) * size]

    repeat(w1.shape[1] // 256, units)
    repeat(dim // 256, columns)


def image_out_kernel(after, mine, theirs, vectors, out):
    branch = mine[...].astype(F32) + theirs[...].astype(F32)
    out[...] = (after[...] + (branch + vector(vectors, FC2_BIAS))).astype(BF)


def core_swap(x):
    return lax.ppermute(x, "mp", [(i, i ^ 1) for i in range(lax.axis_size("mp"))])


def side_swap(x):
    return lax.ppermute(x, "mp", [(i, i ^ 2) for i in range(lax.axis_size("mp"))])


def dp_swap(x, bits):
    n_dp, n_mp = lax.axis_size("dp"), lax.axis_size("mp")
    pairs = [
        (d * n_mp + m, (d ^ bits[m % 2]) * n_mp + m) for d in range(n_dp) for m in range(n_mp)
    ]
    return lax.ppermute(x, ("dp", "mp"), pairs)


def per_device(
    text_in,
    segment_ids,
    valid_lengths,
    text_grad,
    attn_gain,
    attn_shift,
    qkv_weight,
    qv_bias,
    out_weight,
    out_bias,
    mlp_gain,
    mlp_shift,
    fc1_weight,
    fc1_bias,
    fc2_weight,
    fc2_bias,
    images,
    img_attn_gain,
    img_attn_shift,
    img_qkv_weight,
    img_qv_bias,
    img_out_weight,
    img_out_bias,
    img_mlp_gain,
    img_mlp_shift,
    img_fc1_weight,
    img_fc1_bias,
    img_fc2_weight,
    img_fc2_bias,
):
    size, dim = text_in.shape
    row_count, length = segment_ids.shape
    width = qkv_weight.shape[2]
    n_dp = lax.axis_size("dp")
    tokens = 4 * size

    w_t = qkv_weight.transpose(1, 2, 0).reshape(3 * width, dim)
    img_w_t = img_qkv_weight.transpose(1, 2, 0).reshape(3 * width, dim)
    used = 4 * width + 16
    total_rows = -(-used // (16 * n_dp)) * 16 * n_dp
    part_rows = total_rows // n_dp

    rows_first = 2 * size // length
    blocks = row_blocks(row_count, length, rows_first)
    blocks_first = [b for b in blocks if b[0] < rows_first * length]
    blocks_rest = [b for b in blocks if b[0] >= rows_first * length]

    run = Line()
    chunk = shape(size, dim)
    pair = shape(2 * size, dim)

    x0 = text_in
    x2 = side_swap(x0)
    x1 = core_swap(x0)
    vectors, img_vectors = run(
        vectors_kernel,
        [shape(8, dim, dtype=F32)] * 2,
        [
            attn_gain, attn_shift, out_bias, mlp_gain, mlp_shift, fc2_bias, fc1_bias,
            img_attn_gain, img_attn_shift, img_out_bias, img_mlp_gain, img_mlp_shift,
            img_fc2_bias, img_fc1_bias,
        ],
    )
    project_scratch = [pltpu.VMEM((2, size, dim), BF), pltpu.VMEM((8, width), F32)]
    rows_own, qkv_own = run(
        own_rows_kernel,
        [pair, shape(3, 2 * size, width)],
        [x0, x1, vectors, w_t, qv_bias],
        scratch=project_scratch,
    )
    mask = run(
        functools.partial(mask_kernel, blocks),
        [shape(tokens, 2 * length, dtype=F32)],
        [segment_ids, valid_lengths],
        scalars=(1,),
    )
    bundle = run(
        bundle_kernel,
        [shape(total_rows, dim)],
        [img_w_t, img_out_weight, img_qv_bias],
        scratch=[
            pltpu.VMEM((total_rows - 4 * width, dim), BF),
            pltpu.SemaphoreType.DMA((3,)),
        ],
        untouched=(0, 1),
        outside=True,
    )
    t1 = core_swap(text_grad)
    own_other = core_swap(bundle)
    image_rows = images.shape[0]

    def image_attn(first, last, operands, outs, sources):
        args = [images, img_vectors, *operands, *sources]
        shards = len(sources)
        return run(
            functools.partial(image_attn_kernel, first, last, shards),
            outs,
            args,
            scratch=[
                pltpu.VMEM((image_rows, dim), F32),
                pltpu.VMEM((image_rows, dim), BF),
                pltpu.VMEM((image_rows, width), BF),
                pltpu.VMEM((shards, used, dim), BF),
                pltpu.SemaphoreType.DMA((shards,)),
            ],
            untouched=tuple(range(len(args) - shards, len(args))),
        )

    image_wide = shape(image_rows, dim, dtype=F32)
    image_total = image_attn(True, False, [], [image_wide], [bundle])
    t0 = text_grad
    packed = run(
        far_operands_kernel,
        [shape(size + part_rows, dim)],
        [t0, bundle],
        scratch=[pltpu.SemaphoreType.DMA(())],
        untouched=(1,),
        after=[x2],
    )
    x2 = run.hold(x2)
    x3 = core_swap(x2)
    packed = side_swap(packed)

    rows_far, qkv, ctx, keep0, keep1, send0, send1 = run(
        functools.partial(attn_forward_kernel, blocks),
        [pair, shape(3, tokens, width), shape(tokens, width)] + [chunk] * 4,
        [x2, x3, qkv_own, vectors, w_t, qv_bias, out_weight, mask],
        scratch=project_scratch,
    )

    def after_attn(half, mine, theirs):
        stream, rows = run(
            functools.partial(after_attn_kernel, half),
            [shape(size, dim, dtype=F32), chunk],
            [x0, x2, mine, theirs, vectors],
        )
        return stream, rows, core_swap(rows)

    def mlp(half, rows, rows_other):
        return run(
            functools.partial(mlp_kernel, half),
            [pair] * 2 + [chunk] * 4,
            [rows, rows_other, t0, t1, t2, t3, fc1_weight, vectors, fc2_weight],
            scratch=[pltpu.VMEM((2 * size, dim), BF)] * 2,
        )

    def mlp_back(half, stream, mine, theirs):
        value, low, sums = run(
            functools.partial(mlp_back_kernel, half),
            [shape(size, dim, dtype=F32), chunk, shape(2, dim, dtype=F32)],
            [stream, mine, theirs, t0, t2, vectors],
        )
        return value, low, core_swap(low), sums

    other0, other1 = core_swap(send0), core_swap(send1)
    mine0 = run(add_kernel, [chunk], [keep0, other0], after=[packed])
    theirs0 = side_swap(mine0)
    t2, far_part = run(unpack_kernel, [chunk, shape(part_rows, dim)], [packed])
    t3 = core_swap(t2)
    far_bundle = lax.all_gather(far_part, "dp", axis=0, tiled=True)
    image_total = image_attn(False, False, [image_total], [image_wide], [own_other])
    mine1 = run(add_kernel, [chunk], [keep1, other1], after=[theirs0])
    theirs1 = side_swap(mine1)
    stream0, rows0, rows_other0 = after_attn(0, mine0, theirs0)
    act0, hg0, brk0, brs0, mgk0, mgs0 = mlp(0, rows0, rows_other0)
    mg0, br0 = run(
        add_pair_kernel,
        [chunk] * 2,
        [mgk0, core_swap(mgs0), brk0, core_swap(brs0)],
        after=[theirs1],
    )
    mg_theirs0 = side_swap(mg0)
    stream1, rows1, rows_other1 = after_attn(1, mine1, theirs1)
    act1, hg1, brk1, brs1, mgk1, mgs1 = mlp(1, rows1, rows_other1)
    mg1, br1 = run(
        add_pair_kernel,
        [chunk] * 2,
        [mgk1, core_swap(mgs1), brk1, core_swap(brs1)],
        after=[mg_theirs0],
    )
    mg_theirs1 = side_swap(mg1)
    after_grad0, og0, og_other0, mlp_sums0 = mlp_back(0, stream0, mg0, mg_theirs0)

    bits = [2**k for k in range(n_dp.bit_length() - 1)]
    orders = (tuple(bits), tuple(bits[1:] + bits[:1]))
    plain = 2 ** len(bits) != n_dp or dim % (16 * n_dp) != 0
    if plain:
        orders = None
    grad_shapes = [shape(dim, dim, dtype=F32)] if plain else [shape(dim // 2, dim)] * 2

    class Sum:
        def __init__(self, parts, last, sizes):
            self.last, self.sizes, self.step = last, sizes, 0
            if plain:
                total = lax.psum(parts[0], "dp")
                cuts = [sum(sizes[: i + 1]) for i in range(len(sizes) - 1)]
                self.result = jnp.split(total, cuts, axis=0)
                return
            self.keep = parts[0]
            self.exchange(parts[1], 0)

        def exchange(self, send, k):
            self.arriving = dp_swap(send, (orders[0][k], orders[1][k]))

        def advance(self):
            if plain:
                return
            self.step += 1
            rows, levels = self.keep.shape[0], len(bits)
            if self.step < levels:
                self.keep, send = run(
                    add_split_kernel, [shape(rows // 2, dim)] * 2, [self.keep, self.arriving]
                )
                self.exchange(send, self.step)
            elif self.step < 2 * levels:
                if self.step == levels:
                    self.keep = run(add_kernel, [shape(rows, dim)], [self.keep, self.arriving])
                else:
                    self.keep = run(
                        join_kernel, [shape(2 * rows, dim)], [self.keep, self.arriving]
                    )
                self.exchange(self.keep, 2 * levels - 1 - self.step)
            else:
                got = run(
                    functools.partial(self.last, orders),
                    [shape(n, dim, dtype=F32) for n in self.sizes],
                    [self.keep, self.arriving],
                    scratch=[pltpu.VMEM((dim, dim), F32)] if len(self.sizes) > 1 else [],
                )
                self.result = got if len(self.sizes) > 1 else [got]

    def fc_weight(kernel, args):
        *parts, sums = run(
            functools.partial(kernel, orders),
            grad_shapes + [shape(1, dim, dtype=F32)],
            args,
            scratch=[pltpu.VMEM((dim, dim), F32)] + [pltpu.VMEM((tokens, dim), BF)] * 2,
        )
        return Sum(parts, gather_blocks_kernel, (dim,)), sums

    fc2_sum, fc2_bias_sum = fc_weight(fc2_weight_kernel, [act0, act1, t0, t1, t2, t3])

    og_first, cg_first, pg_first = run(
        functools.partial(attn_back_first_kernel, blocks_first),
        [pair, shape(2 * size, width), shape(3, rows_first * length, width)],
        [og0, og_other0, qkv, mask, out_weight],
    )
    fc1_sum, fc1_bias_sum = fc_weight(
        fc1_weight_kernel, [rows0, rows_other0, rows1, rows_other1, hg0, hg1]
    )
    after_grad1, og1, og_other1, mlp_sums1 = mlp_back(1, stream1, mg1, mg_theirs1)
    fc2_sum.advance()
    og_second, pg, p0, p1, p2, p3 = run(
        functools.partial(attn_back_second_kernel, blocks_rest),
        [pair, shape(3, tokens, width)] + [chunk] * 4,
        [og1, og_other1, cg_first, pg_first, qkv, mask, out_weight, w_t],
        scratch=[pltpu.VMEM((tokens, width), BF)],
    )
    p_other1, p_other3 = core_swap(p1), core_swap(p3)
    *parts, out_sum, qv_sum = run(
        functools.partial(attn_weights_kernel, orders),
        grad_shapes + [shape(1, dim, dtype=F32), shape(2, width, dtype=F32)],
        [ctx, og_first, og_second, rows_own, rows_far, pg],
        scratch=[pltpu.VMEM((dim, dim), F32)] + [pltpu.VMEM((tokens, dim), BF)] * 2,
    )
    attn_sum = Sum(parts, gather_attn_kernel, (3 * width, width))
    p_mine, to_side = run(add_pair_kernel, [chunk] * 2, [p0, p_other1, p2, p_other3])
    p_theirs = side_swap(to_side)
    fc1_sum.advance()
    fc2_sum.advance()

    far_bundle = run.hold(far_bundle)
    far_other = core_swap(far_bundle)
    attn_sum.advance()
    image_chunk = shape(image_rows, dim)
    img_after, img_rows0 = image_attn(
        False, True, [image_total], [image_wide, image_chunk], [far_bundle, far_other]
    )
    img_rows2 = side_swap(img_rows0)
    img_rows1 = core_swap(img_rows0)
    fc1_sum.advance()
    fc2_sum.advance()
    text_in_grad, attn_sums = run(
        input_grad_kernel,
        [chunk, shape(2, dim, dtype=F32)],
        [text_in, p_mine, p_theirs, after_grad0, after_grad1, vectors],
    )
    small = run(norm_sums_kernel, [shape(4, dim, dtype=F32)], [mlp_sums0, mlp_sums1, attn_sums])
    attn_sum.advance()
    small = run(add_rows_kernel, [shape(4, dim, dtype=F32)], [small, core_swap(small)])
    small_far = side_swap(small)
    fc1_sum.advance()
    fc2_sum.advance()
    img_rows2 = run.hold(img_rows2)
    img_rows3 = core_swap(img_rows2)
    attn_sum.advance()
    i0, i1, i2, i3 = run(
        image_mlp_kernel,
        [image_chunk] * 4,
        [img_rows0, img_rows1, img_rows2, img_rows3, img_fc1_weight, img_vectors, img_fc2_weight],
        scratch=[pltpu.VMEM((4 * image_rows, dim), BF)] * 2,
        vmem=24,
    )
    i_mine, i_side = run(
        add_pair_kernel, [image_chunk] * 2, [i0, core_swap(i1), i2, core_swap(i3)]
    )
    i_theirs = side_swap(i_side)
    small = run(
        small_kernel,
        [shape(8, dim, dtype=F32)],
        [small, small_far, fc2_bias_sum, fc1_bias_sum, out_sum, qv_sum],
    )
    if plain:
        small_far = lax.psum(small, "dp")
        small = jnp.zeros_like(small)
    else:
        small_far = dp_swap(small, (bits[0], bits[0]))
    fc1_sum.advance()
    fc2_sum.advance()
    attn_sum.advance()
    if not plain:
        for bit in bits[1:]:
            small = run(add_rows_kernel, [shape(8, dim, dtype=F32)], [small, small_far])
            small_far = dp_swap(small, (bit, bit))
    image_out = run(
        image_out_kernel, [image_chunk], [img_after, i_mine, i_theirs, img_vectors]
    )
    far_branch = run(far_branch_kernel, [chunk], [br0, br1])
    br_theirs = side_swap(far_branch)
    fc1_sum.advance()
    fc2_sum.advance()
    attn_sum.advance()
    text_out = run(
        text_out_kernel,
        [chunk],
        [br0, br1, br_theirs, stream0, stream1, vectors],
    )
    for total in (fc2_sum, fc1_sum, attn_sum):
        while not plain and total.step < 2 * len(bits):
            total.advance()
    small = run(add_rows_kernel, [shape(8, dim, dtype=F32)], [small, small_far])
    (grad_fc2_weight,) = fc2_sum.result
    (grad_fc1_weight,) = fc1_sum.result
    grad_qkv, grad_out_weight = attn_sum.result
    return (
        text_out,
        image_out,
        text_in_grad,
        small[2],
        small[3],
        grad_qkv.reshape(3, width, dim).transpose(2, 0, 1),
        jnp.stack([small[7, :width], small[7, 2 * width : 3 * width]]),
        grad_out_weight,
        small[6],
        small[0],
        small[1],
        grad_fc1_weight,
        small[5],
        grad_fc2_weight,
        small[4],
    )


def solution(mesh):
    in_specs = (
        P(("dp", "mp"), None),
        P("dp", None),
        P("dp"),
        P(("dp", "mp"), None),
        P(),
        P(),
        P(None, None, "mp"),
        P(None, "mp"),
        P("mp", None),
        P(),
        P(),
        P(),
        P(None, "mp"),
        P("mp"),
        P("mp", None),
        P(),
        P(("dp", "mp"), None),
        P(),
        P(),
        P(None, None, "mp"),
        P(None, "mp"),
        P("mp", None),
        P(),
        P(),
        P(),
        P(None, "mp"),
        P("mp"),
        P("mp", None),
        P(),
    )
    out_specs = (
        P(("dp", "mp"), None),
        P(("dp", "mp"), None),
        P(("dp", "mp"), None),
        P(),
        P(),
        P(None, None, "mp"),
        P(None, "mp"),
        P("mp", None),
        P(),
        P(),
        P(),
        P(None, "mp"),
        P("mp"),
        P("mp", None),
        P(),
    )
    return jax.shard_map(
        per_device, mesh=mesh, in_specs=in_specs, out_specs=out_specs, check_vma=False
    )
```

```python
import functools

import jax
import jax.numpy as jnp
from jax import lax
from jax.experimental import pallas as pl
from jax.experimental.pallas import tpu as pltpu
from jax.sharding import PartitionSpec as P

HEAD = 64
IMG_SEQ = 50
EPS = 1e-05
BF = jnp.bfloat16
F32 = jnp.float32
SCALE = HEAD ** (-0.5)
NEG = -1000000000.0
ROOT = 0.7978845608028654
CUBE = 0.044715

NN = (((1,), (0,)), ((), ()))
NT = (((1,), (1,)), ((), ()))
TN = (((0,), (0,)), ((), ()))


def dot(a, b, dims=NN):
    return lax.dot_general(a, b, dims, preferred_element_type=F32)


def shape(*dims, dtype=BF):
    return jax.ShapeDtypeStruct(dims, dtype)


class Late:
    def __init__(self, value):
        self.value, self.shape, self.dtype = value, value.shape, value.dtype


class Fixed:
    def __init__(self, value):
        self.value, self.shape, self.dtype = value, value.shape, value.dtype


class Early:
    def __init__(self, *dims, dtype=BF):
        self.shape, self.dtype = dims, dtype


class Moving:
    def __init__(self, source, target, held, sem):
        self.held, self.shape = held, held.shape
        self.copy = pltpu.make_async_copy(source, target, sem)
        self.waits = False

    def start(self):
        self.copy.start()
        self.waits = True

    def get(self):
        if self.waits:
            self.copy.wait()
            self.waits = False
        return self.held


class Line:
    def __init__(self):
        self.token = None

    def __call__(self, body, outs, args, scratch=(), vmem=16, untouched=(), scalars=(), after=(),
                 same=None, outside=False):
        def place(a):
            if isinstance(a, (Late, Fixed)):
                return pltpu.with_memory_space_constraint(a.value, pltpu.HBM)
            return a

        kinds = list(args)
        real = len(kinds)
        values = [place(a) for a in kinds + list(after)]
        values += [] if self.token is None else [self.token]
        given = len(values)
        late = [i for i, a in enumerate(kinds) if isinstance(a, Late)]
        fixed = [i for i, a in enumerate(kinds) if isinstance(a, Fixed)]
        early = [i for i, o in enumerate(outs) if isinstance(o, Early)]

        def in_space(i):
            if i >= real or i in untouched:
                return pl.ANY
            if i in late or i in fixed:
                return pltpu.HBM
            return pltpu.SMEM if i in scalars else pltpu.VMEM

        def out_space(i):
            if outside or same is not None:
                return pl.ANY
            return pltpu.HBM if i in early else pltpu.VMEM

        moving = [kinds[i] for i in late] + [outs[i] for i in early]
        held = [pltpu.VMEM(m.shape, m.dtype) for m in moving]
        sems = [pltpu.SemaphoreType.DMA((len(held),))] if held else []
        first = given + len(outs) + 1

        def run(*refs):
            ins, results = list(refs[:real]), list(refs[given : given + len(outs)])
            places = refs[first : first + len(held)]
            for k, i in enumerate(late):
                ins[i] = Moving(ins[i], places[k], places[k], refs[-1].at[k])
                ins[i].start()
            for k, i in enumerate(early, len(late)):
                results[i] = Moving(places[k], results[i], places[k], refs[-1].at[k])
            body(*ins, *results, *refs[first + len(held) : len(refs) - len(sems)])
            for moved in [ins[i] for i in late] + [results[i] for i in early]:
                moved.get()

        results = pl.pallas_call(
            run,
            out_shape=(
                *(
                    pltpu.HBM(o.shape, o.dtype)
                    if i in early
                    else jax.ShapeDtypeStruct(o.shape, o.dtype)
                    for i, o in enumerate(outs)
                ),
                shape(8, 128, dtype=F32),
            ),
            in_specs=[pl.BlockSpec(memory_space=in_space(i)) for i in range(given)],
            out_specs=tuple(
                [pl.BlockSpec(memory_space=out_space(i)) for i in range(len(outs))]
                + [pl.BlockSpec(memory_space=pl.ANY)]
            ),
            scratch_shapes=held + list(scratch) + sems,
            input_output_aliases={} if same is None else {same: 0},
            compiler_params=pltpu.CompilerParams(vmem_limit_bytes=vmem * 1024 * 1024),
            cost_estimate=pl.CostEstimate(flops=1, bytes_accessed=1, transcendentals=0),
        )(*values)
        self.token = results[-1]
        return results[:-1] if len(outs) > 1 else results[0]

    def hold(self, value, after=()):
        return self(lambda *refs: None, [shape(*value.shape, dtype=value.dtype)], [value],
                    untouched=(0,), same=0, after=after)


def norm(x):
    centred = x - jnp.mean(x, axis=-1, keepdims=True)
    inverse = lax.rsqrt(jnp.mean(centred * centred, axis=-1, keepdims=True) + EPS)
    return centred * inverse, inverse


def norm_back(upstream, gain, normed, inverse):
    scaled = upstream * gain
    first = jnp.mean(scaled, axis=-1, keepdims=True)
    second = jnp.mean(scaled * normed, axis=-1, keepdims=True)
    return inverse * (scaled - first - normed * second)


def head_marks(width, dtype):
    lane = lax.broadcasted_iota(jnp.int32, (1, width), 1) // HEAD
    return [jnp.where(lane == h, 1.0, 0.0).astype(dtype) for h in range(width // HEAD)]


def stack_heads(rows, marks):
    return jnp.concatenate([rows * mark for mark in marks], axis=0)


def fold_heads(stacked, count, marks):
    total = stacked[:count] * marks[0]
    for h in range(1, len(marks)):
        total += stacked[h * count : (h + 1) * count] * marks[h]
    return total


def masked_scores(q_stack, k, mask):
    raw = dot(q_stack, k, NT)
    heads = raw.shape[0] // mask.shape[0]
    raw = raw.reshape(heads, mask.shape[0], mask.shape[1])
    return jnp.where(mask[None] > 0, raw * SCALE, NEG)


def softmax_parts(scores):
    peak = jnp.max(scores, axis=-1, keepdims=True)
    weights = jnp.exp(scores - peak)
    return weights, jnp.sum(weights, axis=-1, keepdims=True)


def attend(q, k, v, mask):
    count = q.shape[0]
    scores = masked_scores(stack_heads(q, head_marks(q.shape[1], BF)), k, mask)
    weights, total = softmax_parts(scores)
    probs = (weights / total).astype(BF).reshape(-1, mask.shape[1])
    return fold_heads(dot(probs, v), count, head_marks(q.shape[1], F32)).astype(BF)


def attend_back(q, k, v, grad, mask):
    count = q.shape[0]
    low = head_marks(q.shape[1], BF)
    q_stack = stack_heads(q, low)
    g_stack = stack_heads(grad, low)
    weights, total = softmax_parts(masked_scores(q_stack, k, mask))
    probs = weights / total
    prob_grad = dot(g_stack, v, NT).reshape(probs.shape)
    centre = jnp.sum(prob_grad * probs, axis=-1, keepdims=True)
    score_grad = (probs * (prob_grad - centre)).astype(BF).reshape(-1, mask.shape[1])
    probs_low = probs.astype(BF).reshape(-1, mask.shape[1])
    v_grad = dot(probs_low, g_stack, TN)
    q_grad = fold_heads(dot(score_grad, k), count, head_marks(q.shape[1], F32)) * SCALE
    k_grad = dot(score_grad, q_stack, TN) * SCALE
    return q_grad.astype(BF), k_grad.astype(BF), v_grad.astype(BF)


def gelu_parts(v):
    square = v * v
    t = jnp.tanh(ROOT * (v + CUBE * (square * v)))
    half = 0.5 * (1.0 + t)
    slope = half + 0.5 * v * (1.0 - t * t) * (ROOT * (1.0 + 3.0 * CUBE * square))
    return v * half, slope


def repeat(count, body):
    def step(i, carry):
        body(i)
        return carry

    lax.fori_loop(0, count, step, 0)


def lanes(index, size):
    return pl.ds(pl.multiple_of(index * size, 128), size)


def pieces_of(count, parts):
    most = -(-count // (16 * parts)) * 16
    return [min(most, count - low) for low in range(0, count, most)]


def put_pieces(value, outs):
    low = 0
    for out in outs:
        out[...] = value[low : low + out.shape[0]]
        low += out.shape[0]


def join_pieces(refs):
    return jnp.concatenate([ref[...] for ref in refs], axis=0)


def chunk_start(index, size):
    return pl.ds(pl.multiple_of(index * size, 16), size)


def row_blocks(count, length, first):
    blocks = []
    for low, high in ((0, first), (first, count)):
        row = low
        if (high - low) % 2:
            blocks.append((row * length, length))
            row += 1
        while row < high:
            blocks.append((row * length, 2 * length))
            row += 2
    return blocks


def mask_kernel(blocks, segments, lengths, mask):
    length = segments.shape[1]
    square = (length, length)
    key = lax.broadcasted_iota(jnp.int32, square, 1)
    diagonal = key == lax.broadcasted_iota(jnp.int32, square, 0)
    mask[...] = jnp.zeros(mask.shape, F32)
    for start, count in blocks:
        for place in range(count // length):
            row = start // length + place
            along = jnp.broadcast_to(segments[row : row + 1, :].astype(F32), square)
            seen = (along == along.T) & ((key < lengths[row]) | diagonal)
            low = start + place * length
            mask[low : low + length, place * length : (place + 1) * length] = jnp.where(
                seen, 1.0, 0.0
            )


def bundle_kernel(w_t, out_w, qv, bundle, held, sems):
    width = qv.shape[1]
    held[...] = jnp.zeros(held.shape, held.dtype)
    held[0:2, :width] = qv[...]
    start, copies = 0, []
    for k, piece in enumerate((w_t, out_w, held)):
        rows = piece.shape[0]
        copies.append(pltpu.make_async_copy(piece, bundle.at[start : start + rows], sems.at[k]))
        copies[-1].start()
        start += rows
    for copy in copies:
        copy.wait()


ATTN_GAIN, ATTN_SHIFT, OUT_BIAS, MLP_GAIN, MLP_SHIFT, FC2_BIAS, FC1_BIAS = range(7)


def vectors_kernel(*refs):
    *items, text, image = refs
    for out, own in ((text, items[: len(items) // 2]), (image, items[len(items) // 2 :])):
        out[...] = jnp.zeros(out.shape, F32)
        for k, item in enumerate(own):
            out[k : k + 1, :] = item.get()[...].astype(F32).reshape(1, -1)


def vector(vectors, index):
    return vectors[index : index + 1, :]


def project(x_pair, vectors, w_t, bias, rows_out, qkv, bias_rows, at):
    size = x_pair.shape[1]
    width = bias.shape[1]
    gain, shift = vector(vectors, ATTN_GAIN), vector(vectors, ATTN_SHIFT)
    bias_rows[...] = jnp.zeros(bias_rows.shape, F32)
    bias_rows[0:1, :] = bias[...].astype(F32)[0:1]
    bias_rows[2:3, :] = bias[...].astype(F32)[1:2]

    def normalize(i):
        normed, _ = norm(x_pair[i].astype(F32))
        rows[chunk_start(i, size), :] = (normed * gain + shift).astype(BF)

    def part(i):
        value = dot(rows[...], w_t[chunk_start(i, width), :], NT) + bias_rows[pl.ds(i, 1), :]
        qkv[i, at, :] = value.astype(BF)

    rows = rows_out.held
    repeat(2, normalize)
    rows_out.start()
    repeat(3, part)


def own_rows_kernel(x0, x1, vectors, w_t, bias, rows_out, qkv, x_pair, bias_rows):
    core = lax.axis_index("mp") % 2
    x_pair[core] = x0[...]
    x_pair[1 - core] = x1[...]
    project(x_pair, vectors, w_t, bias, rows_out, qkv, bias_rows, slice(None))


def far_operands_kernel(grad, bundle, packed, sem):
    size = grad.shape[0]
    part = packed.shape[0] - size
    copy = pltpu.make_async_copy(
        bundle.at[chunk_start(lax.axis_index("dp"), part)], packed.at[size:], sem
    )
    copy.start()
    packed[:size] = grad[...]
    copy.wait()


def unpack_kernel(packed, part):
    part[...] = packed[packed.shape[0] - part.shape[0] :]


def arrange_kernel(t0, t1, packed, packed_other, half0, half1):
    size = t0.shape[0]
    here = lax.axis_index("mp") // 2 == 0
    parts = ((slice(0, size), t0, packed), (slice(size, 2 * size), t1, packed_other))
    for at, own, far in parts:
        half0.held[at, :] = jnp.where(here, own[...], far[:size])
        half1.held[at, :] = jnp.where(here, far[:size], own[...])
    half0.start()
    half1.start()


def block_loop(blocks, body, unroll=False):
    if unroll:
        for start, tokens in blocks:
            body(pl.ds(start, tokens), tokens)
        return
    singles = [b for b in blocks if b[1] != blocks[-1][1]]
    pairs = [b[0] for b in blocks if b[1] == blocks[-1][1]]
    count = blocks[-1][1]
    for start, tokens in singles:
        body(pl.ds(start, tokens), tokens)

    def pair(i):
        start = pairs[0] + i * count
        for k in range(1, len(pairs)):
            gap = pairs[k] - pairs[k - 1] - count
            if gap:
                start = start + jnp.where(i >= k, gap, 0)
        body(pl.ds(pl.multiple_of(start, 16), count), count)

    repeat(len(pairs), pair)


def attn_forward_kernel(blocks, x0, x2, x3, qkv_own, vectors, w_t, bias, out_w, mask,
                        rows_out, qkv_out, ctx_out, x_mine, keep0, keep1, send0, send1,
                        x_pair, bias_rows):
    qkv, ctx = qkv_out.held, ctx_out.held
    me = lax.axis_index("mp")
    core, side = me % 2, me // 2
    size, dim = x2.shape
    x_pair[core] = x2[...]
    x_pair[1 - core] = x3[...]
    x_mine.held[side] = x0[...]
    x_mine.held[1 - side] = x2[...]
    x_mine.start()
    far = chunk_start(1 - side, 2 * size)
    project(x_pair, vectors, w_t, bias, rows_out, qkv, bias_rows, far)
    own = chunk_start(side, 2 * size)
    for part in range(3):
        qkv[part, own, :] = qkv_own[part]
    qkv_out.start()

    def block(at, count):
        ctx[at, :] = attend(qkv[0, at, :], qkv[1, at, :], qkv[2, at, :], mask[at, :count])

    block_loop(blocks, block, unroll=True)
    ctx_out.start()

    def columns(i):
        cols = lanes(i, 256)
        weight = out_w[:, cols]
        for half, (keep, send) in enumerate(((keep0, send0), (keep1, send1))):
            theirs = ctx[chunk_start(2 * half + 1 - core, size), :]
            send[:, cols] = dot(theirs, weight).astype(BF)
            mine = ctx[chunk_start(2 * half + core, size), :]
            keep[:, cols] = dot(mine, weight).astype(BF)

    repeat(dim // 256, columns)


def add_kernel(a, b, out):
    out[...] = (a[...].astype(F32) + b[...].astype(F32)).astype(BF)


def add_pieces_kernel(a, *rest):
    *pieces, out = rest
    out[...] = (a[...].astype(F32) + join_pieces(pieces).astype(F32)).astype(BF)


def branch_sums_kernel(keep0, other0, keep1, other1, mine0, mine1):
    for keep, other, mine in ((keep0, other0, mine0), (keep1, other1, mine1)):
        mine.held[...] = (keep[...].astype(F32) + other[...].astype(F32)).astype(BF)
        mine.start()


def add_pair_kernel(a0, b0, a1, b1, out0, out1):
    for a, b, out in ((a0, b0, out0), (a1, b1, out1)):
        out[...] = (a[...].astype(F32) + b[...].astype(F32)).astype(BF)


def add_split_kernel(a, b, keep, send):
    half = keep.shape[0]
    keep[...] = (a[:half].astype(F32) + b[:half].astype(F32)).astype(BF)
    send[...] = (a[half:].astype(F32) + b[half:].astype(F32)).astype(BF)


def join_kernel(a, b, out):
    half = a.shape[0]
    out[:half] = a[...]
    out[half:] = b[...]


def after_attn_kernel(half, x_mine, mine, theirs, vectors, after_out, rows, *pieces):
    total = mine[...].astype(F32) + theirs[...].astype(F32)
    stream = x_mine[half].astype(F32) + (total + vector(vectors, OUT_BIAS))
    after_out.held[...] = stream
    after_out.start()
    normed, _ = norm(stream)
    value = (normed * vector(vectors, MLP_GAIN) + vector(vectors, MLP_SHIFT)).astype(BF)
    rows[...] = value
    put_pieces(value, pieces)


def mlp_kernel(count, rows0, *rest):
    pieces, (grad, w1, vectors, w2), rest = rest[:count], rest[count : count + 4], rest[count + 4 :]
    rows_out, act_out, hg_out, br_keep, br_send, mg_keep, *mg_sends = rest
    size, dim = rows0.shape
    rows, act, hid_grad = rows_out.held, act_out.held, hg_out.held
    rows[:size, :] = rows0[...]
    rows[size:, :] = join_pieces(pieces)
    rows_out.start()
    grad = grad

    def units(i):
        cols = lanes(i, 256)
        hidden = dot(rows[...], w1[:, cols]) + vectors[FC1_BIAS : FC1_BIAS + 1, cols]
        active, slope = gelu_parts(hidden)
        act[:, cols] = active.astype(BF)
        active_grad = dot(grad[...], w2[cols, :], NT)
        hid_grad[:, cols] = (active_grad * slope).astype(BF)

    def columns(i):
        cols = lanes(i, 256)
        value = dot(hid_grad[...], w1[cols, :], NT).astype(BF)
        mg_keep[:, cols] = value[:size]
        low = size
        for send in mg_sends:
            send[:, cols] = value[low : low + send.shape[0]]
            low += send.shape[0]

    def branch_columns(i):
        cols = lanes(i, 256)
        value = dot(act[...], w2[:, cols]).astype(BF)
        br_keep.held[:, cols] = value[:size]
        br_send.held[:, cols] = value[size:]

    repeat(w1.shape[1] // 256, units)
    act_out.start()
    hg_out.start()
    repeat(dim // 256, branch_columns)
    br_keep.start()
    br_send.start()
    repeat(dim // 256, columns)


def mlp_back_kernel(after, mine, theirs, grad, vectors, ag_out, out_grad, sums, *pieces):
    size = mine.shape[0]
    rows_grad = mine[...].astype(F32) + theirs[...].astype(F32)
    normed, inverse = norm(after[...])
    sums[...] = jnp.concatenate(
        [
            jnp.sum(rows_grad * normed, axis=0, keepdims=True),
            jnp.sum(rows_grad, axis=0, keepdims=True),
        ],
        axis=0,
    )
    value = grad[:size, :].astype(F32) + norm_back(
        rows_grad, vector(vectors, MLP_GAIN), normed, inverse
    )
    ag_out.held[...] = value
    ag_out.start()
    low = value.astype(BF)
    out_grad[...] = low
    put_pieces(low, pieces)


def attn_back_first_kernel(blocks, count, og_mine, *rest):
    og_others, (qkv, mask, out_w, og, cg, pg) = rest[:count], rest[count:]
    core = lax.axis_index("mp") % 2
    size = og_mine.shape[0]
    og[chunk_start(core, size), :] = og_mine[...]
    og[chunk_start(1 - core, size), :] = join_pieces(og_others)
    cg[...] = dot(og[...], out_w[...], NT).astype(BF)
    qkv = qkv

    def block(at, count):
        grads = attend_back(
            qkv[0, at, :], qkv[1, at, :], qkv[2, at, :], cg[at, :], mask[at, :count]
        )
        for part in range(3):
            pg[part, at, :] = grads[part]

    block_loop(blocks, block)


def attn_back_second_kernel(blocks, count, og_mine, *rest):
    og_others, rest = rest[:count], rest[count:]
    cg_first, pg_first, qkv, mask, out_w, w_t, og, pg, p0, p1, p2, p3, cg = rest
    me = lax.axis_index("mp")
    core = me % 2
    size, dim = og_mine.shape
    width = out_w.shape[0]
    half = 2 * size
    done = pg_first.shape[1]
    og[chunk_start(core, size), :] = og_mine[...]
    og[chunk_start(1 - core, size), :] = join_pieces(og_others)
    cg[half:, :] = dot(og[...], out_w[...], NT).astype(BF)
    cg[:half, :] = cg_first[...]
    qkv = qkv
    for part in range(3):
        pg[part, :done, :] = pg_first[part]

    def block(at, count):
        grads = attend_back(
            qkv[0, at, :], qkv[1, at, :], qkv[2, at, :], cg[at, :], mask[at, :count]
        )
        for part in range(3):
            pg[part, at, :] = grads[part]

    block_loop(blocks, block, unroll=True)

    def columns(i):
        cols = lanes(i, 256)
        for j, out in ((3, p3), (1, p1), (2, p2), (0, p0)):
            at = chunk_start(me ^ j, size)
            total = dot(pg[0, at, :], w_t[:width, cols])
            for part in range(1, 3):
                total += dot(pg[part, at, :], w_t[part * width : (part + 1) * width, cols])
            out[:, cols] = total.astype(BF)

    repeat(dim // 256, columns)


def place_in(relative, order):
    place = 0
    for k, bit in enumerate(order):
        place = place + ((relative // bit) % 2) * 2 ** (len(order) - 1 - k)
    return place


def place_of(relative, orders):
    core = lax.axis_index("mp") % 2
    return jnp.where(core == 0, place_in(relative, orders[0]), place_in(relative, orders[1]))


def emit(full, outs, orders):
    if orders is None:
        outs[0][...] = full[...]
        return
    keep, send = outs
    blocks = 2 ** len(orders[0])
    size = full.shape[0] // blocks
    here = lax.axis_index("dp")

    def block(b):
        place = place_of(here ^ b, orders)
        value = full[chunk_start(b, size), :].astype(BF)

        @pl.when(place < blocks // 2)
        def _():
            keep[chunk_start(place, size), :] = value

        @pl.when(place >= blocks // 2)
        def _():
            send[chunk_start(place - blocks // 2, size), :] = value

    repeat(blocks, block)


def weight_product(left, right, full):
    def block(i):
        at = pl.ds(pl.multiple_of(i * 256, 256), 256)
        full[at, :] = dot(left[:, lanes(i, 256)], right[...], TN)

    repeat(left.shape[1] // 256, block)


def row_sum(ref):
    return jnp.sum(ref[...].astype(F32), axis=0, keepdims=True)


def fc_weight_kernel(orders, left0, left1, right0, right1, *rest):
    *outs, sums, full, left, right = rest
    half = left0.shape[0]
    for at, a, b in ((slice(0, half), left0, right0), (slice(half, 2 * half), left1, right1)):
        left[at, :] = a[...]
        right[at, :] = b[...]
    weight_product(left, right, full)
    emit(full, outs, orders)
    sums[...] = row_sum(right)


def attn_weights_kernel(orders, ctx, og0, og1, rows_own, rows_far, pg, *rest):
    *outs, out_sum, qv_sum, full, rows, og = rest
    half = og0.shape[0]
    side = lax.axis_index("mp") // 2
    width = ctx.shape[1]
    rows[chunk_start(side, half), :] = rows_own[...]
    rows[chunk_start(1 - side, half), :] = rows_far[...]
    og[:half, :] = og0[...]
    og[half:, :] = og1[...]

    def part(i):
        full[chunk_start(i, width), :] = dot(pg[i], rows[...], TN)

    repeat(3, part)
    full[3 * width :, :] = dot(ctx[...], og[...], TN)
    emit(full, outs, orders)
    out_sum[...] = row_sum(og)
    qv_sum[...] = jnp.concatenate(
        [jnp.sum(pg[part].astype(F32), axis=0, keepdims=True) for part in (0, 2)], axis=0
    )


def gather_blocks_kernel(orders, low_half, high_half, out):
    blocks = 2 ** len(orders[0])
    size = 2 * low_half.shape[0] // blocks
    here = lax.axis_index("dp")

    def block(b):
        place = place_of(here ^ b, orders)
        at = chunk_start(place % (blocks // 2), size)
        value = jnp.where(place < blocks // 2, low_half[at, :], high_half[at, :])
        out[chunk_start(b, size), :] = value.astype(F32)

    repeat(blocks, block)


def gather_attn_kernel(orders, low_half, high_half, qkv, out_w, full):
    gather_blocks_kernel(orders, low_half, high_half, full)
    rows = qkv.shape[0]
    qkv[...] = full[:rows, :]
    out_w[...] = full[rows:, :]


def input_grad_kernel(x, mine, theirs, after_grad0, after_grad1, vectors, grad, sums):
    side = lax.axis_index("mp") // 2
    normed, inverse = norm(x[...].astype(F32))
    rows_grad = mine[...].astype(F32) + theirs[...].astype(F32)
    sums[...] = jnp.concatenate(
        [
            jnp.sum(rows_grad * normed, axis=0, keepdims=True),
            jnp.sum(rows_grad, axis=0, keepdims=True),
        ],
        axis=0,
    )
    after_grad = jnp.where(side == 0, after_grad0[...], after_grad1[...])
    value = after_grad + norm_back(
        rows_grad, vector(vectors, ATTN_GAIN), normed, inverse
    )
    grad[...] = value.astype(BF)


def text_out_kernel(mine0, mine1, theirs, after0, after1, vectors, out):
    side = lax.axis_index("mp") // 2
    after = jnp.where(side == 0, after0[...], after1[...])
    mine = jnp.where(side == 0, mine0[...], mine1[...])
    branch = mine.astype(F32) + theirs[...].astype(F32)
    out[...] = (after + (branch + vector(vectors, FC2_BIAS))).astype(BF)


def far_branch_kernel(br0, br1, far):
    far[...] = jnp.where(lax.axis_index("mp") // 2 == 0, br1[...], br0[...])


def add_rows_kernel(a, b, out):
    out[...] = a[...] + b[...]


def norm_sums_kernel(mlp0, mlp1, attn, out):
    out[0:2, :] = mlp0[...] + mlp1[...]
    out[2:4, :] = attn[...]


def small_kernel(sums, far, fc2, fc1, out_b, qv, out):
    width = qv.shape[1]
    out[0:2, :] = sums[0:2, :]
    out[2:4, :] = sums[2:4, :] + far[2:4, :]
    out[4:5, :] = fc2[...]
    out[5:6, :] = fc1[...]
    out[6:7, :] = out_b[...]
    out[7:8, :] = jnp.zeros((1, out.shape[1]), F32)
    out[7:8, :width] = qv[0:1, :]
    out[7:8, 2 * width : 3 * width] = qv[1:2, :]


def image_windows(count, images):
    windows = []
    per = 4
    for low in range(0, images, per):
        start = (low * IMG_SEQ + 15) // 16 * 16 if low else 0
        end = min(count, ((low + per) * IMG_SEQ + 15) // 16 * 16)
        if low + per >= images:
            end = count
        key_start = start // IMG_SEQ * IMG_SEQ // 16 * 16
        key_end = min(count, ((end - 1) // IMG_SEQ * IMG_SEQ + IMG_SEQ + 15) // 16 * 16)
        windows.append((start, end, key_start, key_end))
    return windows


def image_attn_kernel(first, x0, x1, vectors, *rest):
    if first:
        source, result, rows, context, total, weights, sem = rest
    else:
        before, source, keep, *sends, rows, context, total, weights, sem = rest
    count, dim = x0.shape
    images = count // IMG_SEQ
    width = dim // 4
    copy = pltpu.make_async_copy(source.at[0 : 4 * width + 16], weights, sem)
    copy.start()
    for k, x in enumerate((x0, x1)):
        normed, _ = norm(x[...].astype(F32))
        rows[k * count : (k + 1) * count, :] = (
            normed * vector(vectors, ATTN_GAIN) + vector(vectors, ATTN_SHIFT)
        ).astype(BF)
    windows = image_windows(count, images)
    copy.wait()
    bias = weights[4 * width : 4 * width + 16, :].astype(F32)

    def chunk(c):
        own = rows[chunk_start(c, count), :]
        q = (dot(own, weights[:width, :], NT) + bias[0:1, :width]).astype(BF)
        k = dot(own, weights[width : 2 * width, :], NT).astype(BF)
        v = (dot(own, weights[2 * width : 3 * width, :], NT) + bias[1:2, :width]).astype(BF)
        for q_low, q_high, k_low, k_high in windows:
            extent = (q_high - q_low, k_high - k_low)
            q_image = (lax.broadcasted_iota(jnp.int32, extent, 0) + q_low) // IMG_SEQ
            k_image = (lax.broadcasted_iota(jnp.int32, extent, 1) + k_low) // IMG_SEQ
            mask = jnp.where(q_image == k_image, 1.0, 0.0)
            place = pl.ds(pl.multiple_of(c * count + q_low, 16), q_high - q_low)
            context[place, :] = attend(
                q[q_low:q_high], k[k_low:k_high], v[k_low:k_high], mask
            )

    def columns(i):
        cols = lanes(i, 256)
        total[:, cols] = dot(context[...], weights[3 * width : 4 * width, cols])

    repeat(2, chunk)
    repeat(dim // 256, columns)
    if first:
        result.held[...] = total[...]
        result.start()
        return
    keep[...] = total[:count, :] + before[:count, :]
    put_pieces((total[count:, :] + before[count:, :]).astype(BF), sends)


def image_norm_kernel(x, keep, vectors, *rest):
    *others, after_out, rows = rest
    total = keep[...] + join_pieces(others).astype(F32)
    after = x[...].astype(F32) + (total + vector(vectors, OUT_BIAS))
    after_out.held[...] = after
    after_out.start()
    normed, _ = norm(after)
    rows[...] = (normed * vector(vectors, MLP_GAIN) + vector(vectors, MLP_SHIFT)).astype(BF)


def image_mlp_kernel(rows0, rows2, vec0, vec1, w1a, w2a, w1b, w2b, mine, far, rows, active, total):
    size, dim = rows0.shape
    rows[:size, :] = rows0[...]
    rows[size:, :] = rows2[...]
    total[...] = jnp.zeros(total.shape, F32)
    for vectors, w1, w2 in ((vec0, w1a, w2a), (vec1, w1b, w2b)):
        w1 = w1.get()

        def units(i):
            cols = lanes(i, 256)
            hidden = dot(rows[...], w1[:, cols]) + vectors[FC1_BIAS : FC1_BIAS + 1, cols]
            active[:, cols] = gelu_parts(hidden)[0].astype(BF)

        repeat(w1.shape[1] // 256, units)
        w2 = w2.get()

        def columns(i):
            cols = lanes(i, 256)
            total[:, cols] += dot(active[...], w2[:, cols])

        repeat(dim // 256, columns)
    mine[...] = total[:size, :].astype(BF)
    far[...] = total[size:, :].astype(BF)


def image_out_kernel(after, mine, theirs, vectors, out):
    branch = mine[...].astype(F32) + theirs[...].astype(F32)
    out[...] = (after[...] + (branch + vector(vectors, FC2_BIAS))).astype(BF)


def core_swap(x):
    return lax.ppermute(x, "mp", [(i, i ^ 1) for i in range(lax.axis_size("mp"))])


def side_swap(x):
    return lax.ppermute(x, "mp", [(i, i ^ 2) for i in range(lax.axis_size("mp"))])


def dp_swap(x, bits):
    n_dp, n_mp = lax.axis_size("dp"), lax.axis_size("mp")
    pairs = [
        (d * n_mp + m, (d ^ bits[m % 2]) * n_mp + m) for d in range(n_dp) for m in range(n_mp)
    ]
    return lax.ppermute(x, ("dp", "mp"), pairs)


def per_device(
    text_in,
    segment_ids,
    valid_lengths,
    text_grad,
    attn_gain,
    attn_shift,
    qkv_weight,
    qv_bias,
    out_weight,
    out_bias,
    mlp_gain,
    mlp_shift,
    fc1_weight,
    fc1_bias,
    fc2_weight,
    fc2_bias,
    images,
    img_attn_gain,
    img_attn_shift,
    img_qkv_weight,
    img_qv_bias,
    img_out_weight,
    img_out_bias,
    img_mlp_gain,
    img_mlp_shift,
    img_fc1_weight,
    img_fc1_bias,
    img_fc2_weight,
    img_fc2_bias,
):
    size, dim = text_in.shape
    row_count, length = segment_ids.shape
    width = qkv_weight.shape[2]
    n_dp = lax.axis_size("dp")
    tokens = 4 * size

    w_t = qkv_weight.transpose(1, 2, 0).reshape(3 * width, dim)
    img_w_t = img_qkv_weight.transpose(1, 2, 0).reshape(3 * width, dim)
    used = 4 * width + 16
    total_rows = -(-used // (16 * n_dp)) * 16 * n_dp
    part_rows = total_rows // n_dp

    rows_first = 2 * size // length
    blocks = row_blocks(row_count, length, rows_first)
    blocks_first = [b for b in blocks if b[0] < rows_first * length]
    blocks_rest = [b for b in blocks if b[0] >= rows_first * length]

    run = Line()
    chunk = shape(size, dim)
    pair = shape(2 * size, dim)

    x0 = text_in
    x2 = side_swap(x0)
    x1 = core_swap(x0)
    vectors, img_vectors = run(
        vectors_kernel,
        [shape(8, dim, dtype=F32)] * 2,
        [
            Late(v)
            for v in (
                attn_gain, attn_shift, out_bias, mlp_gain, mlp_shift, fc2_bias, fc1_bias,
                img_attn_gain, img_attn_shift, img_out_bias, img_mlp_gain, img_mlp_shift,
                img_fc2_bias, img_fc1_bias,
            )
        ],
    )
    project_scratch = [pltpu.VMEM((2, size, dim), BF), pltpu.VMEM((8, width), F32)]
    rows_own, qkv_own = run(
        own_rows_kernel,
        [Early(2 * size, dim), shape(3, 2 * size, width)],
        [x0, x1, vectors, w_t, qv_bias],
        scratch=project_scratch,
    )
    mask = run(
        functools.partial(mask_kernel, blocks),
        [shape(tokens, 2 * length, dtype=F32)],
        [segment_ids, valid_lengths],
        scalars=(1,),
    )
    bundle = run(
        bundle_kernel,
        [shape(total_rows, dim)],
        [img_w_t, img_out_weight, img_qv_bias],
        scratch=[
            pltpu.VMEM((total_rows - 4 * width, dim), BF),
            pltpu.SemaphoreType.DMA((3,)),
        ],
        untouched=(0, 1),
        outside=True,
    )
    t0 = text_grad
    t1 = core_swap(t0)
    packed = run(
        far_operands_kernel,
        [shape(size + part_rows, dim)],
        [t0, bundle],
        scratch=[pltpu.SemaphoreType.DMA(())],
        untouched=(1,),
        after=[x2],
    )
    x2 = run.hold(x2)
    x3 = core_swap(x2)
    packed = side_swap(packed)

    rows_far, qkv, ctx, x_mine, keep0, keep1, send0, send1 = run(
        functools.partial(attn_forward_kernel, blocks),
        [
            Early(2 * size, dim),
            Early(3, tokens, width),
            Early(tokens, width),
            Early(2, size, dim),
        ]
        + [chunk] * 4,
        [x0, x2, x3, qkv_own, vectors, w_t, qv_bias, out_weight, mask],
        scratch=project_scratch,
    )

    thirds, halves = pieces_of(size, 3), pieces_of(size, 2)

    def after_attn(half, mine, theirs):
        stream, rows, *sends = run(
            functools.partial(after_attn_kernel, half),
            [Early(size, dim, dtype=F32), chunk] + [shape(n, dim) for n in thirds],
            [x_mine, mine, theirs, vectors],
        )
        return stream, (rows, *map(core_swap, sends))

    def mlp(rows, grad):
        all_rows, act, hid_grad, br_keep, br_send, mg_keep, *mg_sends = run(
            functools.partial(mlp_kernel, len(rows) - 1),
            [Early(2 * size, dim)] * 3
            + [Early(size, dim)] * 2
            + [chunk]
            + [shape(n, dim) for n in halves],
            [*rows, grad, fc1_weight, vectors, fc2_weight],
        )
        partial = (mg_keep, *map(core_swap, mg_sends))
        return all_rows, act, hid_grad, (br_keep, core_swap(br_send)), partial

    def mlp_back(stream, mine, theirs, grad):
        value, low, sums, *sends = run(
            mlp_back_kernel,
            [Early(size, dim, dtype=F32), chunk, shape(2, dim, dtype=F32)]
            + [shape(n, dim) for n in thirds],
            [stream, mine, theirs, grad, vectors],
        )
        return value, (low, *map(core_swap, sends)), sums

    other0, other1 = core_swap(send0), core_swap(send1)
    mine0 = run(add_kernel, [chunk], [keep0, other0], after=[packed])
    theirs0 = side_swap(mine0)
    far_part = run(unpack_kernel, [shape(part_rows, dim)], [packed])
    far_bundle = lax.all_gather(far_part, "dp", axis=0, tiled=True)

    image_rows = images.shape[0]
    image_chunk = shape(image_rows, dim)
    img_other = core_swap(images)
    img_w1_other, img_w2_other = core_swap(img_fc1_weight), core_swap(img_fc2_weight)
    img_vectors_other = core_swap(img_vectors)
    image_scratch = [
        pltpu.VMEM((2 * image_rows, dim), BF),
        pltpu.VMEM((2 * image_rows, width), BF),
        pltpu.VMEM((2 * image_rows, dim), F32),
        pltpu.VMEM((used, dim), BF),
        pltpu.SemaphoreType.DMA(()),
    ]
    image_total = run(
        functools.partial(image_attn_kernel, True),
        [Early(2 * image_rows, dim, dtype=F32)],
        [images, img_other, img_vectors, Fixed(bundle)],
        scratch=image_scratch,
        after=[Fixed(img_w1_other), img_vectors_other],
    )
    tg0, tg1 = run(
        arrange_kernel, [Early(2 * size, dim)] * 2, [t0, t1, packed, core_swap(packed)]
    )
    mine1 = run(add_kernel, [chunk], [keep1, other1], after=[theirs0])
    theirs1 = side_swap(mine1)
    stream0, rows0 = after_attn(0, mine0, theirs0)
    all_rows0, act0, hg0, branch0, partial0 = mlp(rows0, tg0)
    mg0 = run(add_pieces_kernel, [chunk], partial0, after=[theirs1, Fixed(img_w2_other)])
    mg_theirs0 = side_swap(mg0)
    stream1, rows1 = after_attn(1, mine1, theirs1)
    all_rows1, act1, hg1, branch1, partial1 = mlp(rows1, tg1)

    bits = [2**k for k in range(n_dp.bit_length() - 1)]
    along_x = tuple(bits)
    mixed, even = (along_x, tuple(bits[1:] + bits[:1])), (along_x, along_x)
    plain = 2 ** len(bits) != n_dp or dim % (16 * n_dp) != 0
    if plain:
        mixed = even = None
    grad_shapes = [shape(dim, dim, dtype=F32)] if plain else [shape(dim // 2, dim)] * 2

    class Sum:
        def __init__(self, parts, orders, last, sizes):
            self.orders, self.last, self.sizes, self.step = orders, last, sizes, 0
            if plain:
                total = lax.psum(parts[0], "dp")
                cuts = [sum(sizes[: i + 1]) for i in range(len(sizes) - 1)]
                self.result = jnp.split(total, cuts, axis=0)
                return
            self.keep = parts[0]
            self.exchange(parts[1], 0)

        def exchange(self, send, k):
            self.arriving = dp_swap(send, (self.orders[0][k], self.orders[1][k]))

        def advance(self):
            if plain or self.step == 2 * len(bits):
                return
            self.step += 1
            rows, levels = self.keep.shape[0], len(bits)
            if self.step < levels:
                self.keep, send = run(
                    add_split_kernel, [shape(rows // 2, dim)] * 2, [self.keep, self.arriving]
                )
                self.exchange(send, self.step)
            elif self.step < 2 * levels:
                if self.step == levels:
                    self.keep = run(add_kernel, [shape(rows, dim)], [self.keep, self.arriving])
                else:
                    self.keep = run(
                        join_kernel, [shape(2 * rows, dim)], [self.keep, self.arriving]
                    )
                self.exchange(self.keep, 2 * levels - 1 - self.step)
            else:
                got = run(
                    functools.partial(self.last, self.orders),
                    [shape(n, dim, dtype=F32) for n in self.sizes],
                    [self.keep, self.arriving],
                    scratch=[pltpu.VMEM((dim, dim), F32)] if len(self.sizes) > 1 else [],
                )
                self.result = got if len(self.sizes) > 1 else [got]

    def advance(*totals):
        for total in totals:
            total.advance()

    def fc_weight(orders, args):
        *parts, sums = run(
            functools.partial(fc_weight_kernel, orders),
            grad_shapes + [shape(1, dim, dtype=F32)],
            args,
            scratch=[pltpu.VMEM((dim, dim), F32)] + [pltpu.VMEM((tokens, dim), BF)] * 2,
        )
        return Sum(parts, orders, gather_blocks_kernel, (dim,)), sums

    fc2_sum, fc2_bias_sum = fc_weight(mixed, [act0, act1, tg0, tg1])
    mg1 = run(add_pieces_kernel, [chunk], partial1, after=[mg_theirs0])
    mg_theirs1 = side_swap(mg1)
    after_grad0, og0, mlp_sums0 = mlp_back(stream0, mg0, mg_theirs0, tg0)
    fc1_sum, fc1_bias_sum = fc_weight(even, [all_rows0, all_rows1, hg0, hg1])
    fc2_sum.advance()

    og_first, cg_first, pg_first = run(
        functools.partial(attn_back_first_kernel, blocks_first, len(og0) - 1),
        [pair, shape(2 * size, width), shape(3, rows_first * length, width)],
        [*og0, qkv, mask, out_weight],
    )
    after_grad1, og1, mlp_sums1 = mlp_back(stream1, mg1, mg_theirs1, tg1)
    og_second, pg, p0, p1, p2, p3 = run(
        functools.partial(attn_back_second_kernel, blocks_rest, len(og1) - 1),
        [pair, shape(3, tokens, width)] + [chunk] * 4,
        [*og1, cg_first, pg_first, qkv, mask, out_weight, w_t],
        scratch=[pltpu.VMEM((tokens, width), BF)],
    )
    p_other1, p_other3 = core_swap(p1), core_swap(p3)
    fc2_sum.advance()
    fc1_sum.advance()
    *parts, out_sum, qv_sum = run(
        functools.partial(attn_weights_kernel, mixed),
        grad_shapes + [shape(1, dim, dtype=F32), shape(2, width, dtype=F32)],
        [ctx, og_first, og_second, rows_own, rows_far, pg],
        scratch=[pltpu.VMEM((dim, dim), F32)] + [pltpu.VMEM((tokens, dim), BF)] * 2,
    )
    attn_sum = Sum(parts, mixed, gather_attn_kernel, (3 * width, width))

    img_keep, *img_sends = run(
        functools.partial(image_attn_kernel, False),
        [shape(image_rows, dim, dtype=F32)] + [shape(n, dim) for n in pieces_of(image_rows, 3)],
        [images, img_other, img_vectors, image_total, Fixed(far_bundle)],
        scratch=image_scratch,
        vmem=20,
    )
    img_after, img_rows0 = run(
        image_norm_kernel,
        [Early(image_rows, dim, dtype=F32), image_chunk],
        [images, img_keep, img_vectors, *map(core_swap, img_sends)],
    )
    img_rows2 = side_swap(img_rows0)
    p_mine, to_side = run(add_pair_kernel, [chunk] * 2, [p0, p_other1, p2, p_other3])
    p_theirs = side_swap(to_side)
    advance(fc2_sum, fc1_sum, attn_sum)
    br0, br1 = run(branch_sums_kernel, [Early(size, dim)] * 2, [*branch0, *branch1])
    far_branch = run(far_branch_kernel, [chunk], [br0, br1])
    br_theirs = side_swap(far_branch)
    advance(fc2_sum, fc1_sum, attn_sum)
    text_in_grad, attn_sums = run(
        input_grad_kernel,
        [chunk, shape(2, dim, dtype=F32)],
        [text_in, p_mine, p_theirs, after_grad0, after_grad1, vectors],
    )
    small = run(norm_sums_kernel, [shape(4, dim, dtype=F32)], [mlp_sums0, mlp_sums1, attn_sums])
    small_near = core_swap(small)
    i_mine, i_side = run(
        image_mlp_kernel,
        [image_chunk] * 2,
        [
            img_rows0, img_rows2, img_vectors, img_vectors_other,
            Late(img_fc1_weight), Late(img_fc2_weight), Late(img_w1_other), Late(img_w2_other),
        ],
        scratch=[pltpu.VMEM((2 * image_rows, dim), BF)] * 2
        + [pltpu.VMEM((2 * image_rows, dim), F32)],
        vmem=24,
    )
    i_theirs = side_swap(i_side)
    small = run(add_rows_kernel, [shape(4, dim, dtype=F32)], [small, small_near])
    small_far = side_swap(small)
    advance(fc1_sum, attn_sum, fc2_sum)
    text_out = run(
        text_out_kernel,
        [chunk],
        [br0, br1, br_theirs, stream0, stream1, vectors],
    )
    small = run(
        small_kernel,
        [shape(8, dim, dtype=F32)],
        [small, small_far, fc2_bias_sum, fc1_bias_sum, out_sum, qv_sum],
    )
    if plain:
        small_far = lax.psum(small, "dp")
        small = jnp.zeros_like(small)
    else:
        small_far = dp_swap(small, (bits[0], bits[0]))
    advance(attn_sum, fc1_sum, fc2_sum)
    image_out = run(
        image_out_kernel, [image_chunk], [img_after, i_mine, i_theirs, img_vectors]
    )
    if not plain:
        for bit in bits[1:]:
            small = run(add_rows_kernel, [shape(8, dim, dtype=F32)], [small, small_far])
            small_far = dp_swap(small, (bit, bit))
            advance(attn_sum, fc1_sum)
    small = run(add_rows_kernel, [shape(8, dim, dtype=F32)], [small, small_far])
    for total in (fc2_sum, fc1_sum, attn_sum):
        while not plain and total.step < 2 * len(bits):
            total.advance()
    (grad_fc2_weight,) = fc2_sum.result
    (grad_fc1_weight,) = fc1_sum.result
    grad_qkv, grad_out_weight = attn_sum.result
    return (
        text_out,
        image_out,
        text_in_grad,
        small[2],
        small[3],
        grad_qkv.reshape(3, width, dim).transpose(2, 0, 1),
        jnp.stack([small[7, :width], small[7, 2 * width : 3 * width]]),
        grad_out_weight,
        small[6],
        small[0],
        small[1],
        grad_fc1_weight,
        small[5],
        grad_fc2_weight,
        small[4],
    )


def solution(mesh):
    in_specs = (
        P(("dp", "mp"), None),
        P("dp", None),
        P("dp"),
        P(("dp", "mp"), None),
        P(),
        P(),
        P(None, None, "mp"),
        P(None, "mp"),
        P("mp", None),
        P(),
        P(),
        P(),
        P(None, "mp"),
        P("mp"),
        P("mp", None),
        P(),
        P(("dp", "mp"), None),
        P(),
        P(),
        P(None, None, "mp"),
        P(None, "mp"),
        P("mp", None),
        P(),
        P(),
        P(),
        P(None, "mp"),
        P("mp"),
        P("mp", None),
        P(),
    )
    out_specs = (
        P(("dp", "mp"), None),
        P(("dp", "mp"), None),
        P(("dp", "mp"), None),
        P(),
        P(),
        P(None, None, "mp"),
        P(None, "mp"),
        P("mp", None),
        P(),
        P(),
        P(),
        P(None, "mp"),
        P("mp"),
        P("mp", None),
        P(),
    )
    return jax.shard_map(
        per_device, mesh=mesh, in_specs=in_specs, out_specs=out_specs, check_vma=False
    )
```

```python
import functools

import jax
import jax.numpy as jnp
from jax import lax
from jax.experimental import pallas as pl
from jax.experimental.pallas import tpu as pltpu
from jax.sharding import PartitionSpec as P

HEAD = 64
IMG_SEQ = 50
EPS = 1e-05
BF = jnp.bfloat16
F32 = jnp.float32
SCALE = HEAD ** (-0.5)
NEG = -1000000000.0
ROOT = 0.7978845608028654
CUBE = 0.044715

PLAN = (
    "fc2_weight", "mlp_sum", "mlp_back0", "fc1_weight", "fc2", "attn_back0", "mlp_back1",
    "attn_back1", "fc2", "fc1", "attn_weights",
    "p_sums", "image_attn", "fc2", "fc1", "qkv", "image_norm", "fc2", "fc1", "qkv", "input",
    "branch", "qkv", "fc2", "small_near", "image_mlp", "fc1", "text_out", "small_side", "qkv",
    "fc1", "fc2", "small_dp", "qkv", "fc1", "small_dp", "qkv", "image_out", "small_dp",
)

ORDERS = ("mixed", "even", "mixed")
PIECES = (3, 2, 3, 3, 2)

NN = (((1,), (0,)), ((), ()))
NT = (((1,), (1,)), ((), ()))
TN = (((0,), (0,)), ((), ()))


def dot(a, b, dims=NN):
    return lax.dot_general(a, b, dims, preferred_element_type=F32)


def shape(*dims, dtype=BF):
    return jax.ShapeDtypeStruct(dims, dtype)


class Late:
    def __init__(self, value):
        self.value, self.shape, self.dtype = value, value.shape, value.dtype


class Fixed:
    def __init__(self, value):
        self.value, self.shape, self.dtype = value, value.shape, value.dtype


class Early:
    def __init__(self, *dims, dtype=BF):
        self.shape, self.dtype = dims, dtype


class Pinned(Early):
    pass


class Moving:
    def __init__(self, source, target, held, sem):
        self.held, self.shape = held, held.shape
        self.copy = pltpu.make_async_copy(source, target, sem)
        self.waits = False

    def start(self):
        self.copy.start()
        self.waits = True

    def get(self):
        if self.waits:
            self.copy.wait()
            self.waits = False
        return self.held


class Line:
    def __init__(self):
        self.token = None

    def __call__(self, body, outs, args, scratch=(), vmem=16, untouched=(), scalars=(), after=(),
                 same=None, outside=False):
        def place(a):
            if isinstance(a, (Late, Fixed)):
                return pltpu.with_memory_space_constraint(a.value, pltpu.HBM)
            return a

        kinds = list(args)
        real = len(kinds)
        values = [place(a) for a in kinds + list(after)]
        values += [] if self.token is None else [self.token]
        given = len(values)
        late = [i for i, a in enumerate(kinds) if isinstance(a, Late)]
        fixed = [i for i, a in enumerate(kinds) if isinstance(a, Fixed)]
        early = [i for i, o in enumerate(outs) if type(o) is Early]

        def in_space(i):
            if i >= real or i in untouched:
                return pl.ANY
            if i in late or i in fixed:
                return pltpu.HBM
            return pltpu.SMEM if i in scalars else pltpu.VMEM

        def out_space(i):
            if isinstance(outs[i], Early):
                return pltpu.HBM
            return pl.ANY if outside or same is not None else pltpu.VMEM

        moving = [kinds[i] for i in late] + [outs[i] for i in early]
        held = [pltpu.VMEM(m.shape, m.dtype) for m in moving]
        sems = [pltpu.SemaphoreType.DMA((len(held),))] if held else []
        first = given + len(outs) + 1

        def run(*refs):
            ins, results = list(refs[:real]), list(refs[given : given + len(outs)])
            places = refs[first : first + len(held)]
            for k, i in enumerate(late):
                ins[i] = Moving(ins[i], places[k], places[k], refs[-1].at[k])
                ins[i].start()
            for k, i in enumerate(early, len(late)):
                results[i] = Moving(places[k], results[i], places[k], refs[-1].at[k])
            body(*ins, *results, *refs[first + len(held) : len(refs) - len(sems)])
            for moved in [ins[i] for i in late] + [results[i] for i in early]:
                moved.get()

        results = pl.pallas_call(
            run,
            out_shape=(
                *(
                    pltpu.HBM(o.shape, o.dtype)
                    if isinstance(o, Early)
                    else jax.ShapeDtypeStruct(o.shape, o.dtype)
                    for i, o in enumerate(outs)
                ),
                shape(8, 128, dtype=F32),
            ),
            in_specs=[pl.BlockSpec(memory_space=in_space(i)) for i in range(given)],
            out_specs=tuple(
                [pl.BlockSpec(memory_space=out_space(i)) for i in range(len(outs))]
                + [pl.BlockSpec(memory_space=pl.ANY)]
            ),
            scratch_shapes=held + list(scratch) + sems,
            input_output_aliases={} if same is None else {same: 0},
            compiler_params=pltpu.CompilerParams(vmem_limit_bytes=vmem * 1024 * 1024),
            cost_estimate=pl.CostEstimate(flops=1, bytes_accessed=1, transcendentals=0),
        )(*values)
        self.token = results[-1]
        return results[:-1] if len(outs) > 1 else results[0]

    def hold(self, value, after=()):
        return self(lambda *refs: None, [shape(*value.shape, dtype=value.dtype)], [value],
                    untouched=(0,), same=0, after=after)


def norm(x):
    centred = x - jnp.mean(x, axis=-1, keepdims=True)
    inverse = lax.rsqrt(jnp.mean(centred * centred, axis=-1, keepdims=True) + EPS)
    return centred * inverse, inverse


def norm_back(upstream, gain, normed, inverse):
    scaled = upstream * gain
    first = jnp.mean(scaled, axis=-1, keepdims=True)
    second = jnp.mean(scaled * normed, axis=-1, keepdims=True)
    return inverse * (scaled - first - normed * second)


def head_marks(width, dtype):
    lane = lax.broadcasted_iota(jnp.int32, (1, width), 1) // HEAD
    return [jnp.where(lane == h, 1.0, 0.0).astype(dtype) for h in range(width // HEAD)]


def stack_heads(rows, marks):
    return jnp.concatenate([rows * mark for mark in marks], axis=0)


def fold_heads(stacked, count, marks):
    total = stacked[:count] * marks[0]
    for h in range(1, len(marks)):
        total += stacked[h * count : (h + 1) * count] * marks[h]
    return total


def masked_scores(q_stack, k, mask):
    raw = dot(q_stack, k, NT)
    heads = raw.shape[0] // mask.shape[0]
    raw = raw.reshape(heads, mask.shape[0], mask.shape[1])
    return jnp.where(mask[None] > 0, raw * SCALE, NEG)


def softmax_parts(scores):
    peak = jnp.max(scores, axis=-1, keepdims=True)
    weights = jnp.exp(scores - peak)
    return weights, jnp.sum(weights, axis=-1, keepdims=True)


def attend(q, k, v, mask):
    count = q.shape[0]
    scores = masked_scores(stack_heads(q, head_marks(q.shape[1], BF)), k, mask)
    weights, total = softmax_parts(scores)
    probs = (weights / total).astype(BF).reshape(-1, mask.shape[1])
    return fold_heads(dot(probs, v), count, head_marks(q.shape[1], F32)).astype(BF)


def attend_back(q, k, v, grad, mask):
    count = q.shape[0]
    low = head_marks(q.shape[1], BF)
    q_stack = stack_heads(q, low)
    g_stack = stack_heads(grad, low)
    weights, total = softmax_parts(masked_scores(q_stack, k, mask))
    probs = weights / total
    prob_grad = dot(g_stack, v, NT).reshape(probs.shape)
    centre = jnp.sum(prob_grad * probs, axis=-1, keepdims=True)
    score_grad = (probs * (prob_grad - centre)).astype(BF).reshape(-1, mask.shape[1])
    probs_low = probs.astype(BF).reshape(-1, mask.shape[1])
    v_grad = dot(probs_low, g_stack, TN)
    q_grad = fold_heads(dot(score_grad, k), count, head_marks(q.shape[1], F32)) * SCALE
    k_grad = dot(score_grad, q_stack, TN) * SCALE
    return q_grad.astype(BF), k_grad.astype(BF), v_grad.astype(BF)


def gelu_parts(v):
    square = v * v
    t = jnp.tanh(ROOT * (v + CUBE * (square * v)))
    half = 0.5 * (1.0 + t)
    slope = half + 0.5 * v * (1.0 - t * t) * (ROOT * (1.0 + 3.0 * CUBE * square))
    return v * half, slope


def repeat(count, body):
    def step(i, carry):
        body(i)
        return carry

    lax.fori_loop(0, count, step, 0)


def lanes(index, size):
    return pl.ds(pl.multiple_of(index * size, 128), size)


def pieces_of(count, parts):
    most = -(-count // (16 * parts)) * 16
    return [min(most, count - low) for low in range(0, count, most)]


def put_pieces(value, outs):
    low = 0
    for out in outs:
        out[...] = value[low : low + out.shape[0]]
        low += out.shape[0]


def join_pieces(refs):
    return jnp.concatenate([ref[...] for ref in refs], axis=0)


def chunk_start(index, size):
    return pl.ds(pl.multiple_of(index * size, 16), size)


def row_blocks(count, length, first):
    blocks = []
    for low, high in ((0, first), (first, count)):
        row = low
        if (high - low) % 2:
            blocks.append((row * length, length))
            row += 1
        while row < high:
            blocks.append((row * length, 2 * length))
            row += 2
    return blocks


def mask_kernel(blocks, segments, lengths, mask):
    length = segments.shape[1]
    square = (length, length)
    key = lax.broadcasted_iota(jnp.int32, square, 1)
    diagonal = key == lax.broadcasted_iota(jnp.int32, square, 0)
    mask[...] = jnp.zeros(mask.shape, F32)
    for start, count in blocks:
        for place in range(count // length):
            row = start // length + place
            along = jnp.broadcast_to(segments[row : row + 1, :].astype(F32), square)
            seen = (along == along.T) & ((key < lengths[row]) | diagonal)
            low = start + place * length
            mask[low : low + length, place * length : (place + 1) * length] = jnp.where(
                seen, 1.0, 0.0
            )


def bundle_kernel(w_t, out_w, qv, bundle, held, sems):
    width = qv.shape[1]
    held[...] = jnp.zeros(held.shape, held.dtype)
    held[0:2, :width] = qv[...]
    start, copies = 0, []
    for k, piece in enumerate((w_t, out_w, held)):
        rows = piece.shape[0]
        copies.append(pltpu.make_async_copy(piece, bundle.at[start : start + rows], sems.at[k]))
        copies[-1].start()
        start += rows
    for copy in copies:
        copy.wait()


ATTN_GAIN, ATTN_SHIFT, OUT_BIAS, MLP_GAIN, MLP_SHIFT, FC2_BIAS, FC1_BIAS, FC1_BIAS_OTHER = range(8)


def vectors_kernel(*refs):
    *items, text, image = refs
    for out, own in ((text, items[:7]), (image, items[7:])):
        out[...] = jnp.zeros(out.shape, F32)
        for k, item in enumerate(own):
            out[k : k + 1, :] = item.get()[...].astype(F32).reshape(1, -1)


def vector(vectors, index):
    return vectors[index : index + 1, :]


def project(x_pair, vectors, w_t, bias, rows_out, qkv, bias_rows, at):
    size = x_pair.shape[1]
    width = bias.shape[1]
    gain, shift = vector(vectors, ATTN_GAIN), vector(vectors, ATTN_SHIFT)
    bias_rows[...] = jnp.zeros(bias_rows.shape, F32)
    bias_rows[0:1, :] = bias[...].astype(F32)[0:1]
    bias_rows[2:3, :] = bias[...].astype(F32)[1:2]

    def normalize(i):
        normed, _ = norm(x_pair[i].astype(F32))
        rows[chunk_start(i, size), :] = (normed * gain + shift).astype(BF)

    def part(i):
        value = dot(rows[...], w_t[chunk_start(i, width), :], NT) + bias_rows[pl.ds(i, 1), :]
        qkv[i, at, :] = value.astype(BF)

    rows = rows_out.held
    repeat(2, normalize)
    rows_out.start()
    repeat(3, part)


def own_rows_kernel(x0, x1, vectors, w_t, bias, rows_out, qkv, x_pair, bias_rows):
    core = lax.axis_index("mp") % 2
    x_pair[core] = x0[...]
    x_pair[1 - core] = x1[...]
    project(x_pair, vectors, w_t, bias, rows_out, qkv, bias_rows, slice(None))


def far_operands_kernel(grad, bundle, packed, sem):
    size = grad.shape[0]
    part = packed.shape[0] - size
    copy = pltpu.make_async_copy(
        bundle.at[chunk_start(lax.axis_index("dp"), part)], packed.at[size:], sem
    )
    copy.start()
    packed[:size] = grad[...]
    copy.wait()


def unpack_kernel(packed, part):
    part[...] = packed[packed.shape[0] - part.shape[0] :]


def arrange_kernel(t0, t1, packed, packed_other, half0, half1):
    size = t0.shape[0]
    here = lax.axis_index("mp") // 2 == 0
    parts = ((slice(0, size), t0, packed), (slice(size, 2 * size), t1, packed_other))
    for at, own, far in parts:
        half0.held[at, :] = jnp.where(here, own[...], far[:size])
        half1.held[at, :] = jnp.where(here, far[:size], own[...])
    half0.start()
    half1.start()


def block_loop(blocks, body, unroll=False):
    if unroll:
        for start, tokens in blocks:
            body(pl.ds(start, tokens), tokens)
        return
    singles = [b for b in blocks if b[1] != blocks[-1][1]]
    pairs = [b[0] for b in blocks if b[1] == blocks[-1][1]]
    count = blocks[-1][1]
    for start, tokens in singles:
        body(pl.ds(start, tokens), tokens)

    def pair(i):
        start = pairs[0] + i * count
        for k in range(1, len(pairs)):
            gap = pairs[k] - pairs[k - 1] - count
            if gap:
                start = start + jnp.where(i >= k, gap, 0)
        body(pl.ds(pl.multiple_of(start, 16), count), count)

    repeat(len(pairs), pair)


def attn_forward_kernel(blocks, x0, x2, x3, qkv_own, vectors, w_t, bias, out_w, mask,
                        rows_out, qkv_out, ctx_out, x_mine, keep0, keep1, send0, send1,
                        x_pair, bias_rows):
    qkv, ctx = qkv_out.held, ctx_out.held
    me = lax.axis_index("mp")
    core, side = me % 2, me // 2
    size, dim = x2.shape
    x_pair[core] = x2[...]
    x_pair[1 - core] = x3[...]
    x_mine.held[side] = x0[...]
    x_mine.held[1 - side] = x2[...]
    x_mine.start()
    far = chunk_start(1 - side, 2 * size)
    project(x_pair, vectors, w_t, bias, rows_out, qkv, bias_rows, far)
    own = chunk_start(side, 2 * size)
    for part in range(3):
        qkv[part, own, :] = qkv_own[part]
    qkv_out.start()

    def block(at, count):
        ctx[at, :] = attend(qkv[0, at, :], qkv[1, at, :], qkv[2, at, :], mask[at, :count])

    block_loop(blocks, block, unroll=True)
    ctx_out.start()

    def columns(i):
        cols = lanes(i, 256)
        weight = out_w[:, cols]
        for half, (keep, send) in enumerate(((keep0, send0), (keep1, send1))):
            theirs = ctx[chunk_start(2 * half + 1 - core, size), :]
            send[:, cols] = dot(theirs, weight).astype(BF)
            mine = ctx[chunk_start(2 * half + core, size), :]
            keep[:, cols] = dot(mine, weight).astype(BF)

    repeat(dim // 256, columns)


def add_kernel(a, b, out):
    out[...] = (a[...].astype(F32) + b[...].astype(F32)).astype(BF)


def add_pieces_kernel(a, *rest):
    *pieces, out = rest
    out[...] = (a[...].astype(F32) + join_pieces(pieces).astype(F32)).astype(BF)


def branch_sums_kernel(keep0, other0, keep1, other1, mine0, mine1):
    for keep, other, mine in ((keep0, other0, mine0), (keep1, other1, mine1)):
        mine.held[...] = (keep[...].astype(F32) + other[...].astype(F32)).astype(BF)
        mine.start()


def add_pair_kernel(a0, b0, a1, b1, out0, out1):
    for a, b, out in ((a0, b0, out0), (a1, b1, out1)):
        out[...] = (a[...].astype(F32) + b[...].astype(F32)).astype(BF)


def add_split_kernel(a, b, keep, send):
    half = keep.shape[0]
    keep[...] = (a[:half].astype(F32) + b[:half].astype(F32)).astype(BF)
    send[...] = (a[half:].astype(F32) + b[half:].astype(F32)).astype(BF)


def join_kernel(a, b, out):
    half = a.shape[0]
    out[:half] = a[...]
    out[half:] = b[...]


def after_attn_kernel(half, x_mine, mine, theirs, vectors, after_out, rows, *pieces):
    total = mine[...].astype(F32) + theirs[...].astype(F32)
    stream = x_mine[half].astype(F32) + (total + vector(vectors, OUT_BIAS))
    after_out.held[...] = stream
    after_out.start()
    normed, _ = norm(stream)
    value = (normed * vector(vectors, MLP_GAIN) + vector(vectors, MLP_SHIFT)).astype(BF)
    rows[...] = value
    put_pieces(value, pieces)


def mlp_kernel(count, rows0, *rest):
    pieces, (grad, w1, vectors, w2), rest = rest[:count], rest[count : count + 4], rest[count + 4 :]
    rows_out, act_out, hg_out, br_keep, br_send, mg_keep, *mg_sends = rest
    size, dim = rows0.shape
    rows, act, hid_grad = rows_out.held, act_out.held, hg_out.held
    rows[:size, :] = rows0[...]
    rows[size:, :] = join_pieces(pieces)
    rows_out.start()
    grad = grad

    def units(i):
        cols = lanes(i, 256)
        hidden = dot(rows[...], w1[:, cols]) + vectors[FC1_BIAS : FC1_BIAS + 1, cols]
        active, slope = gelu_parts(hidden)
        act[:, cols] = active.astype(BF)
        active_grad = dot(grad[...], w2[cols, :], NT)
        hid_grad[:, cols] = (active_grad * slope).astype(BF)

    def columns(i):
        cols = lanes(i, 256)
        value = dot(hid_grad[...], w1[cols, :], NT).astype(BF)
        mg_keep[:, cols] = value[:size]
        low = size
        for send in mg_sends:
            send[:, cols] = value[low : low + send.shape[0]]
            low += send.shape[0]

    def branch_columns(i):
        cols = lanes(i, 256)
        value = dot(act[...], w2[:, cols]).astype(BF)
        br_keep.held[:, cols] = value[:size]
        br_send.held[:, cols] = value[size:]

    repeat(w1.shape[1] // 256, units)
    act_out.start()
    hg_out.start()
    repeat(dim // 256, branch_columns)
    br_keep.start()
    br_send.start()
    repeat(dim // 256, columns)


def mlp_back_kernel(after, mine, theirs, grad, vectors, ag_out, out_grad, sums, *pieces):
    size = mine.shape[0]
    rows_grad = mine[...].astype(F32) + theirs[...].astype(F32)
    normed, inverse = norm(after[...])
    sums[...] = jnp.concatenate(
        [
            jnp.sum(rows_grad * normed, axis=0, keepdims=True),
            jnp.sum(rows_grad, axis=0, keepdims=True),
        ],
        axis=0,
    )
    value = grad[:size, :].astype(F32) + norm_back(
        rows_grad, vector(vectors, MLP_GAIN), normed, inverse
    )
    ag_out.held[...] = value
    ag_out.start()
    low = value.astype(BF)
    out_grad[...] = low
    put_pieces(low, pieces)


def attn_back_first_kernel(blocks, count, og_mine, *rest):
    og_others, (qkv, mask, out_w, og, cg, pg) = rest[:count], rest[count:]
    core = lax.axis_index("mp") % 2
    size = og_mine.shape[0]
    og[chunk_start(core, size), :] = og_mine[...]
    og[chunk_start(1 - core, size), :] = join_pieces(og_others)
    cg[...] = dot(og[...], out_w[...], NT).astype(BF)
    qkv = qkv

    def block(at, count):
        grads = attend_back(
            qkv[0, at, :], qkv[1, at, :], qkv[2, at, :], cg[at, :], mask[at, :count]
        )
        for part in range(3):
            pg[part, at, :] = grads[part]

    block_loop(blocks, block)


def attn_back_second_kernel(blocks, count, og_mine, *rest):
    og_others, rest = rest[:count], rest[count:]
    cg_first, pg_first, qkv, mask, out_w, w_t, og, pg, p0, p1, p2, p3, cg = rest
    me = lax.axis_index("mp")
    core = me % 2
    size, dim = og_mine.shape
    width = out_w.shape[0]
    half = 2 * size
    done = pg_first.shape[1]
    og[chunk_start(core, size), :] = og_mine[...]
    og[chunk_start(1 - core, size), :] = join_pieces(og_others)
    cg[half:, :] = dot(og[...], out_w[...], NT).astype(BF)
    cg[:half, :] = cg_first[...]
    qkv = qkv
    for part in range(3):
        pg[part, :done, :] = pg_first[part]

    def block(at, count):
        grads = attend_back(
            qkv[0, at, :], qkv[1, at, :], qkv[2, at, :], cg[at, :], mask[at, :count]
        )
        for part in range(3):
            pg[part, at, :] = grads[part]

    block_loop(blocks, block, unroll=True)

    def columns(i):
        cols = lanes(i, 256)
        for j, out in ((3, p3), (1, p1), (2, p2), (0, p0)):
            at = chunk_start(me ^ j, size)
            total = dot(pg[0, at, :], w_t[:width, cols])
            for part in range(1, 3):
                total += dot(pg[part, at, :], w_t[part * width : (part + 1) * width, cols])
            out[:, cols] = total.astype(BF)

    repeat(dim // 256, columns)


def place_in(relative, order):
    place = 0
    for k, bit in enumerate(order):
        place = place + ((relative // bit) % 2) * 2 ** (len(order) - 1 - k)
    return place


def place_of(relative, orders):
    core = lax.axis_index("mp") % 2
    return jnp.where(core == 0, place_in(relative, orders[0]), place_in(relative, orders[1]))


def emit(full, outs, orders):
    if orders is None:
        outs[0][...] = full[...]
        return
    keep, send = outs
    blocks = 2 ** len(orders[0])
    size = full.shape[0] // blocks
    here = lax.axis_index("dp")

    def block(b):
        place = place_of(here ^ b, orders)
        value = full[chunk_start(b, size), :].astype(BF)

        @pl.when(place < blocks // 2)
        def _():
            keep[chunk_start(place, size), :] = value

        @pl.when(place >= blocks // 2)
        def _():
            send[chunk_start(place - blocks // 2, size), :] = value

    repeat(blocks, block)


def row_sum(ref):
    return jnp.sum(ref[...].astype(F32), axis=0, keepdims=True)


def fc_weight_kernel(orders, left0, left1, right0, right1, *rest):
    *outs, sums, full = rest

    def block(i):
        cols = lanes(i, 256)
        full[pl.ds(pl.multiple_of(i * 256, 256), 256), :] = dot(
            left0[:, cols], right0[...], TN
        ) + dot(left1[:, cols], right1[...], TN)

    repeat(left0.shape[1] // 256, block)
    emit(full, outs, orders)
    sums[...] = row_sum(right0) + row_sum(right1)


def attn_weights_kernel(orders, ctx, og0, og1, rows_own, rows_far, pg, *rest):
    *outs, out_sum, qv_sum, full = rest
    half = og0.shape[0]
    side = lax.axis_index("mp") // 2
    width = ctx.shape[1]
    own, far = chunk_start(side, half), chunk_start(1 - side, half)

    def part(i):
        full[chunk_start(i, width), :] = dot(pg[i, own, :], rows_own[...], TN) + dot(
            pg[i, far, :], rows_far[...], TN
        )

    repeat(3, part)
    full[3 * width :, :] = dot(ctx[:half, :], og0[...], TN) + dot(ctx[half:, :], og1[...], TN)
    emit(full, outs, orders)
    out_sum[...] = row_sum(og0) + row_sum(og1)
    qv_sum[...] = jnp.concatenate(
        [jnp.sum(pg[part].astype(F32), axis=0, keepdims=True) for part in (0, 2)], axis=0
    )


def gather_blocks_kernel(orders, low_half, high_half, *rest):
    *outs, held, sems = rest
    blocks = 2 ** len(orders[0])
    size = 2 * low_half.shape[0] // blocks
    here = lax.axis_index("dp")
    copies, out, low = [], 0, 0
    for b in range(blocks):
        place = place_of(here ^ b, orders)
        at = chunk_start(place % (blocks // 2), size)
        value = jnp.where(place < blocks // 2, low_half[at, :], high_half[at, :])
        held[b * size : (b + 1) * size, :] = value.astype(F32)
        done = 0
        while done < size:
            count = min(size - done, outs[out].shape[0] - low)
            start = b * size + done
            copies.append(
                pltpu.make_async_copy(
                    held.at[start : start + count],
                    outs[out].at[low : low + count],
                    sems.at[len(copies)],
                )
            )
            copies[-1].start()
            done, low = done + count, low + count
            if low == outs[out].shape[0]:
                out, low = out + 1, 0
    for copy in copies:
        copy.wait()


def input_grad_kernel(x, mine, theirs, after_grad0, after_grad1, vectors, grad, sums):
    side = lax.axis_index("mp") // 2
    normed, inverse = norm(x[...].astype(F32))
    rows_grad = mine[...].astype(F32) + theirs[...].astype(F32)
    sums[...] = jnp.concatenate(
        [
            jnp.sum(rows_grad * normed, axis=0, keepdims=True),
            jnp.sum(rows_grad, axis=0, keepdims=True),
        ],
        axis=0,
    )
    after_grad = jnp.where(side == 0, after_grad0[...], after_grad1[...])
    value = after_grad + norm_back(
        rows_grad, vector(vectors, ATTN_GAIN), normed, inverse
    )
    grad[...] = value.astype(BF)


def text_out_kernel(mine0, mine1, theirs, after0, after1, vectors, out):
    side = lax.axis_index("mp") // 2
    after = jnp.where(side == 0, after0[...], after1[...])
    mine = jnp.where(side == 0, mine0[...], mine1[...])
    branch = mine.astype(F32) + theirs[...].astype(F32)
    out[...] = (after + (branch + vector(vectors, FC2_BIAS))).astype(BF)


def far_branch_kernel(br0, br1, far):
    far[...] = jnp.where(lax.axis_index("mp") // 2 == 0, br1[...], br0[...])


def add_rows_kernel(a, b, out):
    out[...] = a[...] + b[...]


def norm_sums_kernel(mlp0, mlp1, attn, out):
    out[0:2, :] = mlp0[...] + mlp1[...]
    out[2:4, :] = attn[...]


def small_kernel(sums, far, fc2, fc1, out_b, qv, out):
    width = qv.shape[1]
    out[0:2, :] = sums[0:2, :]
    out[2:4, :] = sums[2:4, :] + far[2:4, :]
    out[4:5, :] = fc2[...]
    out[5:6, :] = fc1[...]
    out[6:7, :] = out_b[...]
    out[7:8, :] = jnp.zeros((1, out.shape[1]), F32)
    out[7:8, :width] = qv[0:1, :]
    out[7:8, 2 * width : 3 * width] = qv[1:2, :]


def image_windows(count, images):
    windows = []
    per = 4
    for low in range(0, images, per):
        start = (low * IMG_SEQ + 15) // 16 * 16 if low else 0
        end = min(count, ((low + per) * IMG_SEQ + 15) // 16 * 16)
        if low + per >= images:
            end = count
        key_start = start // IMG_SEQ * IMG_SEQ // 16 * 16
        key_end = min(count, ((end - 1) // IMG_SEQ * IMG_SEQ + IMG_SEQ + 15) // 16 * 16)
        windows.append((start, end, key_start, key_end))
    return windows


def image_attn_kernel(first, x0, x1, vectors, *rest):
    if first:
        source, own_out, other_out, rows, qkv, context, total, weights, sem = rest
    else:
        own_before, other_before, source, keep, *sends, rows, qkv, context, total, weights, sem = rest
    count, dim = x0.shape
    images = count // IMG_SEQ
    width = dim // 4
    copy = pltpu.make_async_copy(source.at[0 : 4 * width + 16], weights, sem)
    copy.start()
    rows[:count, :] = x0.get()[...]
    rows[count:, :] = x1.get()[...]

    def normalize(c):
        at = chunk_start(c, count)
        normed, _ = norm(rows[at, :].astype(F32))
        rows[at, :] = (
            normed * vector(vectors, ATTN_GAIN) + vector(vectors, ATTN_SHIFT)
        ).astype(BF)

    repeat(2, normalize)
    windows = image_windows(count, images)
    copy.wait()
    bias = weights[4 * width : 4 * width + 16, :].astype(F32)
    bias_rows = (bias[0:1, :width], jnp.zeros((1, width), F32), bias[1:2, :width])

    def chunk(c):
        own = rows[chunk_start(c, count), :]
        for part in range(3):
            value = dot(own, weights[part * width : (part + 1) * width, :], NT)
            qkv[part] = (value + bias_rows[part]).astype(BF)
        for q_low, q_high, k_low, k_high in windows:
            extent = (q_high - q_low, k_high - k_low)
            q_image = (lax.broadcasted_iota(jnp.int32, extent, 0) + q_low) // IMG_SEQ
            k_image = (lax.broadcasted_iota(jnp.int32, extent, 1) + k_low) // IMG_SEQ
            mask = jnp.where(q_image == k_image, 1.0, 0.0)
            place = pl.ds(pl.multiple_of(c * count + q_low, 16), q_high - q_low)
            context[place, :] = attend(
                qkv[0, q_low:q_high, :], qkv[1, k_low:k_high, :], qkv[2, k_low:k_high, :], mask
            )

    def columns(i):
        cols = lanes(i, 256)
        total[:, cols] = dot(context[...], weights[3 * width : 4 * width, cols])

    repeat(2, chunk)
    repeat(dim // 256, columns)
    if first:
        own_out.held[...] = total[:count, :]
        own_out.start()
        other_out.held[...] = total[count:, :].astype(BF)
        other_out.start()
        return
    keep[...] = total[:count, :] + own_before.get()[...]
    put_pieces((total[count:, :] + other_before.get()[...].astype(F32)).astype(BF), sends)


def image_norm_kernel(x, keep, vectors, *rest):
    *others, after_out, rows = rest
    total = keep[...] + join_pieces(others).astype(F32)
    after = x[...].astype(F32) + (total + vector(vectors, OUT_BIAS))
    after_out.held[...] = after
    after_out.start()
    normed, _ = norm(after)
    rows[...] = (normed * vector(vectors, MLP_GAIN) + vector(vectors, MLP_SHIFT)).astype(BF)


def image_mlp_kernel(rows0, rows2, vectors, w1a, w2a, w1b, w2b, mine, far, rows, active, total):
    size, dim = rows0.shape
    rows[:size, :] = rows0[...]
    rows[size:, :] = rows2[...]
    for bias, w1, w2 in ((FC1_BIAS, w1a, w2a), (FC1_BIAS_OTHER, w1b, w2b)):
        w1 = w1.get()

        def units(i):
            cols = lanes(i, 256)
            hidden = dot(rows[...], w1[:, cols]) + vectors[bias : bias + 1, cols]
            active[:, cols] = gelu_parts(hidden)[0].astype(BF)

        repeat(w1.shape[1] // 256, units)
        w2 = w2.get()

        def columns(i):
            cols = lanes(i, 256)
            value = dot(active[...], w2[:, cols])
            total[:, cols] = value if bias == FC1_BIAS else total[:, cols] + value

        repeat(dim // 256, columns)
    mine[...] = total[:size, :].astype(BF)
    far[...] = total[size:, :].astype(BF)


def image_out_kernel(after, mine, theirs, vectors, out):
    branch = mine[...].astype(F32) + theirs[...].astype(F32)
    out[...] = (after[...] + (branch + vector(vectors, FC2_BIAS))).astype(BF)


def core_swap(x):
    return lax.ppermute(x, "mp", [(i, i ^ 1) for i in range(lax.axis_size("mp"))])


def side_swap(x):
    return lax.ppermute(x, "mp", [(i, i ^ 2) for i in range(lax.axis_size("mp"))])


def dp_swap(x, bits):
    n_dp, n_mp = lax.axis_size("dp"), lax.axis_size("mp")
    pairs = [
        (d * n_mp + m, (d ^ bits[m % 2]) * n_mp + m) for d in range(n_dp) for m in range(n_mp)
    ]
    return lax.ppermute(x, ("dp", "mp"), pairs)


def per_device(
    text_in,
    segment_ids,
    valid_lengths,
    text_grad,
    attn_gain,
    attn_shift,
    qkv_weight,
    qv_bias,
    out_weight,
    out_bias,
    mlp_gain,
    mlp_shift,
    fc1_weight,
    fc1_bias,
    fc2_weight,
    fc2_bias,
    images,
    img_attn_gain,
    img_attn_shift,
    img_qkv_weight,
    img_qv_bias,
    img_out_weight,
    img_out_bias,
    img_mlp_gain,
    img_mlp_shift,
    img_fc1_weight,
    img_fc1_bias,
    img_fc2_weight,
    img_fc2_bias,
):
    size, dim = text_in.shape
    row_count, length = segment_ids.shape
    width = qkv_weight.shape[2]
    n_dp = lax.axis_size("dp")
    tokens = 4 * size

    w_t = qkv_weight.transpose(1, 2, 0).reshape(3 * width, dim)
    img_w_t = img_qkv_weight.transpose(1, 2, 0).reshape(3 * width, dim)
    used = 4 * width + 16
    total_rows = -(-used // (16 * n_dp)) * 16 * n_dp
    part_rows = total_rows // n_dp

    rows_first = 2 * size // length
    blocks = row_blocks(row_count, length, rows_first)
    blocks_first = [b for b in blocks if b[0] < rows_first * length]
    blocks_rest = [b for b in blocks if b[0] >= rows_first * length]

    run = Line()
    chunk = shape(size, dim)
    pair = shape(2 * size, dim)

    x0 = text_in
    x2 = side_swap(x0)
    x1 = core_swap(x0)
    vectors, img_vectors = run(
        vectors_kernel,
        [shape(8, dim, dtype=F32)] * 2,
        [
            Late(v)
            for v in (
                attn_gain, attn_shift, out_bias, mlp_gain, mlp_shift, fc2_bias, fc1_bias,
                img_attn_gain, img_attn_shift, img_out_bias, img_mlp_gain, img_mlp_shift,
                img_fc2_bias, img_fc1_bias, core_swap(img_fc1_bias),
            )
        ],
    )
    project_scratch = [pltpu.VMEM((2, size, dim), BF), pltpu.VMEM((8, width), F32)]
    rows_own, qkv_own = run(
        own_rows_kernel,
        [Early(2 * size, dim), shape(3, 2 * size, width)],
        [x0, x1, vectors, w_t, qv_bias],
        scratch=project_scratch,
    )
    mask = run(
        functools.partial(mask_kernel, blocks),
        [shape(tokens, 2 * length, dtype=F32)],
        [segment_ids, valid_lengths],
        scalars=(1,),
    )
    bundle = run(
        bundle_kernel,
        [shape(total_rows, dim)],
        [img_w_t, img_out_weight, img_qv_bias],
        scratch=[
            pltpu.VMEM((total_rows - 4 * width, dim), BF),
            pltpu.SemaphoreType.DMA((3,)),
        ],
        untouched=(0, 1),
        outside=True,
    )
    t0 = text_grad
    t1 = core_swap(t0)
    packed = run(
        far_operands_kernel,
        [shape(size + part_rows, dim)],
        [t0, bundle],
        scratch=[pltpu.SemaphoreType.DMA(())],
        untouched=(1,),
        after=[x2],
    )
    x2 = run.hold(x2)
    x3 = core_swap(x2)
    packed = side_swap(packed)

    rows_far, qkv, ctx, x_mine, keep0, keep1, send0, send1 = run(
        functools.partial(attn_forward_kernel, blocks),
        [
            Early(2 * size, dim),
            Early(3, tokens, width),
            Early(tokens, width),
            Early(2, size, dim),
        ]
        + [chunk] * 4,
        [x0, x2, x3, qkv_own, vectors, w_t, qv_bias, out_weight, mask],
        scratch=project_scratch,
    )

    row_cuts, sum_cuts, *og_cuts = [pieces_of(size, n) for n in PIECES[:4]]

    def after_attn(half, mine, theirs):
        stream, rows, *sends = run(
            functools.partial(after_attn_kernel, half),
            [Early(size, dim, dtype=F32), chunk] + [shape(n, dim) for n in row_cuts],
            [x_mine, mine, theirs, vectors],
        )
        return stream, (rows, *map(core_swap, sends))

    def mlp(rows, grad):
        all_rows, act, hid_grad, br_keep, br_send, mg_keep, *mg_sends = run(
            functools.partial(mlp_kernel, len(rows) - 1),
            [Early(2 * size, dim)] * 3
            + [Early(size, dim)] * 2
            + [chunk]
            + [shape(n, dim) for n in sum_cuts],
            [*rows, grad, fc1_weight, vectors, fc2_weight],
        )
        partial = (mg_keep, *map(core_swap, mg_sends))
        return all_rows, act, hid_grad, (br_keep, core_swap(br_send)), partial

    def mlp_back(half, stream, mine, theirs, grad):
        value, low, sums, *sends = run(
            mlp_back_kernel,
            [Early(size, dim, dtype=F32), chunk, shape(2, dim, dtype=F32)]
            + [shape(n, dim) for n in og_cuts[half]],
            [stream, mine, theirs, grad, vectors],
        )
        return value, (low, *map(core_swap, sends)), sums

    other0, other1 = core_swap(send0), core_swap(send1)
    mine0 = run(add_kernel, [chunk], [keep0, other0], after=[packed])
    theirs0 = side_swap(mine0)
    far_part = run(unpack_kernel, [shape(part_rows, dim)], [packed])
    far_bundle = lax.all_gather(far_part, "dp", axis=0, tiled=True)

    image_rows = images.shape[0]
    image_chunk = shape(image_rows, dim)
    img_other = core_swap(images)
    img_w1_other, img_w2_other = core_swap(img_fc1_weight), core_swap(img_fc2_weight)
    image_scratch = [
        pltpu.VMEM((2 * image_rows, dim), BF),
        pltpu.VMEM((3, image_rows, width), BF),
        pltpu.VMEM((2 * image_rows, width), BF),
        pltpu.VMEM((2 * image_rows, dim), F32),
        pltpu.VMEM((used, dim), BF),
        pltpu.SemaphoreType.DMA(()),
    ]
    image_total = run(
        functools.partial(image_attn_kernel, True),
        [Early(image_rows, dim, dtype=F32), Early(image_rows, dim)],
        [Late(images), Late(img_other), img_vectors, Fixed(bundle)],
        scratch=image_scratch,
        after=[Fixed(img_w1_other)],
    )
    mine1 = run(add_kernel, [chunk], [keep1, other1], after=[theirs0])
    theirs1 = side_swap(mine1)
    stream0, rows0 = after_attn(0, mine0, theirs0)
    tg0, tg1 = run(
        arrange_kernel, [Early(2 * size, dim)] * 2, [t0, t1, packed, core_swap(packed)]
    )
    all_rows0, act0, hg0, branch0, partial0 = mlp(rows0, tg0)
    mg0 = run(add_pieces_kernel, [chunk], partial0, after=[theirs1, Fixed(img_w2_other)])
    mg_theirs0 = side_swap(mg0)
    stream1, rows1 = after_attn(1, mine1, theirs1)
    all_rows1, act1, hg1, branch1, partial1 = mlp(rows1, tg1)

    bits = [2**k for k in range(n_dp.bit_length() - 1)]
    along_x = tuple(bits)
    kinds = {
        "even": (along_x, along_x),
        "mixed": (along_x, tuple(bits[1:] + bits[:1])),
        "turned": (along_x, tuple(bits[1:2] + bits[:1] + bits[2:])),
    }
    plain = 2 ** len(bits) != n_dp or dim % (16 * n_dp) != 0
    fc2_order, fc1_order, qkv_order = [None if plain else kinds[name] for name in ORDERS]
    grad_shapes = [shape(dim, dim, dtype=F32)] if plain else [shape(dim // 2, dim)] * 2

    class Sum:
        def __init__(self, parts, orders, sizes):
            self.orders, self.sizes, self.step = orders, sizes, 0
            if plain:
                total = lax.psum(parts[0], "dp")
                cuts = [sum(sizes[: i + 1]) for i in range(len(sizes) - 1)]
                self.result = jnp.split(total, cuts, axis=0)
                return
            self.keep = parts[0]
            self.exchange(parts[1], 0)

        def exchange(self, send, k):
            self.arriving = dp_swap(send, (self.orders[0][k], self.orders[1][k]))

        def advance(self):
            if plain or self.step == 2 * len(bits):
                return
            self.step += 1
            rows, levels = self.keep.shape[0], len(bits)
            if self.step < levels:
                self.keep, send = run(
                    add_split_kernel, [shape(rows // 2, dim)] * 2, [self.keep, self.arriving]
                )
                self.exchange(send, self.step)
            elif self.step < 2 * levels:
                if self.step == levels:
                    self.keep = run(add_kernel, [shape(rows, dim)], [self.keep, self.arriving])
                else:
                    self.keep = run(
                        join_kernel, [shape(2 * rows, dim)], [self.keep, self.arriving]
                    )
                self.exchange(self.keep, 2 * levels - 1 - self.step)
            else:
                got = run(
                    functools.partial(gather_blocks_kernel, self.orders),
                    [Pinned(n, dim, dtype=F32) for n in self.sizes],
                    [self.keep, self.arriving],
                    scratch=[
                        pltpu.VMEM((dim, dim), F32),
                        pltpu.SemaphoreType.DMA((n_dp + len(self.sizes),)),
                    ],
                )
                self.result = got if len(self.sizes) > 1 else [got]

    def fc_weight(orders, args):
        *parts, sums = run(
            functools.partial(fc_weight_kernel, orders),
            grad_shapes + [shape(1, dim, dtype=F32)],
            args,
            scratch=[pltpu.VMEM((dim, dim), F32)],
        )
        return Sum(parts, orders, (dim,)), sums

    got = {}

    def fc2_weight():
        got["fc2"], got["fc2_bias"] = fc_weight(fc2_order, [act0, act1, tg0, tg1])

    def fc1_weight():
        got["fc1"], got["fc1_bias"] = fc_weight(fc1_order, [all_rows0, all_rows1, hg0, hg1])

    def mlp_sum():
        got["mg1"] = run(add_pieces_kernel, [chunk], partial1, after=[mg_theirs0])
        got["mg_theirs1"] = side_swap(got["mg1"])

    def mlp_back0():
        got["grad0"], got["og0"], got["sums0"] = mlp_back(0, stream0, mg0, mg_theirs0, tg0)

    def mlp_back1():
        got["grad1"], got["og1"], got["sums1"] = mlp_back(
            1, stream1, got["mg1"], got["mg_theirs1"], tg1
        )

    def attn_back0():
        og = got["og0"]
        got["first"] = run(
            functools.partial(attn_back_first_kernel, blocks_first, len(og) - 1),
            [pair, shape(2 * size, width), shape(3, rows_first * length, width)],
            [*og, qkv, mask, out_weight],
        )

    def attn_back1():
        og = got["og1"]
        got["og_second"], got["pg"], p0, p1, p2, p3 = run(
            functools.partial(attn_back_second_kernel, blocks_rest, len(og) - 1),
            [pair, shape(3, tokens, width)] + [chunk] * 4,
            [*og, *got["first"][1:], qkv, mask, out_weight, w_t],
            scratch=[pltpu.VMEM((tokens, width), BF)],
        )
        got["parts"] = [p0, core_swap(p1), p2, core_swap(p3)]

    def attn_weights():
        *parts, got["out_bias"], got["qv_bias"] = run(
            functools.partial(attn_weights_kernel, qkv_order),
            grad_shapes + [shape(1, dim, dtype=F32), shape(2, width, dtype=F32)],
            [ctx, got["first"][0], got["og_second"], rows_own, rows_far, got["pg"]],
            scratch=[pltpu.VMEM((dim, dim), F32)],
        )
        got["qkv"] = Sum(parts, qkv_order, (3 * width, width))

    image_cuts = pieces_of(image_rows, PIECES[4])

    def p_sums():
        got["p"], to_side = run(add_pair_kernel, [chunk] * 2, got["parts"])
        got["p_far"] = side_swap(to_side)

    def image_attn():
        got["img"], *sends = run(
            functools.partial(image_attn_kernel, False),
            [shape(image_rows, dim, dtype=F32)] + [shape(n, dim) for n in image_cuts],
            [
                Late(images), Late(img_other), img_vectors, *map(Late, image_total),
                Fixed(far_bundle),
            ],
            scratch=image_scratch,
            vmem=20,
        )
        got["img_others"] = [core_swap(part) for part in sends]

    def image_norm():
        got["img_after"], got["rows0"] = run(
            image_norm_kernel,
            [Early(image_rows, dim, dtype=F32), image_chunk],
            [images, got["img"], img_vectors, *got["img_others"]],
        )
        got["rows2"] = side_swap(got["rows0"])

    def image_mlp():
        got["img_mine"], far = run(
            image_mlp_kernel,
            [image_chunk] * 2,
            [
                got["rows0"], got["rows2"], img_vectors,
                Late(img_fc1_weight), Late(img_fc2_weight),
                Late(img_w1_other), Late(img_w2_other),
            ],
            scratch=[pltpu.VMEM((2 * image_rows, dim), BF)] * 2
            + [pltpu.VMEM((2 * image_rows, dim), F32)],
            vmem=24,
        )
        got["img_far"] = side_swap(far)

    def image_out():
        got["image_out"] = run(
            image_out_kernel,
            [image_chunk],
            [got["img_after"], got["img_mine"], got["img_far"], img_vectors],
        )

    def input_grad():
        got["input"], attn_sums = run(
            input_grad_kernel,
            [chunk, shape(2, dim, dtype=F32)],
            [text_in, got["p"], got["p_far"], got["grad0"], got["grad1"], vectors],
        )
        got["small"] = run(
            norm_sums_kernel, [shape(4, dim, dtype=F32)], [got["sums0"], got["sums1"], attn_sums]
        )
        got["small_far"] = core_swap(got["small"])

    def branch():
        br0, br1 = run(branch_sums_kernel, [Early(size, dim)] * 2, [*branch0, *branch1])
        far = run(far_branch_kernel, [chunk], [br0, br1])
        got["branch"] = (br0, br1, side_swap(far))

    def text_out():
        got["text_out"] = run(
            text_out_kernel, [chunk], [*got["branch"], stream0, stream1, vectors]
        )

    def small_near():
        got["small"] = run(
            add_rows_kernel, [shape(4, dim, dtype=F32)], [got["small"], got["small_far"]]
        )
        got["small_far"] = side_swap(got["small"])

    later = [] if plain else list(bits)

    def small_next():
        if later:
            bit = later.pop(0)
            got["small_far"] = dp_swap(got["small"], (bit, bit))

    def small_side():
        got["small"] = run(
            small_kernel,
            [shape(8, dim, dtype=F32)],
            [
                got["small"], got["small_far"],
                got["fc2_bias"], got["fc1_bias"], got["out_bias"], got["qv_bias"],
            ],
        )
        small_next()

    def small_dp():
        if not plain:
            got["small"] = run(
                add_rows_kernel, [shape(8, dim, dtype=F32)], [got["small"], got["small_far"]]
            )
            small_next()

    steps = dict(
        fc2_weight=fc2_weight, fc1_weight=fc1_weight, mlp_sum=mlp_sum,
        mlp_back0=mlp_back0, mlp_back1=mlp_back1, attn_back0=attn_back0, attn_back1=attn_back1,
        attn_weights=attn_weights,
        p_sums=p_sums, image_attn=image_attn, image_norm=image_norm, image_mlp=image_mlp,
        image_out=image_out, input=input_grad, branch=branch, text_out=text_out,
        small_near=small_near, small_side=small_side, small_dp=small_dp,
        fc1=lambda: got["fc1"].advance(),
        fc2=lambda: got["fc2"].advance(),
        qkv=lambda: got["qkv"].advance(),
    )
    for name in PLAN:
        steps[name]()
    small = lax.psum(got["small"], "dp") if plain else got["small"]
    (grad_fc2_weight,) = got["fc2"].result
    (grad_fc1_weight,) = got["fc1"].result
    grad_qkv, grad_out_weight = got["qkv"].result
    return (
        got["text_out"],
        got["image_out"],
        got["input"],
        small[2],
        small[3],
        grad_qkv.reshape(3, width, dim).transpose(2, 0, 1),
        jnp.stack([small[7, :width], small[7, 2 * width : 3 * width]]),
        grad_out_weight,
        small[6],
        small[0],
        small[1],
        grad_fc1_weight,
        small[5],
        grad_fc2_weight,
        small[4],
    )


def solution(mesh):
    in_specs = (
        P(("dp", "mp"), None),
        P("dp", None),
        P("dp"),
        P(("dp", "mp"), None),
        P(),
        P(),
        P(None, None, "mp"),
        P(None, "mp"),
        P("mp", None),
        P(),
        P(),
        P(),
        P(None, "mp"),
        P("mp"),
        P("mp", None),
        P(),
        P(("dp", "mp"), None),
        P(),
        P(),
        P(None, None, "mp"),
        P(None, "mp"),
        P("mp", None),
        P(),
        P(),
        P(),
        P(None, "mp"),
        P("mp"),
        P("mp", None),
        P(),
    )
    out_specs = (
        P(("dp", "mp"), None),
        P(("dp", "mp"), None),
        P(("dp", "mp"), None),
        P(),
        P(),
        P(None, None, "mp"),
        P(None, "mp"),
        P("mp", None),
        P(),
        P(),
        P(),
        P(None, "mp"),
        P("mp"),
        P("mp", None),
        P(),
    )
    return jax.shard_map(
        per_device, mesh=mesh, in_specs=in_specs, out_specs=out_specs, check_vma=False
    )
```

```python
import functools

import jax
import jax.numpy as jnp
from jax import lax
from jax.experimental import pallas as pl
from jax.experimental.pallas import tpu as pltpu
from jax.sharding import PartitionSpec as P

HEAD = 64
IMG_SEQ = 50
EPS = 1e-05
BF = jnp.bfloat16
F32 = jnp.float32
SCALE = HEAD ** (-0.5)
NEG = -1000000000.0
ROOT = 0.7978845608028654
CUBE = 0.044715

PLAN = (
    "fc2_weight", "mlp_sum", "mlp_back0", "fc1_weight", "fc2", "attn_back0", "mlp_back1",
    "attn_back1", "fc2", "fc1", "attn_weights", "p_sums", "image_attn", "fc1", "fc2", "qkv",
    "image_norm", "fc2", "fc1", "qkv", "branch", "input", "qkv", "fc2", "small_near", "image_mlp",
    "fc1", "text_out", "small_side", "qkv", "fc1", "fc2", "small_dp", "qkv", "fc1", "small_dp",
    "image_out", "qkv", "small_dp",
)

ORDERS = ("mixed", "even", "turned")
PIECES = (3, 2, 3, 3, 2)

NN = (((1,), (0,)), ((), ()))
NT = (((1,), (1,)), ((), ()))
TN = (((0,), (0,)), ((), ()))


def dot(a, b, dims=NN):
    return lax.dot_general(a, b, dims, preferred_element_type=F32)


def shape(*dims, dtype=BF):
    return jax.ShapeDtypeStruct(dims, dtype)


class Late:
    def __init__(self, value):
        self.value, self.shape, self.dtype = value, value.shape, value.dtype


class Fixed:
    def __init__(self, value):
        self.value, self.shape, self.dtype = value, value.shape, value.dtype


class Early:
    def __init__(self, *dims, dtype=BF):
        self.shape, self.dtype = dims, dtype


class Pinned(Early):
    pass


class Moving:
    def __init__(self, source, target, held, sem):
        self.held, self.shape = held, held.shape
        self.copy = pltpu.make_async_copy(source, target, sem)
        self.waits = False

    def start(self):
        self.copy.start()
        self.waits = True

    def get(self):
        if self.waits:
            self.copy.wait()
            self.waits = False
        return self.held


class Line:
    def __init__(self):
        self.token = None

    def __call__(self, body, outs, args, scratch=(), vmem=16, untouched=(), scalars=(), after=(),
                 same=None, outside=False):
        def place(a):
            if isinstance(a, (Late, Fixed)):
                return pltpu.with_memory_space_constraint(a.value, pltpu.HBM)
            return a

        kinds = list(args)
        real = len(kinds)
        values = [place(a) for a in kinds + list(after)]
        values += [] if self.token is None else [self.token]
        given = len(values)
        late = [i for i, a in enumerate(kinds) if isinstance(a, Late)]
        fixed = [i for i, a in enumerate(kinds) if isinstance(a, Fixed)]
        early = [i for i, o in enumerate(outs) if type(o) is Early]

        def in_space(i):
            if i >= real or i in untouched:
                return pl.ANY
            if i in late or i in fixed:
                return pltpu.HBM
            return pltpu.SMEM if i in scalars else pltpu.VMEM

        def out_space(i):
            if isinstance(outs[i], Early):
                return pltpu.HBM
            return pl.ANY if outside or same is not None else pltpu.VMEM

        moving = [kinds[i] for i in late] + [outs[i] for i in early]
        held = [pltpu.VMEM(m.shape, m.dtype) for m in moving]
        sems = [pltpu.SemaphoreType.DMA((len(held),))] if held else []
        first = given + len(outs) + 1

        def run(*refs):
            ins, results = list(refs[:real]), list(refs[given : given + len(outs)])
            places = refs[first : first + len(held)]
            for k, i in enumerate(late):
                ins[i] = Moving(ins[i], places[k], places[k], refs[-1].at[k])
                ins[i].start()
            for k, i in enumerate(early, len(late)):
                results[i] = Moving(places[k], results[i], places[k], refs[-1].at[k])
            body(*ins, *results, *refs[first + len(held) : len(refs) - len(sems)])
            for moved in [ins[i] for i in late] + [results[i] for i in early]:
                moved.get()

        results = pl.pallas_call(
            run,
            out_shape=(
                *(
                    pltpu.HBM(o.shape, o.dtype)
                    if isinstance(o, Early)
                    else jax.ShapeDtypeStruct(o.shape, o.dtype)
                    for i, o in enumerate(outs)
                ),
                shape(8, 128, dtype=F32),
            ),
            in_specs=[pl.BlockSpec(memory_space=in_space(i)) for i in range(given)],
            out_specs=tuple(
                [pl.BlockSpec(memory_space=out_space(i)) for i in range(len(outs))]
                + [pl.BlockSpec(memory_space=pl.ANY)]
            ),
            scratch_shapes=held + list(scratch) + sems,
            input_output_aliases={} if same is None else {same: 0},
            compiler_params=pltpu.CompilerParams(vmem_limit_bytes=vmem * 1024 * 1024),
            cost_estimate=pl.CostEstimate(flops=1, bytes_accessed=1, transcendentals=0),
        )(*values)
        self.token = results[-1]
        return results[:-1] if len(outs) > 1 else results[0]

    def hold(self, value, after=()):
        return self(lambda *refs: None, [shape(*value.shape, dtype=value.dtype)], [value],
                    untouched=(0,), same=0, after=after)


def norm(x):
    centred = x - jnp.mean(x, axis=-1, keepdims=True)
    inverse = lax.rsqrt(jnp.mean(centred * centred, axis=-1, keepdims=True) + EPS)
    return centred * inverse, inverse


def norm_back(upstream, gain, normed, inverse):
    scaled = upstream * gain
    first = jnp.mean(scaled, axis=-1, keepdims=True)
    second = jnp.mean(scaled * normed, axis=-1, keepdims=True)
    return inverse * (scaled - first - normed * second)


def head_marks(width, dtype):
    lane = lax.broadcasted_iota(jnp.int32, (1, width), 1) // HEAD
    return [jnp.where(lane == h, 1.0, 0.0).astype(dtype) for h in range(width // HEAD)]


def stack_heads(rows, marks):
    return jnp.concatenate([rows * mark for mark in marks], axis=0)


def fold_heads(stacked, count, marks):
    total = stacked[:count] * marks[0]
    for h in range(1, len(marks)):
        total += stacked[h * count : (h + 1) * count] * marks[h]
    return total


def masked_scores(q_stack, k, mask):
    raw = dot(q_stack, k, NT)
    heads = raw.shape[0] // mask.shape[0]
    raw = raw.reshape(heads, mask.shape[0], mask.shape[1])
    return jnp.where(mask[None] > 0, raw * SCALE, NEG)


def softmax_parts(scores):
    peak = jnp.max(scores, axis=-1, keepdims=True)
    weights = jnp.exp(scores - peak)
    return weights, jnp.sum(weights, axis=-1, keepdims=True)


def attend(q, k, v, mask):
    count = q.shape[0]
    scores = masked_scores(stack_heads(q, head_marks(q.shape[1], BF)), k, mask)
    weights, total = softmax_parts(scores)
    probs = (weights / total).astype(BF).reshape(-1, mask.shape[1])
    return fold_heads(dot(probs, v), count, head_marks(q.shape[1], F32)).astype(BF)


def attend_back(q, k, v, grad, mask):
    count = q.shape[0]
    low = head_marks(q.shape[1], BF)
    q_stack = stack_heads(q, low)
    g_stack = stack_heads(grad, low)
    weights, total = softmax_parts(masked_scores(q_stack, k, mask))
    probs = weights / total
    prob_grad = dot(g_stack, v, NT).reshape(probs.shape)
    centre = jnp.sum(prob_grad * probs, axis=-1, keepdims=True)
    score_grad = (probs * (prob_grad - centre)).astype(BF).reshape(-1, mask.shape[1])
    probs_low = probs.astype(BF).reshape(-1, mask.shape[1])
    v_grad = dot(probs_low, g_stack, TN)
    q_grad = fold_heads(dot(score_grad, k), count, head_marks(q.shape[1], F32)) * SCALE
    k_grad = dot(score_grad, q_stack, TN) * SCALE
    return q_grad.astype(BF), k_grad.astype(BF), v_grad.astype(BF)


def gelu_parts(v):
    square = v * v
    t = jnp.tanh(ROOT * (v + CUBE * (square * v)))
    half = 0.5 * (1.0 + t)
    slope = half + 0.5 * v * (1.0 - t * t) * (ROOT * (1.0 + 3.0 * CUBE * square))
    return v * half, slope


def repeat(count, body):
    def step(i, carry):
        body(i)
        return carry

    lax.fori_loop(0, count, step, 0)


def lanes(index, size):
    return pl.ds(pl.multiple_of(index * size, 128), size)


def pieces_of(count, parts):
    most = -(-count // (16 * parts)) * 16
    return [min(most, count - low) for low in range(0, count, most)]


def put_pieces(value, outs):
    low = 0
    for out in outs:
        out[...] = value[low : low + out.shape[0]]
        low += out.shape[0]


def join_pieces(refs):
    return jnp.concatenate([ref[...] for ref in refs], axis=0)


def chunk_start(index, size):
    return pl.ds(pl.multiple_of(index * size, 16), size)


def row_blocks(count, length, first):
    blocks = []
    for low, high in ((0, first), (first, count)):
        row = low
        if (high - low) % 2:
            blocks.append((row * length, length))
            row += 1
        while row < high:
            blocks.append((row * length, 2 * length))
            row += 2
    return blocks


def mask_kernel(blocks, segments, lengths, mask):
    length = segments.shape[1]
    square = (length, length)
    key = lax.broadcasted_iota(jnp.int32, square, 1)
    diagonal = key == lax.broadcasted_iota(jnp.int32, square, 0)
    mask[...] = jnp.zeros(mask.shape, F32)
    for start, count in blocks:
        for place in range(count // length):
            row = start // length + place
            along = jnp.broadcast_to(segments[row : row + 1, :].astype(F32), square)
            seen = (along == along.T) & ((key < lengths[row]) | diagonal)
            low = start + place * length
            mask[low : low + length, place * length : (place + 1) * length] = jnp.where(
                seen, 1.0, 0.0
            )


def bundle_kernel(w_t, out_w, qv, bundle, held, sems):
    width = qv.shape[1]
    held[...] = jnp.zeros(held.shape, held.dtype)
    held[0:2, :width] = qv[...]
    start, copies = 0, []
    for k, piece in enumerate((w_t, out_w, held)):
        rows = piece.shape[0]
        copies.append(pltpu.make_async_copy(piece, bundle.at[start : start + rows], sems.at[k]))
        copies[-1].start()
        start += rows
    for copy in copies:
        copy.wait()


ATTN_GAIN, ATTN_SHIFT, OUT_BIAS, MLP_GAIN, MLP_SHIFT, FC2_BIAS, FC1_BIAS, FC1_BIAS_OTHER = range(8)


def vectors_kernel(*refs):
    *items, text, image = refs
    for out, own in ((text, items[:7]), (image, items[7:])):
        out[...] = jnp.zeros(out.shape, F32)
        for k, item in enumerate(own):
            out[k : k + 1, :] = item.get()[...].astype(F32).reshape(1, -1)


def vector(vectors, index):
    return vectors[index : index + 1, :]


def project(x_pair, vectors, w_t, bias, rows_out, qkv, bias_rows, at):
    size = x_pair.shape[1]
    width = bias.shape[1]
    gain, shift = vector(vectors, ATTN_GAIN), vector(vectors, ATTN_SHIFT)
    bias_rows[...] = jnp.zeros(bias_rows.shape, F32)
    bias_rows[0:1, :] = bias[...].astype(F32)[0:1]
    bias_rows[2:3, :] = bias[...].astype(F32)[1:2]

    def normalize(i):
        normed, _ = norm(x_pair[i].astype(F32))
        rows[chunk_start(i, size), :] = (normed * gain + shift).astype(BF)

    def part(i):
        value = dot(rows[...], w_t[chunk_start(i, width), :], NT) + bias_rows[pl.ds(i, 1), :]
        qkv[i, at, :] = value.astype(BF)

    rows = rows_out.held
    repeat(2, normalize)
    rows_out.start()
    repeat(3, part)


def own_rows_kernel(x0, x1, vectors, w_t, bias, rows_out, qkv, x_pair, bias_rows):
    core = lax.axis_index("mp") % 2
    x_pair[core] = x0[...]
    x_pair[1 - core] = x1[...]
    project(x_pair, vectors, w_t, bias, rows_out, qkv, bias_rows, slice(None))


def far_operands_kernel(grad, bundle, packed, sem):
    size = grad.shape[0]
    part = packed.shape[0] - size
    copy = pltpu.make_async_copy(
        bundle.at[chunk_start(lax.axis_index("dp"), part)], packed.at[size:], sem
    )
    copy.start()
    packed[:size] = grad[...]
    copy.wait()


def unpack_kernel(packed, part):
    part[...] = packed[packed.shape[0] - part.shape[0] :]


def arrange_kernel(t0, t1, packed, packed_other, half0, half1):
    size = t0.shape[0]
    here = lax.axis_index("mp") // 2 == 0
    parts = ((slice(0, size), t0, packed), (slice(size, 2 * size), t1, packed_other))
    for at, own, far in parts:
        half0.held[at, :] = jnp.where(here, own[...], far[:size])
        half1.held[at, :] = jnp.where(here, far[:size], own[...])
    half0.start()
    half1.start()


def block_loop(blocks, body, unroll=False):
    if unroll:
        for start, tokens in blocks:
            body(pl.ds(start, tokens), tokens)
        return
    singles = [b for b in blocks if b[1] != blocks[-1][1]]
    pairs = [b[0] for b in blocks if b[1] == blocks[-1][1]]
    count = blocks[-1][1]
    for start, tokens in singles:
        body(pl.ds(start, tokens), tokens)

    def pair(i):
        start = pairs[0] + i * count
        for k in range(1, len(pairs)):
            gap = pairs[k] - pairs[k - 1] - count
            if gap:
                start = start + jnp.where(i >= k, gap, 0)
        body(pl.ds(pl.multiple_of(start, 16), count), count)

    repeat(len(pairs), pair)


def attn_forward_kernel(blocks, x0, x2, x3, qkv_own, vectors, w_t, bias, out_w, mask,
                        rows_out, qkv_out, ctx_out, x_mine, keep0, keep1, send0, send1,
                        x_pair, bias_rows):
    qkv, ctx = qkv_out.held, ctx_out.held
    me = lax.axis_index("mp")
    core, side = me % 2, me // 2
    size, dim = x2.shape
    x_pair[core] = x2[...]
    x_pair[1 - core] = x3[...]
    x_mine.held[side] = x0[...]
    x_mine.held[1 - side] = x2[...]
    x_mine.start()
    far = chunk_start(1 - side, 2 * size)
    project(x_pair, vectors, w_t, bias, rows_out, qkv, bias_rows, far)
    own = chunk_start(side, 2 * size)
    for part in range(3):
        qkv[part, own, :] = qkv_own[part]
    qkv_out.start()

    def block(at, count):
        ctx[at, :] = attend(qkv[0, at, :], qkv[1, at, :], qkv[2, at, :], mask[at, :count])

    block_loop(blocks, block, unroll=True)
    ctx_out.start()

    def columns(i):
        cols = lanes(i, 256)
        weight = out_w[:, cols]
        for half, (keep, send) in enumerate(((keep0, send0), (keep1, send1))):
            theirs = ctx[chunk_start(2 * half + 1 - core, size), :]
            send[:, cols] = dot(theirs, weight).astype(BF)
            mine = ctx[chunk_start(2 * half + core, size), :]
            keep[:, cols] = dot(mine, weight).astype(BF)

    repeat(dim // 256, columns)


def add_kernel(a, b, out):
    out[...] = (a[...].astype(F32) + b[...].astype(F32)).astype(BF)


def add_pieces_kernel(a, *rest):
    *pieces, out = rest
    out[...] = (a[...].astype(F32) + join_pieces(pieces).astype(F32)).astype(BF)


def branch_sums_kernel(keep0, other0, keep1, other1, mine0, mine1):
    for keep, other, mine in ((keep0, other0, mine0), (keep1, other1, mine1)):
        mine.held[...] = (keep[...].astype(F32) + other[...].astype(F32)).astype(BF)
        mine.start()


def add_pair_kernel(a0, b0, a1, b1, out0, out1):
    for a, b, out in ((a0, b0, out0), (a1, b1, out1)):
        out[...] = (a[...].astype(F32) + b[...].astype(F32)).astype(BF)


def add_split_kernel(a, b, keep, send):
    half = keep.shape[0]
    keep[...] = (a[:half].astype(F32) + b[:half].astype(F32)).astype(BF)
    send[...] = (a[half:].astype(F32) + b[half:].astype(F32)).astype(BF)


def join_kernel(a, b, out):
    half = a.shape[0]
    out[:half] = a[...]
    out[half:] = b[...]


def after_attn_kernel(half, x_mine, mine, theirs, vectors, after_out, rows, *pieces):
    total = mine[...].astype(F32) + theirs[...].astype(F32)
    stream = x_mine[half].astype(F32) + (total + vector(vectors, OUT_BIAS))
    after_out.held[...] = stream
    after_out.start()
    normed, _ = norm(stream)
    value = (normed * vector(vectors, MLP_GAIN) + vector(vectors, MLP_SHIFT)).astype(BF)
    rows[...] = value
    put_pieces(value, pieces)


def mlp_kernel(count, rows0, *rest):
    pieces, (grad, w1, vectors, w2), rest = rest[:count], rest[count : count + 4], rest[count + 4 :]
    rows_out, act_out, hg_out, br_keep, br_send, mg_keep, *mg_sends = rest
    size, dim = rows0.shape
    rows, act, hid_grad = rows_out.held, act_out.held, hg_out.held
    rows[:size, :] = rows0[...]
    rows[size:, :] = join_pieces(pieces)
    rows_out.start()
    grad = grad

    def units(i):
        cols = lanes(i, 256)
        hidden = dot(rows[...], w1[:, cols]) + vectors[FC1_BIAS : FC1_BIAS + 1, cols]
        active, slope = gelu_parts(hidden)
        act[:, cols] = active.astype(BF)
        active_grad = dot(grad[...], w2[cols, :], NT)
        hid_grad[:, cols] = (active_grad * slope).astype(BF)

    def columns(i):
        cols = lanes(i, 256)
        value = dot(hid_grad[...], w1[cols, :], NT).astype(BF)
        mg_keep[:, cols] = value[:size]
        low = size
        for send in mg_sends:
            send[:, cols] = value[low : low + send.shape[0]]
            low += send.shape[0]

    def branch_columns(i):
        cols = lanes(i, 256)
        value = dot(act[...], w2[:, cols]).astype(BF)
        br_keep.held[:, cols] = value[:size]
        br_send.held[:, cols] = value[size:]

    repeat(w1.shape[1] // 256, units)
    act_out.start()
    hg_out.start()
    repeat(dim // 256, branch_columns)
    br_keep.start()
    br_send.start()
    repeat(dim // 256, columns)


def mlp_back_kernel(after, mine, theirs, grad, vectors, ag_out, out_grad, sums, *pieces):
    size = mine.shape[0]
    rows_grad = mine[...].astype(F32) + theirs[...].astype(F32)
    normed, inverse = norm(after[...])
    sums[...] = jnp.concatenate(
        [
            jnp.sum(rows_grad * normed, axis=0, keepdims=True),
            jnp.sum(rows_grad, axis=0, keepdims=True),
        ],
        axis=0,
    )
    value = grad[:size, :].astype(F32) + norm_back(
        rows_grad, vector(vectors, MLP_GAIN), normed, inverse
    )
    ag_out.held[...] = value
    ag_out.start()
    low = value.astype(BF)
    out_grad[...] = low
    put_pieces(low, pieces)


def attn_back_first_kernel(blocks, count, og_mine, *rest):
    og_others, (qkv, mask, out_w, og, cg, pg) = rest[:count], rest[count:]
    core = lax.axis_index("mp") % 2
    size = og_mine.shape[0]
    og[chunk_start(core, size), :] = og_mine[...]
    og[chunk_start(1 - core, size), :] = join_pieces(og_others)
    cg[...] = dot(og[...], out_w[...], NT).astype(BF)
    qkv = qkv

    def block(at, count):
        grads = attend_back(
            qkv[0, at, :], qkv[1, at, :], qkv[2, at, :], cg[at, :], mask[at, :count]
        )
        for part in range(3):
            pg[part, at, :] = grads[part]

    block_loop(blocks, block)


def attn_back_second_kernel(blocks, count, og_mine, *rest):
    og_others, rest = rest[:count], rest[count:]
    cg_first, pg_first, qkv, mask, out_w, w_t, og, pg, p0, p1, p2, p3, cg = rest
    me = lax.axis_index("mp")
    core = me % 2
    size, dim = og_mine.shape
    width = out_w.shape[0]
    half = 2 * size
    done = pg_first.shape[1]
    og[chunk_start(core, size), :] = og_mine[...]
    og[chunk_start(1 - core, size), :] = join_pieces(og_others)
    cg[half:, :] = dot(og[...], out_w[...], NT).astype(BF)
    cg[:half, :] = cg_first[...]
    qkv = qkv
    for part in range(3):
        pg[part, :done, :] = pg_first[part]

    def block(at, count):
        grads = attend_back(
            qkv[0, at, :], qkv[1, at, :], qkv[2, at, :], cg[at, :], mask[at, :count]
        )
        for part in range(3):
            pg[part, at, :] = grads[part]

    block_loop(blocks, block, unroll=True)

    def columns(i):
        cols = lanes(i, 256)
        for j, out in ((3, p3), (1, p1), (2, p2), (0, p0)):
            at = chunk_start(me ^ j, size)
            total = dot(pg[0, at, :], w_t[:width, cols])
            for part in range(1, 3):
                total += dot(pg[part, at, :], w_t[part * width : (part + 1) * width, cols])
            out[:, cols] = total.astype(BF)

    repeat(dim // 256, columns)


def place_in(relative, order):
    place = 0
    for k, bit in enumerate(order):
        place = place + ((relative // bit) % 2) * 2 ** (len(order) - 1 - k)
    return place


def place_of(relative, orders):
    core = lax.axis_index("mp") % 2
    return jnp.where(core == 0, place_in(relative, orders[0]), place_in(relative, orders[1]))


def emit(full, outs, orders):
    if orders is None:
        outs[0][...] = full[...]
        return
    keep, send = outs
    blocks = 2 ** len(orders[0])
    size = full.shape[0] // blocks
    here = lax.axis_index("dp")

    def block(b):
        place = place_of(here ^ b, orders)
        value = full[chunk_start(b, size), :].astype(BF)

        @pl.when(place < blocks // 2)
        def _():
            keep[chunk_start(place, size), :] = value

        @pl.when(place >= blocks // 2)
        def _():
            send[chunk_start(place - blocks // 2, size), :] = value

    repeat(blocks, block)


def row_sum(ref):
    return jnp.sum(ref[...].astype(F32), axis=0, keepdims=True)


def fc_weight_kernel(orders, left0, left1, right0, right1, *rest):
    *outs, sums, full = rest

    def block(i):
        cols = lanes(i, 256)
        full[pl.ds(pl.multiple_of(i * 256, 256), 256), :] = dot(
            left0[:, cols], right0[...], TN
        ) + dot(left1[:, cols], right1[...], TN)

    repeat(left0.shape[1] // 256, block)
    emit(full, outs, orders)
    sums[...] = row_sum(right0) + row_sum(right1)


def attn_weights_kernel(orders, ctx, og0, og1, rows_own, rows_far, pg, *rest):
    *outs, out_sum, qv_sum, full = rest
    half = og0.shape[0]
    side = lax.axis_index("mp") // 2
    width = ctx.shape[1]
    own, far = chunk_start(side, half), chunk_start(1 - side, half)

    def part(i):
        full[chunk_start(i, width), :] = dot(pg[i, own, :], rows_own[...], TN) + dot(
            pg[i, far, :], rows_far[...], TN
        )

    repeat(3, part)
    full[3 * width :, :] = dot(ctx[:half, :], og0[...], TN) + dot(ctx[half:, :], og1[...], TN)
    emit(full, outs, orders)
    out_sum[...] = row_sum(og0) + row_sum(og1)
    qv_sum[...] = jnp.concatenate(
        [jnp.sum(pg[part].astype(F32), axis=0, keepdims=True) for part in (0, 2)], axis=0
    )


def gather_blocks_kernel(orders, low_half, high_half, *rest):
    *outs, held, sems = rest
    blocks = 2 ** len(orders[0])
    size = 2 * low_half.shape[0] // blocks
    here = lax.axis_index("dp")
    copies, out, low = [], 0, 0
    for b in range(blocks):
        place = place_of(here ^ b, orders)
        at = chunk_start(place % (blocks // 2), size)
        value = jnp.where(place < blocks // 2, low_half[at, :], high_half[at, :])
        held[b * size : (b + 1) * size, :] = value.astype(F32)
        done = 0
        while done < size:
            count = min(size - done, outs[out].shape[0] - low)
            start = b * size + done
            copies.append(
                pltpu.make_async_copy(
                    held.at[start : start + count],
                    outs[out].at[low : low + count],
                    sems.at[len(copies)],
                )
            )
            copies[-1].start()
            done, low = done + count, low + count
            if low == outs[out].shape[0]:
                out, low = out + 1, 0
    for copy in copies:
        copy.wait()


def input_grad_kernel(x, mine, theirs, after_grad0, after_grad1, vectors, grad, sums):
    side = lax.axis_index("mp") // 2
    normed, inverse = norm(x[...].astype(F32))
    rows_grad = mine[...].astype(F32) + theirs[...].astype(F32)
    sums[...] = jnp.concatenate(
        [
            jnp.sum(rows_grad * normed, axis=0, keepdims=True),
            jnp.sum(rows_grad, axis=0, keepdims=True),
        ],
        axis=0,
    )
    after_grad = jnp.where(side == 0, after_grad0[...], after_grad1[...])
    value = after_grad + norm_back(
        rows_grad, vector(vectors, ATTN_GAIN), normed, inverse
    )
    grad[...] = value.astype(BF)


def text_out_kernel(mine0, mine1, theirs, after0, after1, vectors, out):
    side = lax.axis_index("mp") // 2
    after = jnp.where(side == 0, after0[...], after1[...])
    mine = jnp.where(side == 0, mine0[...], mine1[...])
    branch = mine.astype(F32) + theirs[...].astype(F32)
    out[...] = (after + (branch + vector(vectors, FC2_BIAS))).astype(BF)


def far_branch_kernel(br0, br1, far):
    far[...] = jnp.where(lax.axis_index("mp") // 2 == 0, br1[...], br0[...])


def add_rows_kernel(a, b, out):
    out[...] = a[...] + b[...]


def norm_sums_kernel(mlp0, mlp1, attn, out):
    out[0:2, :] = mlp0[...] + mlp1[...]
    out[2:4, :] = attn[...]


def small_kernel(sums, far, fc2, fc1, out_b, qv, out):
    width = qv.shape[1]
    out[0:2, :] = sums[0:2, :]
    out[2:4, :] = sums[2:4, :] + far[2:4, :]
    out[4:5, :] = fc2[...]
    out[5:6, :] = fc1[...]
    out[6:7, :] = out_b[...]
    out[7:8, :] = jnp.zeros((1, out.shape[1]), F32)
    out[7:8, :width] = qv[0:1, :]
    out[7:8, 2 * width : 3 * width] = qv[1:2, :]


def image_windows(count, images):
    windows = []
    per = 4
    for low in range(0, images, per):
        start = (low * IMG_SEQ + 15) // 16 * 16 if low else 0
        end = min(count, ((low + per) * IMG_SEQ + 15) // 16 * 16)
        if low + per >= images:
            end = count
        key_start = start // IMG_SEQ * IMG_SEQ // 16 * 16
        key_end = min(count, ((end - 1) // IMG_SEQ * IMG_SEQ + IMG_SEQ + 15) // 16 * 16)
        windows.append((start, end, key_start, key_end))
    return windows


def image_attn_kernel(first, x0, x1, vectors, *rest):
    if first:
        source, own_out, other_out, rows, qkv, context, total, weights, sem = rest
    else:
        own_before, other_before, source, keep, *sends, rows, qkv, context, total, weights, sem = rest
    count, dim = x0.shape
    images = count // IMG_SEQ
    width = dim // 4
    copy = pltpu.make_async_copy(source.at[0 : 4 * width + 16], weights, sem)
    copy.start()
    rows[:count, :] = x0.get()[...]
    rows[count:, :] = x1.get()[...]

    def normalize(c):
        at = chunk_start(c, count)
        normed, _ = norm(rows[at, :].astype(F32))
        rows[at, :] = (
            normed * vector(vectors, ATTN_GAIN) + vector(vectors, ATTN_SHIFT)
        ).astype(BF)

    repeat(2, normalize)
    windows = image_windows(count, images)
    copy.wait()
    bias = weights[4 * width : 4 * width + 16, :].astype(F32)
    bias_rows = (bias[0:1, :width], jnp.zeros((1, width), F32), bias[1:2, :width])

    def chunk(c):
        own = rows[chunk_start(c, count), :]
        for part in range(3):
            value = dot(own, weights[part * width : (part + 1) * width, :], NT)
            qkv[part] = (value + bias_rows[part]).astype(BF)
        for q_low, q_high, k_low, k_high in windows:
            extent = (q_high - q_low, k_high - k_low)
            q_image = (lax.broadcasted_iota(jnp.int32, extent, 0) + q_low) // IMG_SEQ
            k_image = (lax.broadcasted_iota(jnp.int32, extent, 1) + k_low) // IMG_SEQ
            mask = jnp.where(q_image == k_image, 1.0, 0.0)
            place = pl.ds(pl.multiple_of(c * count + q_low, 16), q_high - q_low)
            context[place, :] = attend(
                qkv[0, q_low:q_high, :], qkv[1, k_low:k_high, :], qkv[2, k_low:k_high, :], mask
            )

    def columns(i):
        cols = lanes(i, 256)
        total[:, cols] = dot(context[...], weights[3 * width : 4 * width, cols])

    repeat(2, chunk)
    repeat(dim // 256, columns)
    if first:
        own_out.held[...] = total[:count, :]
        own_out.start()
        other_out.held[...] = total[count:, :].astype(BF)
        other_out.start()
        return
    keep[...] = total[:count, :] + own_before.get()[...]
    put_pieces((total[count:, :] + other_before.get()[...].astype(F32)).astype(BF), sends)


def image_norm_kernel(x, keep, vectors, *rest):
    *others, after_out, rows = rest
    total = keep[...] + join_pieces(others).astype(F32)
    after = x[...].astype(F32) + (total + vector(vectors, OUT_BIAS))
    after_out.held[...] = after
    after_out.start()
    normed, _ = norm(after)
    rows[...] = (normed * vector(vectors, MLP_GAIN) + vector(vectors, MLP_SHIFT)).astype(BF)


def image_mlp_kernel(rows0, rows2, vectors, w1a, w2a, w1b, w2b, mine, far, rows, active, total):
    size, dim = rows0.shape
    rows[:size, :] = rows0[...]
    rows[size:, :] = rows2[...]
    for bias, w1, w2 in ((FC1_BIAS, w1a, w2a), (FC1_BIAS_OTHER, w1b, w2b)):
        w1 = w1.get()

        def units(i):
            cols = lanes(i, 256)
            hidden = dot(rows[...], w1[:, cols]) + vectors[bias : bias + 1, cols]
            active[:, cols] = gelu_parts(hidden)[0].astype(BF)

        repeat(w1.shape[1] // 256, units)
        w2 = w2.get()

        def columns(i):
            cols = lanes(i, 256)
            value = dot(active[...], w2[:, cols])
            total[:, cols] = value if bias == FC1_BIAS else total[:, cols] + value

        repeat(dim // 256, columns)
    mine[...] = total[:size, :].astype(BF)
    far[...] = total[size:, :].astype(BF)


def image_out_kernel(after, mine, theirs, vectors, out):
    branch = mine[...].astype(F32) + theirs[...].astype(F32)
    out[...] = (after[...] + (branch + vector(vectors, FC2_BIAS))).astype(BF)


def core_swap(x):
    return lax.ppermute(x, "mp", [(i, i ^ 1) for i in range(lax.axis_size("mp"))])


def side_swap(x):
    return lax.ppermute(x, "mp", [(i, i ^ 2) for i in range(lax.axis_size("mp"))])


def dp_swap(x, bits):
    n_dp, n_mp = lax.axis_size("dp"), lax.axis_size("mp")
    pairs = [
        (d * n_mp + m, (d ^ bits[m % 2]) * n_mp + m) for d in range(n_dp) for m in range(n_mp)
    ]
    return lax.ppermute(x, ("dp", "mp"), pairs)


def per_device(
    text_in,
    segment_ids,
    valid_lengths,
    text_grad,
    attn_gain,
    attn_shift,
    qkv_weight,
    qv_bias,
    out_weight,
    out_bias,
    mlp_gain,
    mlp_shift,
    fc1_weight,
    fc1_bias,
    fc2_weight,
    fc2_bias,
    images,
    img_attn_gain,
    img_attn_shift,
    img_qkv_weight,
    img_qv_bias,
    img_out_weight,
    img_out_bias,
    img_mlp_gain,
    img_mlp_shift,
    img_fc1_weight,
    img_fc1_bias,
    img_fc2_weight,
    img_fc2_bias,
):
    size, dim = text_in.shape
    row_count, length = segment_ids.shape
    width = qkv_weight.shape[2]
    n_dp = lax.axis_size("dp")
    tokens = 4 * size

    w_t = qkv_weight.transpose(1, 2, 0).reshape(3 * width, dim)
    img_w_t = img_qkv_weight.transpose(1, 2, 0).reshape(3 * width, dim)
    used = 4 * width + 16
    total_rows = -(-used // (16 * n_dp)) * 16 * n_dp
    part_rows = total_rows // n_dp

    rows_first = 2 * size // length
    blocks = row_blocks(row_count, length, rows_first)
    blocks_first = [b for b in blocks if b[0] < rows_first * length]
    blocks_rest = [b for b in blocks if b[0] >= rows_first * length]

    run = Line()
    chunk = shape(size, dim)
    pair = shape(2 * size, dim)

    x0 = text_in
    x2 = side_swap(x0)
    x1 = core_swap(x0)
    vectors, img_vectors = run(
        vectors_kernel,
        [shape(8, dim, dtype=F32)] * 2,
        [
            Late(v)
            for v in (
                attn_gain, attn_shift, out_bias, mlp_gain, mlp_shift, fc2_bias, fc1_bias,
                img_attn_gain, img_attn_shift, img_out_bias, img_mlp_gain, img_mlp_shift,
                img_fc2_bias, img_fc1_bias, core_swap(img_fc1_bias),
            )
        ],
    )
    project_scratch = [pltpu.VMEM((2, size, dim), BF), pltpu.VMEM((8, width), F32)]
    rows_own, qkv_own = run(
        own_rows_kernel,
        [Early(2 * size, dim), shape(3, 2 * size, width)],
        [x0, x1, vectors, w_t, qv_bias],
        scratch=project_scratch,
    )
    mask = run(
        functools.partial(mask_kernel, blocks),
        [shape(tokens, 2 * length, dtype=F32)],
        [segment_ids, valid_lengths],
        scalars=(1,),
    )
    bundle = run(
        bundle_kernel,
        [shape(total_rows, dim)],
        [img_w_t, img_out_weight, img_qv_bias],
        scratch=[
            pltpu.VMEM((total_rows - 4 * width, dim), BF),
            pltpu.SemaphoreType.DMA((3,)),
        ],
        untouched=(0, 1),
        outside=True,
    )
    t0 = text_grad
    t1 = core_swap(t0)
    packed = run(
        far_operands_kernel,
        [shape(size + part_rows, dim)],
        [t0, bundle],
        scratch=[pltpu.SemaphoreType.DMA(())],
        untouched=(1,),
        after=[x2],
    )
    x2 = run.hold(x2)
    x3 = core_swap(x2)
    packed = side_swap(packed)

    rows_far, qkv, ctx, x_mine, keep0, keep1, send0, send1 = run(
        functools.partial(attn_forward_kernel, blocks),
        [
            Early(2 * size, dim),
            Early(3, tokens, width),
            Early(tokens, width),
            Early(2, size, dim),
        ]
        + [chunk] * 4,
        [x0, x2, x3, qkv_own, vectors, w_t, qv_bias, out_weight, mask],
        scratch=project_scratch,
    )

    row_cuts, sum_cuts, *og_cuts = [pieces_of(size, n) for n in PIECES[:4]]

    def after_attn(half, mine, theirs):
        stream, rows, *sends = run(
            functools.partial(after_attn_kernel, half),
            [Early(size, dim, dtype=F32), chunk] + [shape(n, dim) for n in row_cuts],
            [x_mine, mine, theirs, vectors],
        )
        return stream, (rows, *map(core_swap, sends))

    def mlp(rows, grad):
        all_rows, act, hid_grad, br_keep, br_send, mg_keep, *mg_sends = run(
            functools.partial(mlp_kernel, len(rows) - 1),
            [Early(2 * size, dim)] * 3
            + [Early(size, dim)] * 2
            + [chunk]
            + [shape(n, dim) for n in sum_cuts],
            [*rows, grad, fc1_weight, vectors, fc2_weight],
        )
        partial = (mg_keep, *map(core_swap, mg_sends))
        return all_rows, act, hid_grad, (br_keep, core_swap(br_send)), partial

    def mlp_back(half, stream, mine, theirs, grad):
        value, low, sums, *sends = run(
            mlp_back_kernel,
            [Early(size, dim, dtype=F32), chunk, shape(2, dim, dtype=F32)]
            + [shape(n, dim) for n in og_cuts[half]],
            [stream, mine, theirs, grad, vectors],
        )
        return value, (low, *map(core_swap, sends)), sums

    other0, other1 = core_swap(send0), core_swap(send1)
    mine0 = run(add_kernel, [chunk], [keep0, other0], after=[packed])
    theirs0 = side_swap(mine0)
    far_part = run(unpack_kernel, [shape(part_rows, dim)], [packed])
    far_bundle = lax.all_gather(far_part, "dp", axis=0, tiled=True)

    image_rows = images.shape[0]
    image_chunk = shape(image_rows, dim)
    img_other = core_swap(images)
    img_w1_other, img_w2_other = core_swap(img_fc1_weight), core_swap(img_fc2_weight)
    image_scratch = [
        pltpu.VMEM((2 * image_rows, dim), BF),
        pltpu.VMEM((3, image_rows, width), BF),
        pltpu.VMEM((2 * image_rows, width), BF),
        pltpu.VMEM((2 * image_rows, dim), F32),
        pltpu.VMEM((used, dim), BF),
        pltpu.SemaphoreType.DMA(()),
    ]
    image_total = run(
        functools.partial(image_attn_kernel, True),
        [Early(image_rows, dim, dtype=F32), Early(image_rows, dim)],
        [Late(images), Late(img_other), img_vectors, Fixed(bundle)],
        scratch=image_scratch,
        after=[Fixed(img_w1_other)],
    )
    mine1 = run(add_kernel, [chunk], [keep1, other1], after=[theirs0])
    theirs1 = side_swap(mine1)
    stream0, rows0 = after_attn(0, mine0, theirs0)
    tg0, tg1 = run(
        arrange_kernel, [Early(2 * size, dim)] * 2, [t0, t1, packed, core_swap(packed)]
    )
    all_rows0, act0, hg0, branch0, partial0 = mlp(rows0, tg0)
    mg0 = run(add_pieces_kernel, [chunk], partial0, after=[theirs1, Fixed(img_w2_other)])
    mg_theirs0 = side_swap(mg0)
    stream1, rows1 = after_attn(1, mine1, theirs1)
    all_rows1, act1, hg1, branch1, partial1 = mlp(rows1, tg1)

    bits = [2**k for k in range(n_dp.bit_length() - 1)]
    along_x = tuple(bits)
    kinds = {
        "even": (along_x, along_x),
        "mixed": (along_x, tuple(bits[1:] + bits[:1])),
        "turned": (along_x, tuple(bits[1:2] + bits[:1] + bits[2:])),
    }
    plain = 2 ** len(bits) != n_dp or dim % (16 * n_dp) != 0
    fc2_order, fc1_order, qkv_order = [None if plain else kinds[name] for name in ORDERS]
    grad_shapes = [shape(dim, dim, dtype=F32)] if plain else [shape(dim // 2, dim)] * 2

    class Sum:
        def __init__(self, parts, orders, sizes):
            self.orders, self.sizes, self.step = orders, sizes, 0
            if plain:
                total = lax.psum(parts[0], "dp")
                cuts = [sum(sizes[: i + 1]) for i in range(len(sizes) - 1)]
                self.result = jnp.split(total, cuts, axis=0)
                return
            self.keep = parts[0]
            self.exchange(parts[1], 0)

        def exchange(self, send, k):
            self.arriving = dp_swap(send, (self.orders[0][k], self.orders[1][k]))

        def advance(self):
            if plain or self.step == 2 * len(bits):
                return
            self.step += 1
            rows, levels = self.keep.shape[0], len(bits)
            if self.step < levels:
                self.keep, send = run(
                    add_split_kernel, [shape(rows // 2, dim)] * 2, [self.keep, self.arriving]
                )
                self.exchange(send, self.step)
            elif self.step < 2 * levels:
                if self.step == levels:
                    self.keep = run(add_kernel, [shape(rows, dim)], [self.keep, self.arriving])
                else:
                    self.keep = run(
                        join_kernel, [shape(2 * rows, dim)], [self.keep, self.arriving]
                    )
                self.exchange(self.keep, 2 * levels - 1 - self.step)
            else:
                got = run(
                    functools.partial(gather_blocks_kernel, self.orders),
                    [Pinned(n, dim, dtype=F32) for n in self.sizes],
                    [self.keep, self.arriving],
                    scratch=[
                        pltpu.VMEM((dim, dim), F32),
                        pltpu.SemaphoreType.DMA((n_dp + len(self.sizes),)),
                    ],
                )
                self.result = got if len(self.sizes) > 1 else [got]

    def fc_weight(orders, args):
        *parts, sums = run(
            functools.partial(fc_weight_kernel, orders),
            grad_shapes + [shape(1, dim, dtype=F32)],
            args,
            scratch=[pltpu.VMEM((dim, dim), F32)],
        )
        return Sum(parts, orders, (dim,)), sums

    got = {}

    def fc2_weight():
        got["fc2"], got["fc2_bias"] = fc_weight(fc2_order, [act0, act1, tg0, tg1])

    def fc1_weight():
        got["fc1"], got["fc1_bias"] = fc_weight(fc1_order, [all_rows0, all_rows1, hg0, hg1])

    def mlp_sum():
        got["mg1"] = run(add_pieces_kernel, [chunk], partial1, after=[mg_theirs0])
        got["mg_theirs1"] = side_swap(got["mg1"])

    def mlp_back0():
        got["grad0"], got["og0"], got["sums0"] = mlp_back(0, stream0, mg0, mg_theirs0, tg0)

    def mlp_back1():
        got["grad1"], got["og1"], got["sums1"] = mlp_back(
            1, stream1, got["mg1"], got["mg_theirs1"], tg1
        )

    def attn_back0():
        og = got["og0"]
        got["first"] = run(
            functools.partial(attn_back_first_kernel, blocks_first, len(og) - 1),
            [pair, shape(2 * size, width), shape(3, rows_first * length, width)],
            [*og, qkv, mask, out_weight],
        )

    def attn_back1():
        og = got["og1"]
        got["og_second"], got["pg"], p0, p1, p2, p3 = run(
            functools.partial(attn_back_second_kernel, blocks_rest, len(og) - 1),
            [pair, shape(3, tokens, width)] + [chunk] * 4,
            [*og, *got["first"][1:], qkv, mask, out_weight, w_t],
            scratch=[pltpu.VMEM((tokens, width), BF)],
        )
        got["parts"] = [p0, core_swap(p1), p2, core_swap(p3)]

    def attn_weights():
        *parts, got["out_bias"], got["qv_bias"] = run(
            functools.partial(attn_weights_kernel, qkv_order),
            grad_shapes + [shape(1, dim, dtype=F32), shape(2, width, dtype=F32)],
            [ctx, got["first"][0], got["og_second"], rows_own, rows_far, got["pg"]],
            scratch=[pltpu.VMEM((dim, dim), F32)],
        )
        got["qkv"] = Sum(parts, qkv_order, (3 * width, width))

    image_cuts = pieces_of(image_rows, PIECES[4])

    def p_sums():
        got["p"], to_side = run(add_pair_kernel, [chunk] * 2, got["parts"])
        got["p_far"] = side_swap(to_side)

    def image_attn():
        got["img"], *sends = run(
            functools.partial(image_attn_kernel, False),
            [shape(image_rows, dim, dtype=F32)] + [shape(n, dim) for n in image_cuts],
            [
                Late(images), Late(img_other), img_vectors, *map(Late, image_total),
                Fixed(far_bundle),
            ],
            scratch=image_scratch,
            vmem=20,
        )
        got["img_others"] = [core_swap(part) for part in sends]

    def image_norm():
        got["img_after"], got["rows0"] = run(
            image_norm_kernel,
            [Early(image_rows, dim, dtype=F32), image_chunk],
            [images, got["img"], img_vectors, *got["img_others"]],
        )
        got["rows2"] = side_swap(got["rows0"])

    def image_mlp():
        got["img_mine"], far = run(
            image_mlp_kernel,
            [image_chunk] * 2,
            [
                got["rows0"], got["rows2"], img_vectors,
                Late(img_fc1_weight), Late(img_fc2_weight),
                Late(img_w1_other), Late(img_w2_other),
            ],
            scratch=[pltpu.VMEM((2 * image_rows, dim), BF)] * 2
            + [pltpu.VMEM((2 * image_rows, dim), F32)],
            vmem=24,
        )
        got["img_far"] = side_swap(far)

    def image_out():
        got["image_out"] = run(
            image_out_kernel,
            [image_chunk],
            [got["img_after"], got["img_mine"], got["img_far"], img_vectors],
        )

    def input_grad():
        got["input"], attn_sums = run(
            input_grad_kernel,
            [chunk, shape(2, dim, dtype=F32)],
            [text_in, got["p"], got["p_far"], got["grad0"], got["grad1"], vectors],
        )
        got["small"] = run(
            norm_sums_kernel, [shape(4, dim, dtype=F32)], [got["sums0"], got["sums1"], attn_sums]
        )
        got["small_far"] = core_swap(got["small"])

    def branch():
        br0, br1 = run(branch_sums_kernel, [Early(size, dim)] * 2, [*branch0, *branch1])
        far = run(far_branch_kernel, [chunk], [br0, br1])
        got["branch"] = (br0, br1, side_swap(far))

    def text_out():
        got["text_out"] = run(
            text_out_kernel, [chunk], [*got["branch"], stream0, stream1, vectors]
        )

    def small_near():
        got["small"] = run(
            add_rows_kernel, [shape(4, dim, dtype=F32)], [got["small"], got["small_far"]]
        )
        got["small_far"] = side_swap(got["small"])

    later = [] if plain else list(bits)

    def small_next():
        if later:
            bit = later.pop(0)
            got["small_far"] = dp_swap(got["small"], (bit, bit))

    def small_side():
        got["small"] = run(
            small_kernel,
            [shape(8, dim, dtype=F32)],
            [
                got["small"], got["small_far"],
                got["fc2_bias"], got["fc1_bias"], got["out_bias"], got["qv_bias"],
            ],
        )
        small_next()

    def small_dp():
        if not plain:
            got["small"] = run(
                add_rows_kernel, [shape(8, dim, dtype=F32)], [got["small"], got["small_far"]]
            )
            small_next()

    steps = dict(
        fc2_weight=fc2_weight, fc1_weight=fc1_weight, mlp_sum=mlp_sum,
        mlp_back0=mlp_back0, mlp_back1=mlp_back1, attn_back0=attn_back0, attn_back1=attn_back1,
        attn_weights=attn_weights,
        p_sums=p_sums, image_attn=image_attn, image_norm=image_norm, image_mlp=image_mlp,
        image_out=image_out, input=input_grad, branch=branch, text_out=text_out,
        small_near=small_near, small_side=small_side, small_dp=small_dp,
        fc1=lambda: got["fc1"].advance(),
        fc2=lambda: got["fc2"].advance(),
        qkv=lambda: got["qkv"].advance(),
    )
    for name in PLAN:
        steps[name]()
    small = lax.psum(got["small"], "dp") if plain else got["small"]
    (grad_fc2_weight,) = got["fc2"].result
    (grad_fc1_weight,) = got["fc1"].result
    grad_qkv, grad_out_weight = got["qkv"].result
    return (
        got["text_out"],
        got["image_out"],
        got["input"],
        small[2],
        small[3],
        grad_qkv.reshape(3, width, dim).transpose(2, 0, 1),
        jnp.stack([small[7, :width], small[7, 2 * width : 3 * width]]),
        grad_out_weight,
        small[6],
        small[0],
        small[1],
        grad_fc1_weight,
        small[5],
        grad_fc2_weight,
        small[4],
    )


def solution(mesh):
    in_specs = (
        P(("dp", "mp"), None),
        P("dp", None),
        P("dp"),
        P(("dp", "mp"), None),
        P(),
        P(),
        P(None, None, "mp"),
        P(None, "mp"),
        P("mp", None),
        P(),
        P(),
        P(),
        P(None, "mp"),
        P("mp"),
        P("mp", None),
        P(),
        P(("dp", "mp"), None),
        P(),
        P(),
        P(None, None, "mp"),
        P(None, "mp"),
        P("mp", None),
        P(),
        P(),
        P(),
        P(None, "mp"),
        P("mp"),
        P("mp", None),
        P(),
    )
    out_specs = (
        P(("dp", "mp"), None),
        P(("dp", "mp"), None),
        P(("dp", "mp"), None),
        P(),
        P(),
        P(None, None, "mp"),
        P(None, "mp"),
        P("mp", None),
        P(),
        P(),
        P(),
        P(None, "mp"),
        P("mp"),
        P("mp", None),
        P(),
    )
    return jax.shard_map(
        per_device, mesh=mesh, in_specs=in_specs, out_specs=out_specs, check_vma=False
    )
```

```python
import functools

import jax
import jax.numpy as jnp
from jax import lax
from jax.experimental import pallas as pl
from jax.experimental.pallas import tpu as pltpu
from jax.sharding import PartitionSpec as P

HEAD = 64
IMG_SEQ = 50
EPS = 1e-05
BF = jnp.bfloat16
F32 = jnp.float32
SCALE = HEAD ** (-0.5)
NEG = -1000000000.0
ROOT = 0.7978845608028654
CUBE = 0.044715

PLAN = (
    "fc2_weight", "mlp_sum", "mlp_back0", "fc1_weight", "fc2", "attn_back0", "mlp_back1",
    "attn_back1", "fc2", "fc1", "attn_weights", "p_sums", "image_attn", "fc1", "fc2", "qkv",
    "image_norm", "fc2", "fc1", "branch", "qkv", "input", "qkv", "fc2", "small_near", "image_mlp",
    "fc1", "text_out", "small_side", "qkv", "fc1", "fc2", "small_dp", "qkv", "fc1", "small_dp",
    "image_out", "qkv", "small_dp",
)

ORDERS = ("mixed", "even", "turned")
PIECES = (3, 2, 3, 3, 2)

NN = (((1,), (0,)), ((), ()))
NT = (((1,), (1,)), ((), ()))
TN = (((0,), (0,)), ((), ()))


def dot(a, b, dims=NN):
    return lax.dot_general(a, b, dims, preferred_element_type=F32)


def shape(*dims, dtype=BF):
    return jax.ShapeDtypeStruct(dims, dtype)


class Late:
    def __init__(self, value):
        self.value, self.shape, self.dtype = value, value.shape, value.dtype


class Fixed:
    def __init__(self, value):
        self.value, self.shape, self.dtype = value, value.shape, value.dtype


class Early:
    def __init__(self, *dims, dtype=BF):
        self.shape, self.dtype = dims, dtype


class Pinned(Early):
    pass


class Moving:
    def __init__(self, source, target, held, sem):
        self.held, self.shape = held, held.shape
        self.copy = pltpu.make_async_copy(source, target, sem)
        self.waits = False

    def start(self):
        self.copy.start()
        self.waits = True

    def get(self):
        if self.waits:
            self.copy.wait()
            self.waits = False
        return self.held


class Line:
    def __init__(self):
        self.token = None

    def __call__(self, body, outs, args, scratch=(), vmem=16, untouched=(), scalars=(), after=(),
                 same=None, outside=False):
        def place(a):
            if isinstance(a, (Late, Fixed)):
                return pltpu.with_memory_space_constraint(a.value, pltpu.HBM)
            return a

        kinds = list(args)
        real = len(kinds)
        values = [place(a) for a in kinds + list(after)]
        values += [] if self.token is None else [self.token]
        given = len(values)
        late = [i for i, a in enumerate(kinds) if isinstance(a, Late)]
        fixed = [i for i, a in enumerate(kinds) if isinstance(a, Fixed)]
        early = [i for i, o in enumerate(outs) if type(o) is Early]

        def in_space(i):
            if i >= real or i in untouched:
                return pl.ANY
            if i in late or i in fixed:
                return pltpu.HBM
            return pltpu.SMEM if i in scalars else pltpu.VMEM

        def out_space(i):
            if isinstance(outs[i], Early):
                return pltpu.HBM
            return pl.ANY if outside or same is not None else pltpu.VMEM

        moving = [kinds[i] for i in late] + [outs[i] for i in early]
        held = [pltpu.VMEM(m.shape, m.dtype) for m in moving]
        sems = [pltpu.SemaphoreType.DMA((len(held),))] if held else []
        first = given + len(outs) + 1

        def run(*refs):
            ins, results = list(refs[:real]), list(refs[given : given + len(outs)])
            places = refs[first : first + len(held)]
            for k, i in enumerate(late):
                ins[i] = Moving(ins[i], places[k], places[k], refs[-1].at[k])
                ins[i].start()
            for k, i in enumerate(early, len(late)):
                results[i] = Moving(places[k], results[i], places[k], refs[-1].at[k])
            body(*ins, *results, *refs[first + len(held) : len(refs) - len(sems)])
            for moved in [ins[i] for i in late] + [results[i] for i in early]:
                moved.get()

        results = pl.pallas_call(
            run,
            out_shape=(
                *(
                    pltpu.HBM(o.shape, o.dtype)
                    if isinstance(o, Early)
                    else jax.ShapeDtypeStruct(o.shape, o.dtype)
                    for i, o in enumerate(outs)
                ),
                shape(8, 128, dtype=F32),
            ),
            in_specs=[pl.BlockSpec(memory_space=in_space(i)) for i in range(given)],
            out_specs=tuple(
                [pl.BlockSpec(memory_space=out_space(i)) for i in range(len(outs))]
                + [pl.BlockSpec(memory_space=pl.ANY)]
            ),
            scratch_shapes=held + list(scratch) + sems,
            input_output_aliases={} if same is None else {same: 0},
            compiler_params=pltpu.CompilerParams(vmem_limit_bytes=vmem * 1024 * 1024),
            cost_estimate=pl.CostEstimate(flops=1, bytes_accessed=1, transcendentals=0),
        )(*values)
        self.token = results[-1]
        return results[:-1] if len(outs) > 1 else results[0]

    def hold(self, value, after=()):
        return self(lambda *refs: None, [shape(*value.shape, dtype=value.dtype)], [value],
                    untouched=(0,), same=0, after=after)


def norm(x):
    centred = x - jnp.mean(x, axis=-1, keepdims=True)
    inverse = lax.rsqrt(jnp.mean(centred * centred, axis=-1, keepdims=True) + EPS)
    return centred * inverse, inverse


def norm_back(upstream, gain, normed, inverse):
    scaled = upstream * gain
    first = jnp.mean(scaled, axis=-1, keepdims=True)
    second = jnp.mean(scaled * normed, axis=-1, keepdims=True)
    return inverse * (scaled - first - normed * second)


def head_marks(width, dtype):
    lane = lax.broadcasted_iota(jnp.int32, (1, width), 1) // HEAD
    return [jnp.where(lane == h, 1.0, 0.0).astype(dtype) for h in range(width // HEAD)]


def stack_heads(rows, marks):
    return jnp.concatenate([rows * mark for mark in marks], axis=0)


def fold_heads(stacked, count, marks):
    total = stacked[:count] * marks[0]
    for h in range(1, len(marks)):
        total += stacked[h * count : (h + 1) * count] * marks[h]
    return total


def masked_scores(q_stack, k, mask):
    raw = dot(q_stack, k, NT)
    heads = raw.shape[0] // mask.shape[0]
    raw = raw.reshape(heads, mask.shape[0], mask.shape[1])
    return jnp.where(mask[None] > 0, raw * SCALE, NEG)


def softmax_parts(scores):
    peak = jnp.max(scores, axis=-1, keepdims=True)
    weights = jnp.exp(scores - peak)
    return weights, jnp.sum(weights, axis=-1, keepdims=True)


def attend(q, k, v, mask):
    count = q.shape[0]
    scores = masked_scores(stack_heads(q, head_marks(q.shape[1], BF)), k, mask)
    weights, total = softmax_parts(scores)
    probs = (weights / total).astype(BF).reshape(-1, mask.shape[1])
    return fold_heads(dot(probs, v), count, head_marks(q.shape[1], F32)).astype(BF)


def attend_back(q, k, v, grad, mask):
    count = q.shape[0]
    low = head_marks(q.shape[1], BF)
    q_stack = stack_heads(q, low)
    g_stack = stack_heads(grad, low)
    weights, total = softmax_parts(masked_scores(q_stack, k, mask))
    probs = weights / total
    prob_grad = dot(g_stack, v, NT).reshape(probs.shape)
    centre = jnp.sum(prob_grad * probs, axis=-1, keepdims=True)
    score_grad = (probs * (prob_grad - centre)).astype(BF).reshape(-1, mask.shape[1])
    probs_low = probs.astype(BF).reshape(-1, mask.shape[1])
    v_grad = dot(probs_low, g_stack, TN)
    q_grad = fold_heads(dot(score_grad, k), count, head_marks(q.shape[1], F32)) * SCALE
    k_grad = dot(score_grad, q_stack, TN) * SCALE
    return q_grad.astype(BF), k_grad.astype(BF), v_grad.astype(BF)


def gelu_parts(v):
    square = v * v
    t = jnp.tanh(ROOT * (v + CUBE * (square * v)))
    half = 0.5 * (1.0 + t)
    slope = half + 0.5 * v * (1.0 - t * t) * (ROOT * (1.0 + 3.0 * CUBE * square))
    return v * half, slope


def repeat(count, body):
    def step(i, carry):
        body(i)
        return carry

    lax.fori_loop(0, count, step, 0)


def lanes(index, size):
    return pl.ds(pl.multiple_of(index * size, 128), size)


def pieces_of(count, parts):
    most = -(-count // (16 * parts)) * 16
    return [min(most, count - low) for low in range(0, count, most)]


def put_pieces(value, outs):
    low = 0
    for out in outs:
        out[...] = value[low : low + out.shape[0]]
        low += out.shape[0]


def join_pieces(refs):
    return jnp.concatenate([ref[...] for ref in refs], axis=0)


def chunk_start(index, size):
    return pl.ds(pl.multiple_of(index * size, 16), size)


def row_blocks(count, length, first):
    blocks = []
    for low, high in ((0, first), (first, count)):
        row = low
        if (high - low) % 2:
            blocks.append((row * length, length))
            row += 1
        while row < high:
            blocks.append((row * length, 2 * length))
            row += 2
    return blocks


def mask_kernel(blocks, segments, lengths, mask):
    length = segments.shape[1]
    square = (length, length)
    key = lax.broadcasted_iota(jnp.int32, square, 1)
    diagonal = key == lax.broadcasted_iota(jnp.int32, square, 0)
    mask[...] = jnp.zeros(mask.shape, F32)
    for start, count in blocks:
        for place in range(count // length):
            row = start // length + place
            along = jnp.broadcast_to(segments[row : row + 1, :].astype(F32), square)
            seen = (along == along.T) & ((key < lengths[row]) | diagonal)
            low = start + place * length
            mask[low : low + length, place * length : (place + 1) * length] = jnp.where(
                seen, 1.0, 0.0
            )


def bundle_kernel(w_t, out_w, qv, bundle, held, sems):
    width = qv.shape[1]
    held[...] = jnp.zeros(held.shape, held.dtype)
    held[0:2, :width] = qv[...]
    start, copies = 0, []
    for k, piece in enumerate((w_t, out_w, held)):
        rows = piece.shape[0]
        copies.append(pltpu.make_async_copy(piece, bundle.at[start : start + rows], sems.at[k]))
        copies[-1].start()
        start += rows
    for copy in copies:
        copy.wait()


ATTN_GAIN, ATTN_SHIFT, OUT_BIAS, MLP_GAIN, MLP_SHIFT, FC2_BIAS, FC1_BIAS, FC1_BIAS_OTHER = range(8)


def vectors_kernel(*refs):
    *items, text, image = refs
    for out, own in ((text, items[:7]), (image, items[7:])):
        out[...] = jnp.zeros(out.shape, F32)
        for k, item in enumerate(own):
            out[k : k + 1, :] = item.get()[...].astype(F32).reshape(1, -1)


def vector(vectors, index):
    return vectors[index : index + 1, :]


def project(x_pair, vectors, w_t, bias, rows_out, qkv, bias_rows, at):
    size = x_pair.shape[1]
    width = bias.shape[1]
    gain, shift = vector(vectors, ATTN_GAIN), vector(vectors, ATTN_SHIFT)
    bias_rows[...] = jnp.zeros(bias_rows.shape, F32)
    bias_rows[0:1, :] = bias[...].astype(F32)[0:1]
    bias_rows[2:3, :] = bias[...].astype(F32)[1:2]

    def normalize(i):
        normed, _ = norm(x_pair[i].astype(F32))
        rows[chunk_start(i, size), :] = (normed * gain + shift).astype(BF)

    def part(i):
        value = dot(rows[...], w_t[chunk_start(i, width), :], NT) + bias_rows[pl.ds(i, 1), :]
        qkv[i, at, :] = value.astype(BF)

    rows = rows_out.held
    repeat(2, normalize)
    rows_out.start()
    repeat(3, part)


def own_rows_kernel(x0, x1, vectors, w_t, bias, rows_out, qkv, x_pair, bias_rows):
    core = lax.axis_index("mp") % 2
    x_pair[core] = x0[...]
    x_pair[1 - core] = x1[...]
    project(x_pair, vectors, w_t, bias, rows_out, qkv, bias_rows, slice(None))


def far_operands_kernel(grad, bundle, packed, sem):
    size = grad.shape[0]
    part = packed.shape[0] - size
    copy = pltpu.make_async_copy(
        bundle.at[chunk_start(lax.axis_index("dp"), part)], packed.at[size:], sem
    )
    copy.start()
    packed[:size] = grad[...]
    copy.wait()


def unpack_kernel(packed, part):
    part[...] = packed[packed.shape[0] - part.shape[0] :]


def arrange_kernel(t0, t1, packed, packed_other, half0, half1):
    size = t0.shape[0]
    here = lax.axis_index("mp") // 2 == 0
    parts = ((slice(0, size), t0, packed), (slice(size, 2 * size), t1, packed_other))
    for at, own, far in parts:
        half0.held[at, :] = jnp.where(here, own[...], far[:size])
        half1.held[at, :] = jnp.where(here, far[:size], own[...])
    half0.start()
    half1.start()


def block_loop(blocks, body, unroll=False):
    if unroll:
        for start, tokens in blocks:
            body(pl.ds(start, tokens), tokens)
        return
    singles = [b for b in blocks if b[1] != blocks[-1][1]]
    pairs = [b[0] for b in blocks if b[1] == blocks[-1][1]]
    count = blocks[-1][1]
    for start, tokens in singles:
        body(pl.ds(start, tokens), tokens)

    def pair(i):
        start = pairs[0] + i * count
        for k in range(1, len(pairs)):
            gap = pairs[k] - pairs[k - 1] - count
            if gap:
                start = start + jnp.where(i >= k, gap, 0)
        body(pl.ds(pl.multiple_of(start, 16), count), count)

    repeat(len(pairs), pair)


def attn_forward_kernel(blocks, x0, x2, x3, qkv_own, vectors, w_t, bias, out_w, mask,
                        rows_out, qkv_out, ctx_out, x_mine, keep0, keep1, send0, send1,
                        x_pair, bias_rows):
    qkv, ctx = qkv_out.held, ctx_out.held
    me = lax.axis_index("mp")
    core, side = me % 2, me // 2
    size, dim = x2.shape
    x_pair[core] = x2[...]
    x_pair[1 - core] = x3[...]
    x_mine.held[side] = x0[...]
    x_mine.held[1 - side] = x2[...]
    x_mine.start()
    far = chunk_start(1 - side, 2 * size)
    project(x_pair, vectors, w_t, bias, rows_out, qkv, bias_rows, far)
    own = chunk_start(side, 2 * size)
    for part in range(3):
        qkv[part, own, :] = qkv_own[part]
    qkv_out.start()

    def block(at, count):
        ctx[at, :] = attend(qkv[0, at, :], qkv[1, at, :], qkv[2, at, :], mask[at, :count])

    block_loop(blocks, block, unroll=True)
    ctx_out.start()

    def columns(i):
        cols = lanes(i, 256)
        weight = out_w[:, cols]
        for half, (keep, send) in enumerate(((keep0, send0), (keep1, send1))):
            theirs = ctx[chunk_start(2 * half + 1 - core, size), :]
            send[:, cols] = dot(theirs, weight).astype(BF)
            mine = ctx[chunk_start(2 * half + core, size), :]
            keep[:, cols] = dot(mine, weight).astype(BF)

    repeat(dim // 256, columns)


def add_kernel(a, b, out):
    out[...] = (a[...].astype(F32) + b[...].astype(F32)).astype(BF)


def add_pieces_kernel(a, *rest):
    *pieces, out = rest
    out[...] = (a[...].astype(F32) + join_pieces(pieces).astype(F32)).astype(BF)


def branch_sums_kernel(keep0, other0, keep1, other1, mine0, mine1):
    for keep, other, mine in ((keep0, other0, mine0), (keep1, other1, mine1)):
        mine.held[...] = (keep[...].astype(F32) + other[...].astype(F32)).astype(BF)
        mine.start()


def add_pair_kernel(a0, b0, a1, b1, out0, out1):
    for a, b, out in ((a0, b0, out0), (a1, b1, out1)):
        out[...] = (a[...].astype(F32) + b[...].astype(F32)).astype(BF)


def add_split_kernel(a, b, keep, send):
    half = keep.shape[0]
    keep[...] = (a[:half].astype(F32) + b[:half].astype(F32)).astype(BF)
    send[...] = (a[half:].astype(F32) + b[half:].astype(F32)).astype(BF)


def join_kernel(a, b, out):
    half = a.shape[0]
    out[:half] = a[...]
    out[half:] = b[...]


def after_attn_kernel(half, x_mine, mine, theirs, vectors, after_out, rows, *pieces):
    total = mine[...].astype(F32) + theirs[...].astype(F32)
    stream = x_mine[half].astype(F32) + (total + vector(vectors, OUT_BIAS))
    after_out.held[...] = stream
    after_out.start()
    normed, _ = norm(stream)
    value = (normed * vector(vectors, MLP_GAIN) + vector(vectors, MLP_SHIFT)).astype(BF)
    rows[...] = value
    put_pieces(value, pieces)


def mlp_kernel(count, rows0, *rest):
    pieces, (grad, w1, vectors, w2), rest = rest[:count], rest[count : count + 4], rest[count + 4 :]
    rows_out, act_out, hg_out, br_keep, br_send, mg_keep, *mg_sends = rest
    size, dim = rows0.shape
    rows, act, hid_grad = rows_out.held, act_out.held, hg_out.held
    rows[:size, :] = rows0[...]
    rows[size:, :] = join_pieces(pieces)
    rows_out.start()
    grad = grad

    def units(i):
        cols = lanes(i, 256)
        hidden = dot(rows[...], w1[:, cols]) + vectors[FC1_BIAS : FC1_BIAS + 1, cols]
        active, slope = gelu_parts(hidden)
        act[:, cols] = active.astype(BF)
        active_grad = dot(grad[...], w2[cols, :], NT)
        hid_grad[:, cols] = (active_grad * slope).astype(BF)

    def columns(i):
        cols = lanes(i, 256)
        value = dot(hid_grad[...], w1[cols, :], NT).astype(BF)
        mg_keep[:, cols] = value[:size]
        low = size
        for send in mg_sends:
            send[:, cols] = value[low : low + send.shape[0]]
            low += send.shape[0]

    def branch_columns(i):
        cols = lanes(i, 256)
        value = dot(act[...], w2[:, cols]).astype(BF)
        br_keep.held[:, cols] = value[:size]
        br_send.held[:, cols] = value[size:]

    repeat(w1.shape[1] // 256, units)
    act_out.start()
    hg_out.start()
    repeat(dim // 256, branch_columns)
    br_keep.start()
    br_send.start()
    repeat(dim // 256, columns)


def mlp_back_kernel(after, mine, theirs, grad, vectors, ag_out, out_grad, sums, *pieces):
    size = mine.shape[0]
    rows_grad = mine[...].astype(F32) + theirs[...].astype(F32)
    normed, inverse = norm(after[...])
    sums[...] = jnp.concatenate(
        [
            jnp.sum(rows_grad * normed, axis=0, keepdims=True),
            jnp.sum(rows_grad, axis=0, keepdims=True),
        ],
        axis=0,
    )
    value = grad[:size, :].astype(F32) + norm_back(
        rows_grad, vector(vectors, MLP_GAIN), normed, inverse
    )
    ag_out.held[...] = value
    ag_out.start()
    low = value.astype(BF)
    out_grad[...] = low
    put_pieces(low, pieces)


def attn_back_first_kernel(blocks, count, og_mine, *rest):
    og_others, (qkv, mask, out_w, og, cg, pg) = rest[:count], rest[count:]
    core = lax.axis_index("mp") % 2
    size = og_mine.shape[0]
    og[chunk_start(core, size), :] = og_mine[...]
    og[chunk_start(1 - core, size), :] = join_pieces(og_others)
    cg[...] = dot(og[...], out_w[...], NT).astype(BF)
    qkv = qkv

    def block(at, count):
        grads = attend_back(
            qkv[0, at, :], qkv[1, at, :], qkv[2, at, :], cg[at, :], mask[at, :count]
        )
        for part in range(3):
            pg[part, at, :] = grads[part]

    block_loop(blocks, block)


def attn_back_second_kernel(blocks, count, og_mine, *rest):
    og_others, rest = rest[:count], rest[count:]
    cg_first, pg_first, qkv, mask, out_w, w_t, og, pg, p0, p1, p2, p3, cg = rest
    me = lax.axis_index("mp")
    core = me % 2
    size, dim = og_mine.shape
    width = out_w.shape[0]
    half = 2 * size
    done = pg_first.shape[1]
    og[chunk_start(core, size), :] = og_mine[...]
    og[chunk_start(1 - core, size), :] = join_pieces(og_others)
    cg[half:, :] = dot(og[...], out_w[...], NT).astype(BF)
    cg[:half, :] = cg_first[...]
    qkv = qkv
    for part in range(3):
        pg[part, :done, :] = pg_first[part]

    def block(at, count):
        grads = attend_back(
            qkv[0, at, :], qkv[1, at, :], qkv[2, at, :], cg[at, :], mask[at, :count]
        )
        for part in range(3):
            pg[part, at, :] = grads[part]

    block_loop(blocks, block, unroll=True)

    def columns(i):
        cols = lanes(i, 256)
        for j, out in ((3, p3), (1, p1), (2, p2), (0, p0)):
            at = chunk_start(me ^ j, size)
            total = dot(pg[0, at, :], w_t[:width, cols])
            for part in range(1, 3):
                total += dot(pg[part, at, :], w_t[part * width : (part + 1) * width, cols])
            out[:, cols] = total.astype(BF)

    repeat(dim // 256, columns)


def place_in(relative, order):
    place = 0
    for k, bit in enumerate(order):
        place = place + ((relative // bit) % 2) * 2 ** (len(order) - 1 - k)
    return place


def place_of(relative, orders):
    core = lax.axis_index("mp") % 2
    return jnp.where(core == 0, place_in(relative, orders[0]), place_in(relative, orders[1]))


def emit(full, outs, orders):
    if orders is None:
        outs[0][...] = full[...]
        return
    keep, send = outs
    blocks = 2 ** len(orders[0])
    size = full.shape[0] // blocks
    here = lax.axis_index("dp")

    def block(b):
        place = place_of(here ^ b, orders)
        value = full[chunk_start(b, size), :].astype(BF)

        @pl.when(place < blocks // 2)
        def _():
            keep[chunk_start(place, size), :] = value

        @pl.when(place >= blocks // 2)
        def _():
            send[chunk_start(place - blocks // 2, size), :] = value

    repeat(blocks, block)


def row_sum(ref):
    return jnp.sum(ref[...].astype(F32), axis=0, keepdims=True)


def fc_weight_kernel(orders, left0, left1, right0, right1, *rest):
    *outs, sums, full = rest

    def block(i):
        cols = lanes(i, 256)
        full[pl.ds(pl.multiple_of(i * 256, 256), 256), :] = dot(
            left0[:, cols], right0[...], TN
        ) + dot(left1[:, cols], right1[...], TN)

    repeat(left0.shape[1] // 256, block)
    emit(full, outs, orders)
    sums[...] = row_sum(right0) + row_sum(right1)


def attn_weights_kernel(orders, ctx, og0, og1, rows_own, rows_far, pg, *rest):
    *outs, out_sum, qv_sum, full = rest
    half = og0.shape[0]
    side = lax.axis_index("mp") // 2
    width = ctx.shape[1]
    own, far = chunk_start(side, half), chunk_start(1 - side, half)

    def part(i):
        full[chunk_start(i, width), :] = dot(pg[i, own, :], rows_own[...], TN) + dot(
            pg[i, far, :], rows_far[...], TN
        )

    repeat(3, part)
    full[3 * width :, :] = dot(ctx[:half, :], og0[...], TN) + dot(ctx[half:, :], og1[...], TN)
    emit(full, outs, orders)
    out_sum[...] = row_sum(og0) + row_sum(og1)
    qv_sum[...] = jnp.concatenate(
        [jnp.sum(pg[part].astype(F32), axis=0, keepdims=True) for part in (0, 2)], axis=0
    )


def gather_blocks_kernel(orders, low_half, high_half, *rest):
    *outs, held, sems = rest
    blocks = 2 ** len(orders[0])
    size = 2 * low_half.shape[0] // blocks
    here = lax.axis_index("dp")
    copies, out, low = [], 0, 0
    for b in range(blocks):
        place = place_of(here ^ b, orders)
        at = chunk_start(place % (blocks // 2), size)
        value = jnp.where(place < blocks // 2, low_half[at, :], high_half[at, :])
        held[b * size : (b + 1) * size, :] = value.astype(F32)
        done = 0
        while done < size:
            count = min(size - done, outs[out].shape[0] - low)
            start = b * size + done
            copies.append(
                pltpu.make_async_copy(
                    held.at[start : start + count],
                    outs[out].at[low : low + count],
                    sems.at[len(copies)],
                )
            )
            copies[-1].start()
            done, low = done + count, low + count
            if low == outs[out].shape[0]:
                out, low = out + 1, 0
    for copy in copies:
        copy.wait()


def input_grad_kernel(x, mine, theirs, after_grad0, after_grad1, vectors, grad, sums):
    side = lax.axis_index("mp") // 2
    normed, inverse = norm(x[...].astype(F32))
    rows_grad = mine[...].astype(F32) + theirs[...].astype(F32)
    sums[...] = jnp.concatenate(
        [
            jnp.sum(rows_grad * normed, axis=0, keepdims=True),
            jnp.sum(rows_grad, axis=0, keepdims=True),
        ],
        axis=0,
    )
    after_grad = jnp.where(side == 0, after_grad0[...], after_grad1[...])
    value = after_grad + norm_back(
        rows_grad, vector(vectors, ATTN_GAIN), normed, inverse
    )
    grad[...] = value.astype(BF)


def text_out_kernel(mine0, mine1, theirs, after0, after1, vectors, out):
    side = lax.axis_index("mp") // 2
    after = jnp.where(side == 0, after0[...], after1[...])
    mine = jnp.where(side == 0, mine0[...], mine1[...])
    branch = mine.astype(F32) + theirs[...].astype(F32)
    out[...] = (after + (branch + vector(vectors, FC2_BIAS))).astype(BF)


def far_branch_kernel(br0, br1, far):
    far[...] = jnp.where(lax.axis_index("mp") // 2 == 0, br1[...], br0[...])


def add_rows_kernel(a, b, out):
    out[...] = a[...] + b[...]


def norm_sums_kernel(mlp0, mlp1, attn, out):
    out[0:2, :] = mlp0[...] + mlp1[...]
    out[2:4, :] = attn[...]


def small_kernel(sums, far, fc2, fc1, out_b, qv, out):
    width = qv.shape[1]
    out[0:2, :] = sums[0:2, :]
    out[2:4, :] = sums[2:4, :] + far[2:4, :]
    out[4:5, :] = fc2[...]
    out[5:6, :] = fc1[...]
    out[6:7, :] = out_b[...]
    out[7:8, :] = jnp.zeros((1, out.shape[1]), F32)
    out[7:8, :width] = qv[0:1, :]
    out[7:8, 2 * width : 3 * width] = qv[1:2, :]


def image_windows(count, images):
    windows = []
    per = 4
    for low in range(0, images, per):
        start = (low * IMG_SEQ + 15) // 16 * 16 if low else 0
        end = min(count, ((low + per) * IMG_SEQ + 15) // 16 * 16)
        if low + per >= images:
            end = count
        key_start = start // IMG_SEQ * IMG_SEQ // 16 * 16
        key_end = min(count, ((end - 1) // IMG_SEQ * IMG_SEQ + IMG_SEQ + 15) // 16 * 16)
        windows.append((start, end, key_start, key_end))
    return windows


def image_attn_kernel(first, x0, x1, vectors, *rest):
    if first:
        source, own_out, other_out, rows, qkv, context, total, weights, sem = rest
    else:
        own_before, other_before, source, keep, *sends, rows, qkv, context, total, weights, sem = rest
    count, dim = x0.shape
    images = count // IMG_SEQ
    width = dim // 4
    copy = pltpu.make_async_copy(source.at[0 : 4 * width + 16], weights, sem)
    copy.start()
    rows[:count, :] = x0.get()[...]
    rows[count:, :] = x1.get()[...]

    def normalize(c):
        at = chunk_start(c, count)
        normed, _ = norm(rows[at, :].astype(F32))
        rows[at, :] = (
            normed * vector(vectors, ATTN_GAIN) + vector(vectors, ATTN_SHIFT)
        ).astype(BF)

    repeat(2, normalize)
    windows = image_windows(count, images)
    copy.wait()
    bias = weights[4 * width : 4 * width + 16, :].astype(F32)
    bias_rows = (bias[0:1, :width], jnp.zeros((1, width), F32), bias[1:2, :width])

    def chunk(c):
        own = rows[chunk_start(c, count), :]
        for part in range(3):
            value = dot(own, weights[part * width : (part + 1) * width, :], NT)
            qkv[part] = (value + bias_rows[part]).astype(BF)
        for q_low, q_high, k_low, k_high in windows:
            extent = (q_high - q_low, k_high - k_low)
            q_image = (lax.broadcasted_iota(jnp.int32, extent, 0) + q_low) // IMG_SEQ
            k_image = (lax.broadcasted_iota(jnp.int32, extent, 1) + k_low) // IMG_SEQ
            mask = jnp.where(q_image == k_image, 1.0, 0.0)
            place = pl.ds(pl.multiple_of(c * count + q_low, 16), q_high - q_low)
            context[place, :] = attend(
                qkv[0, q_low:q_high, :], qkv[1, k_low:k_high, :], qkv[2, k_low:k_high, :], mask
            )

    def columns(i):
        cols = lanes(i, 256)
        total[:, cols] = dot(context[...], weights[3 * width : 4 * width, cols])

    repeat(2, chunk)
    repeat(dim // 256, columns)
    if first:
        own_out.held[...] = total[:count, :]
        own_out.start()
        other_out.held[...] = total[count:, :].astype(BF)
        other_out.start()
        return
    keep[...] = total[:count, :] + own_before.get()[...]
    put_pieces((total[count:, :] + other_before.get()[...].astype(F32)).astype(BF), sends)


def image_norm_kernel(x, keep, vectors, *rest):
    *others, after_out, rows = rest
    total = keep[...] + join_pieces(others).astype(F32)
    after = x[...].astype(F32) + (total + vector(vectors, OUT_BIAS))
    after_out.held[...] = after
    after_out.start()
    normed, _ = norm(after)
    rows[...] = (normed * vector(vectors, MLP_GAIN) + vector(vectors, MLP_SHIFT)).astype(BF)


def image_mlp_kernel(rows0, rows2, vectors, w1a, w2a, w1b, w2b, mine, far, rows, active, total):
    size, dim = rows0.shape
    rows[:size, :] = rows0[...]
    rows[size:, :] = rows2[...]
    for bias, w1, w2 in ((FC1_BIAS, w1a, w2a), (FC1_BIAS_OTHER, w1b, w2b)):
        w1 = w1.get()

        def units(i):
            cols = lanes(i, 256)
            hidden = dot(rows[...], w1[:, cols]) + vectors[bias : bias + 1, cols]
            active[:, cols] = gelu_parts(hidden)[0].astype(BF)

        repeat(w1.shape[1] // 256, units)
        w2 = w2.get()

        def columns(i):
            cols = lanes(i, 256)
            value = dot(active[...], w2[:, cols])
            total[:, cols] = value if bias == FC1_BIAS else total[:, cols] + value

        repeat(dim // 256, columns)
    mine[...] = total[:size, :].astype(BF)
    far[...] = total[size:, :].astype(BF)


def image_out_kernel(after, mine, theirs, vectors, out):
    branch = mine[...].astype(F32) + theirs[...].astype(F32)
    out[...] = (after[...] + (branch + vector(vectors, FC2_BIAS))).astype(BF)


def core_swap(x):
    return lax.ppermute(x, "mp", [(i, i ^ 1) for i in range(lax.axis_size("mp"))])


def side_swap(x):
    return lax.ppermute(x, "mp", [(i, i ^ 2) for i in range(lax.axis_size("mp"))])


def dp_swap(x, bits):
    n_dp, n_mp = lax.axis_size("dp"), lax.axis_size("mp")
    pairs = [
        (d * n_mp + m, (d ^ bits[m % 2]) * n_mp + m) for d in range(n_dp) for m in range(n_mp)
    ]
    return lax.ppermute(x, ("dp", "mp"), pairs)


def per_device(
    text_in,
    segment_ids,
    valid_lengths,
    text_grad,
    attn_gain,
    attn_shift,
    qkv_weight,
    qv_bias,
    out_weight,
    out_bias,
    mlp_gain,
    mlp_shift,
    fc1_weight,
    fc1_bias,
    fc2_weight,
    fc2_bias,
    images,
    img_attn_gain,
    img_attn_shift,
    img_qkv_weight,
    img_qv_bias,
    img_out_weight,
    img_out_bias,
    img_mlp_gain,
    img_mlp_shift,
    img_fc1_weight,
    img_fc1_bias,
    img_fc2_weight,
    img_fc2_bias,
):
    size, dim = text_in.shape
    row_count, length = segment_ids.shape
    width = qkv_weight.shape[2]
    n_dp = lax.axis_size("dp")
    tokens = 4 * size

    w_t = qkv_weight.transpose(1, 2, 0).reshape(3 * width, dim)
    img_w_t = img_qkv_weight.transpose(1, 2, 0).reshape(3 * width, dim)
    used = 4 * width + 16
    total_rows = -(-used // (16 * n_dp)) * 16 * n_dp
    part_rows = total_rows // n_dp

    rows_first = 2 * size // length
    blocks = row_blocks(row_count, length, rows_first)
    blocks_first = [b for b in blocks if b[0] < rows_first * length]
    blocks_rest = [b for b in blocks if b[0] >= rows_first * length]

    run = Line()
    chunk = shape(size, dim)
    pair = shape(2 * size, dim)

    x0 = text_in
    x2 = side_swap(x0)
    x1 = core_swap(x0)
    vectors, img_vectors = run(
        vectors_kernel,
        [shape(8, dim, dtype=F32)] * 2,
        [
            Late(v)
            for v in (
                attn_gain, attn_shift, out_bias, mlp_gain, mlp_shift, fc2_bias, fc1_bias,
                img_attn_gain, img_attn_shift, img_out_bias, img_mlp_gain, img_mlp_shift,
                img_fc2_bias, img_fc1_bias, core_swap(img_fc1_bias),
            )
        ],
    )
    project_scratch = [pltpu.VMEM((2, size, dim), BF), pltpu.VMEM((8, width), F32)]
    rows_own, qkv_own = run(
        own_rows_kernel,
        [Early(2 * size, dim), shape(3, 2 * size, width)],
        [x0, x1, vectors, w_t, qv_bias],
        scratch=project_scratch,
    )
    mask = run(
        functools.partial(mask_kernel, blocks),
        [shape(tokens, 2 * length, dtype=F32)],
        [segment_ids, valid_lengths],
        scalars=(1,),
    )
    bundle = run(
        bundle_kernel,
        [shape(total_rows, dim)],
        [img_w_t, img_out_weight, img_qv_bias],
        scratch=[
            pltpu.VMEM((total_rows - 4 * width, dim), BF),
            pltpu.SemaphoreType.DMA((3,)),
        ],
        untouched=(0, 1),
        outside=True,
    )
    t0 = text_grad
    t1 = core_swap(t0)
    packed = run(
        far_operands_kernel,
        [shape(size + part_rows, dim)],
        [t0, bundle],
        scratch=[pltpu.SemaphoreType.DMA(())],
        untouched=(1,),
        after=[x2],
    )
    x2 = run.hold(x2)
    x3 = core_swap(x2)
    packed = side_swap(packed)

    rows_far, qkv, ctx, x_mine, keep0, keep1, send0, send1 = run(
        functools.partial(attn_forward_kernel, blocks),
        [
            Early(2 * size, dim),
            Early(3, tokens, width),
            Early(tokens, width),
            Early(2, size, dim),
        ]
        + [chunk] * 4,
        [x0, x2, x3, qkv_own, vectors, w_t, qv_bias, out_weight, mask],
        scratch=project_scratch,
    )

    row_cuts, sum_cuts, *og_cuts = [pieces_of(size, n) for n in PIECES[:4]]

    def after_attn(half, mine, theirs):
        stream, rows, *sends = run(
            functools.partial(after_attn_kernel, half),
            [Early(size, dim, dtype=F32), chunk] + [shape(n, dim) for n in row_cuts],
            [x_mine, mine, theirs, vectors],
        )
        return stream, (rows, *map(core_swap, sends))

    def mlp(rows, grad):
        all_rows, act, hid_grad, br_keep, br_send, mg_keep, *mg_sends = run(
            functools.partial(mlp_kernel, len(rows) - 1),
            [Early(2 * size, dim)] * 3
            + [Early(size, dim)] * 2
            + [chunk]
            + [shape(n, dim) for n in sum_cuts],
            [*rows, grad, fc1_weight, vectors, fc2_weight],
        )
        partial = (mg_keep, *map(core_swap, mg_sends))
        return all_rows, act, hid_grad, (br_keep, core_swap(br_send)), partial

    def mlp_back(half, stream, mine, theirs, grad):
        value, low, sums, *sends = run(
            mlp_back_kernel,
            [Early(size, dim, dtype=F32), chunk, shape(2, dim, dtype=F32)]
            + [shape(n, dim) for n in og_cuts[half]],
            [stream, mine, theirs, grad, vectors],
        )
        return value, (low, *map(core_swap, sends)), sums

    other0, other1 = core_swap(send0), core_swap(send1)
    mine0 = run(add_kernel, [chunk], [keep0, other0], after=[packed])
    theirs0 = side_swap(mine0)
    far_part = run(unpack_kernel, [shape(part_rows, dim)], [packed])
    far_bundle = lax.all_gather(far_part, "dp", axis=0, tiled=True)

    image_rows = images.shape[0]
    image_chunk = shape(image_rows, dim)
    img_other = core_swap(images)
    img_w1_other, img_w2_other = core_swap(img_fc1_weight), core_swap(img_fc2_weight)
    image_scratch = [
        pltpu.VMEM((2 * image_rows, dim), BF),
        pltpu.VMEM((3, image_rows, width), BF),
        pltpu.VMEM((2 * image_rows, width), BF),
        pltpu.VMEM((2 * image_rows, dim), F32),
        pltpu.VMEM((used, dim), BF),
        pltpu.SemaphoreType.DMA(()),
    ]
    image_total = run(
        functools.partial(image_attn_kernel, True),
        [Early(image_rows, dim, dtype=F32), Early(image_rows, dim)],
        [Late(images), Late(img_other), img_vectors, Fixed(bundle)],
        scratch=image_scratch,
        after=[Fixed(img_w1_other)],
    )
    mine1 = run(add_kernel, [chunk], [keep1, other1], after=[theirs0])
    theirs1 = side_swap(mine1)
    stream0, rows0 = after_attn(0, mine0, theirs0)
    tg0, tg1 = run(
        arrange_kernel, [Early(2 * size, dim)] * 2, [t0, t1, packed, core_swap(packed)]
    )
    all_rows0, act0, hg0, branch0, partial0 = mlp(rows0, tg0)
    mg0 = run(add_pieces_kernel, [chunk], partial0, after=[theirs1, Fixed(img_w2_other)])
    mg_theirs0 = side_swap(mg0)
    stream1, rows1 = after_attn(1, mine1, theirs1)
    all_rows1, act1, hg1, branch1, partial1 = mlp(rows1, tg1)

    bits = [2**k for k in range(n_dp.bit_length() - 1)]
    along_x = tuple(bits)
    kinds = {
        "even": (along_x, along_x),
        "mixed": (along_x, tuple(bits[1:] + bits[:1])),
        "turned": (along_x, tuple(bits[1:2] + bits[:1] + bits[2:])),
    }
    plain = 2 ** len(bits) != n_dp or dim % (16 * n_dp) != 0
    fc2_order, fc1_order, qkv_order = [None if plain else kinds[name] for name in ORDERS]
    grad_shapes = [shape(dim, dim, dtype=F32)] if plain else [shape(dim // 2, dim)] * 2

    class Sum:
        def __init__(self, parts, orders, sizes):
            self.orders, self.sizes, self.step = orders, sizes, 0
            if plain:
                total = lax.psum(parts[0], "dp")
                cuts = [sum(sizes[: i + 1]) for i in range(len(sizes) - 1)]
                self.result = jnp.split(total, cuts, axis=0)
                return
            self.keep = parts[0]
            self.exchange(parts[1], 0)

        def exchange(self, send, k):
            self.arriving = dp_swap(send, (self.orders[0][k], self.orders[1][k]))

        def advance(self):
            if plain or self.step == 2 * len(bits):
                return
            self.step += 1
            rows, levels = self.keep.shape[0], len(bits)
            if self.step < levels:
                self.keep, send = run(
                    add_split_kernel, [shape(rows // 2, dim)] * 2, [self.keep, self.arriving]
                )
                self.exchange(send, self.step)
            elif self.step < 2 * levels:
                if self.step == levels:
                    self.keep = run(add_kernel, [shape(rows, dim)], [self.keep, self.arriving])
                else:
                    self.keep = run(
                        join_kernel, [shape(2 * rows, dim)], [self.keep, self.arriving]
                    )
                self.exchange(self.keep, 2 * levels - 1 - self.step)
            else:
                got = run(
                    functools.partial(gather_blocks_kernel, self.orders),
                    [Pinned(n, dim, dtype=F32) for n in self.sizes],
                    [self.keep, self.arriving],
                    scratch=[
                        pltpu.VMEM((dim, dim), F32),
                        pltpu.SemaphoreType.DMA((n_dp + len(self.sizes),)),
                    ],
                )
                self.result = got if len(self.sizes) > 1 else [got]

    def fc_weight(orders, args):
        *parts, sums = run(
            functools.partial(fc_weight_kernel, orders),
            grad_shapes + [shape(1, dim, dtype=F32)],
            args,
            scratch=[pltpu.VMEM((dim, dim), F32)],
        )
        return Sum(parts, orders, (dim,)), sums

    got = {}

    def fc2_weight():
        got["fc2"], got["fc2_bias"] = fc_weight(fc2_order, [act0, act1, tg0, tg1])

    def fc1_weight():
        got["fc1"], got["fc1_bias"] = fc_weight(fc1_order, [all_rows0, all_rows1, hg0, hg1])

    def mlp_sum():
        got["mg1"] = run(add_pieces_kernel, [chunk], partial1, after=[mg_theirs0])
        got["mg_theirs1"] = side_swap(got["mg1"])

    def mlp_back0():
        got["grad0"], got["og0"], got["sums0"] = mlp_back(0, stream0, mg0, mg_theirs0, tg0)

    def mlp_back1():
        got["grad1"], got["og1"], got["sums1"] = mlp_back(
            1, stream1, got["mg1"], got["mg_theirs1"], tg1
        )

    def attn_back0():
        og = got["og0"]
        got["first"] = run(
            functools.partial(attn_back_first_kernel, blocks_first, len(og) - 1),
            [pair, shape(2 * size, width), shape(3, rows_first * length, width)],
            [*og, qkv, mask, out_weight],
        )

    def attn_back1():
        og = got["og1"]
        got["og_second"], got["pg"], p0, p1, p2, p3 = run(
            functools.partial(attn_back_second_kernel, blocks_rest, len(og) - 1),
            [pair, shape(3, tokens, width)] + [chunk] * 4,
            [*og, *got["first"][1:], qkv, mask, out_weight, w_t],
            scratch=[pltpu.VMEM((tokens, width), BF)],
        )
        got["parts"] = [p0, core_swap(p1), p2, core_swap(p3)]

    def attn_weights():
        *parts, got["out_bias"], got["qv_bias"] = run(
            functools.partial(attn_weights_kernel, qkv_order),
            grad_shapes + [shape(1, dim, dtype=F32), shape(2, width, dtype=F32)],
            [ctx, got["first"][0], got["og_second"], rows_own, rows_far, got["pg"]],
            scratch=[pltpu.VMEM((dim, dim), F32)],
        )
        got["qkv"] = Sum(parts, qkv_order, (3 * width, width))

    image_cuts = pieces_of(image_rows, PIECES[4])

    def p_sums():
        got["p"], to_side = run(add_pair_kernel, [chunk] * 2, got["parts"])
        got["p_far"] = side_swap(to_side)

    def image_attn():
        got["img"], *sends = run(
            functools.partial(image_attn_kernel, False),
            [shape(image_rows, dim, dtype=F32)] + [shape(n, dim) for n in image_cuts],
            [
                Late(images), Late(img_other), img_vectors, *map(Late, image_total),
                Fixed(far_bundle),
            ],
            scratch=image_scratch,
            vmem=20,
        )
        got["img_others"] = [core_swap(part) for part in sends]

    def image_norm():
        got["img_after"], got["rows0"] = run(
            image_norm_kernel,
            [Early(image_rows, dim, dtype=F32), image_chunk],
            [images, got["img"], img_vectors, *got["img_others"]],
        )
        got["rows2"] = side_swap(got["rows0"])

    def image_mlp():
        got["img_mine"], far = run(
            image_mlp_kernel,
            [image_chunk] * 2,
            [
                got["rows0"], got["rows2"], img_vectors,
                Late(img_fc1_weight), Late(img_fc2_weight),
                Late(img_w1_other), Late(img_w2_other),
            ],
            scratch=[pltpu.VMEM((2 * image_rows, dim), BF)] * 2
            + [pltpu.VMEM((2 * image_rows, dim), F32)],
            vmem=24,
        )
        got["img_far"] = side_swap(far)

    def image_out():
        got["image_out"] = run(
            image_out_kernel,
            [image_chunk],
            [got["img_after"], got["img_mine"], got["img_far"], img_vectors],
        )

    def input_grad():
        got["input"], attn_sums = run(
            input_grad_kernel,
            [chunk, shape(2, dim, dtype=F32)],
            [text_in, got["p"], got["p_far"], got["grad0"], got["grad1"], vectors],
        )
        got["small"] = run(
            norm_sums_kernel, [shape(4, dim, dtype=F32)], [got["sums0"], got["sums1"], attn_sums]
        )
        got["small_far"] = core_swap(got["small"])

    def branch():
        br0, br1 = run(branch_sums_kernel, [Early(size, dim)] * 2, [*branch0, *branch1])
        far = run(far_branch_kernel, [chunk], [br0, br1])
        got["branch"] = (br0, br1, side_swap(far))

    def text_out():
        got["text_out"] = run(
            text_out_kernel, [chunk], [*got["branch"], stream0, stream1, vectors]
        )

    def small_near():
        got["small"] = run(
            add_rows_kernel, [shape(4, dim, dtype=F32)], [got["small"], got["small_far"]]
        )
        got["small_far"] = side_swap(got["small"])

    later = [] if plain else list(bits)

    def small_next():
        if later:
            bit = later.pop(0)
            got["small_far"] = dp_swap(got["small"], (bit, bit))

    def small_side():
        got["small"] = run(
            small_kernel,
            [shape(8, dim, dtype=F32)],
            [
                got["small"], got["small_far"],
                got["fc2_bias"], got["fc1_bias"], got["out_bias"], got["qv_bias"],
            ],
        )
        small_next()

    def small_dp():
        if not plain:
            got["small"] = run(
                add_rows_kernel, [shape(8, dim, dtype=F32)], [got["small"], got["small_far"]]
            )
            small_next()

    steps = dict(
        fc2_weight=fc2_weight, fc1_weight=fc1_weight, mlp_sum=mlp_sum,
        mlp_back0=mlp_back0, mlp_back1=mlp_back1, attn_back0=attn_back0, attn_back1=attn_back1,
        attn_weights=attn_weights,
        p_sums=p_sums, image_attn=image_attn, image_norm=image_norm, image_mlp=image_mlp,
        image_out=image_out, input=input_grad, branch=branch, text_out=text_out,
        small_near=small_near, small_side=small_side, small_dp=small_dp,
        fc1=lambda: got["fc1"].advance(),
        fc2=lambda: got["fc2"].advance(),
        qkv=lambda: got["qkv"].advance(),
    )
    for name in PLAN:
        steps[name]()
    small = lax.psum(got["small"], "dp") if plain else got["small"]
    (grad_fc2_weight,) = got["fc2"].result
    (grad_fc1_weight,) = got["fc1"].result
    grad_qkv, grad_out_weight = got["qkv"].result
    return (
        got["text_out"],
        got["image_out"],
        got["input"],
        small[2],
        small[3],
        grad_qkv.reshape(3, width, dim).transpose(2, 0, 1),
        jnp.stack([small[7, :width], small[7, 2 * width : 3 * width]]),
        grad_out_weight,
        small[6],
        small[0],
        small[1],
        grad_fc1_weight,
        small[5],
        grad_fc2_weight,
        small[4],
    )


def solution(mesh):
    in_specs = (
        P(("dp", "mp"), None),
        P("dp", None),
        P("dp"),
        P(("dp", "mp"), None),
        P(),
        P(),
        P(None, None, "mp"),
        P(None, "mp"),
        P("mp", None),
        P(),
        P(),
        P(),
        P(None, "mp"),
        P("mp"),
        P("mp", None),
        P(),
        P(("dp", "mp"), None),
        P(),
        P(),
        P(None, None, "mp"),
        P(None, "mp"),
        P("mp", None),
        P(),
        P(),
        P(),
        P(None, "mp"),
        P("mp"),
        P("mp", None),
        P(),
    )
    out_specs = (
        P(("dp", "mp"), None),
        P(("dp", "mp"), None),
        P(("dp", "mp"), None),
        P(),
        P(),
        P(None, None, "mp"),
        P(None, "mp"),
        P("mp", None),
        P(),
        P(),
        P(),
        P(None, "mp"),
        P("mp"),
        P("mp", None),
        P(),
    )
    return jax.shard_map(
        per_device, mesh=mesh, in_specs=in_specs, out_specs=out_specs, check_vma=False
    )
```
